32 devices in a mesh: batch: 4 (over y, x), blk: 8 (over z, core).
Axes of the slice: x: 2, y: 2, z: 4, core: 2. Of those that a mesh axis runs over, the one named last changes fastest.
Arguments:
- tokens: bfloat16 [4, 4096, 768], P('batch', 'blk'), may hold values from -6 to 6
- lengths: int32 [4, 3], P('batch'), may hold values from 128 to 3839, as said below
- norm_one: bfloat16 [768], P(('batch', 'blk')), may hold values from 0.5 to 1.5
- w_qkv: bfloat16 [768, 2304], P(('batch', 'blk')), may hold values from -0.109375 to 0.109375
- rel_table: float32 [32, 12], replicated, may hold values from -4 to 4
- w_out: bfloat16 [768, 768], P(('batch', 'blk')), may hold values from -6 to 6
- norm_two: bfloat16 [768], P(('batch', 'blk')), may hold values from 0.5 to 1.5
- w_gateup: bfloat16 [768, 4096], P(('batch', 'blk')), may hold values from -0.21875 to 0.21875
- w_down: bfloat16 [2048, 768], P(('batch', 'blk')), may hold values from -0.125 to 0.125
- cotangent: bfloat16 [4, 4096, 768], P('batch', 'blk'), may hold values from -6 to 6
- row_qkv: float32 [768], P(('batch', 'blk')), may hold values from 0.25 to 4
- col_qkv: float32 [2304], replicated, may hold values from 0.25 to 4
- row_out: float32 [768], P(('batch', 'blk')), may hold values from 0.25 to 4
- col_out: float32 [768], replicated, may hold values from 0.25 to 4
- row_gateup: float32 [768], P(('batch', 'blk')), may hold values from 0.25 to 4
- col_gateup: float32 [4096], replicated, may hold values from 0.25 to 4
- row_down: float32 [2048], P(('batch', 'blk')), may hold values from 0.25 to 4
- col_down: float32 [768], replicated, may hold values from 0.25 to 4
Outputs:
- output: bfloat16 [4, 4096, 768], P('batch', 'blk')
- d_tokens: bfloat16 [4, 4096, 768], P('batch', 'blk')
- d_norm_one: float32 [768], P(('batch', 'blk'))
- d_qkv: float32 [768, 2304], P(('batch', 'blk'))
- d_table: float32 [32, 12], replicated
- d_out: float32 [768, 768], P(('batch', 'blk'))
- d_norm_two: float32 [768], P(('batch', 'blk'))
- d_gateup: float32 [768, 4096], P(('batch', 'blk'))
- d_down: float32 [2048, 768], P(('batch', 'blk'))
- new_row_qkv: float32 [768], P(('batch', 'blk'))
- new_col_qkv: float32 [2304], replicated
- new_row_out: float32 [768], P(('batch', 'blk'))
- new_col_out: float32 [768], replicated
- new_row_gateup: float32 [768], P(('batch', 'blk'))
- new_col_gateup: float32 [4096], replicated
- new_row_down: float32 [2048], P(('batch', 'blk'))
- new_col_down: float32 [768], replicated
The draws below stay inside these ranges and needn't reach their ends.
Inputs may be any that keep to these rules, and one draw needn't show every extreme that they name: `lengths`: each row holds 3 documents one after the other from position 0, then 1 to 128 padding positions at the end. The first document is shorter than 512; the third is 128 to 256 long, so the second document begins on the first device of blk and ends on the last.
All inputs are finite; a program needn't handle non-finite values.
Results may differ from the reference program's by a relative error of at most 0.022.
Values may be sent and summed in bfloat16 or wider, within the bound.
No kernel may reach another device: no remote copies, remote signals or barrier semaphores. Data moves between devices by JAX's collectives and lax.ppermute only.
A program may use at most 192 MiB of HBM per device.

```python
import math
import jax
import jax.numpy as jnp
from jax import lax

D = 768
HEADS = 12
DK = 64
FF = 2048
BUCKETS = 32
TOK_DEV = 512
HD = 768
SEQ = 4096
ROWS = 4


def draw_lengths(key, part):
    key = jax.random.fold_in(key, 11)
    first_key, third_key, padding_key, chosen_key = jax.random.split(key, 4)
    first = jax.random.randint(first_key, (ROWS,), TOK_DEV // 4, TOK_DEV)
    third = jax.random.randint(third_key, (ROWS,), TOK_DEV // 4, TOK_DEV // 2 + 1)
    padding = jax.random.randint(padding_key, (ROWS,), 1, TOK_DEV // 4 + 1)
    chosen = jax.random.randint(chosen_key, (), 0, ROWS)
    picked = jnp.arange(ROWS, dtype=jnp.int32) == chosen
    first = jnp.where(picked, TOK_DEV // 4, first)
    third = jnp.where(picked, TOK_DEV // 4, third)
    padding = jnp.where(picked, 1, padding)
    second = SEQ - first - third - padding
    return jnp.stack([first, second, third], axis=1).astype(jnp.int32)


def shard_levels(own_key, dims, cuts, low, largest):
    loudness = 1.0
    for dim, parts in cuts:
        steps = jax.random.uniform(jax.random.fold_in(jax.random.fold_in(own_key, 6), dim), (parts,), jnp.float32, low / len(cuts), largest / len(cuts))
        loudness = loudness * jnp.repeat(jnp.exp(steps), dims[dim] // parts).reshape((-1,) + (1,) * (len(dims) - 1 - dim))
    return loudness


def gaussian(key, shape, scale, most, cuts=(), held_as=jnp.bfloat16):
    entries = scale * jax.random.normal(key, shape, jnp.float32)
    if cuts:
        entries = entries * shard_levels(key, shape, cuts, -0.22, 0.18)
    return jnp.clip(entries, -most, most).astype(held_as)


def setup_inputs(seed: int = 0) -> dict:
    key_of = jax.random.split(jax.random.key(seed), 19)
    tokens = gaussian(key_of[0], (ROWS, SEQ, D), 1.0, 6.0, ((0, 4), (1, 8)))
    lengths = draw_lengths(jax.random.fold_in(key_of[18], 71), 0)
    norm_one = jnp.clip(1.0 + 0.1 * jax.random.normal(key_of[2], (D,), jnp.float32), 0.5, 1.5).astype(jnp.bfloat16)
    w_qkv = gaussian(key_of[3], (D, 3 * HD), (4 * D) ** -0.5, 0.109375, ((0, 32),))
    rel_table = gaussian(key_of[4], (BUCKETS, HEADS), 1.0, 4.0, (), jnp.float32)
    w_out = gaussian(key_of[5], (HD, D), 1 ** -0.5, 6.0, ((0, 32),))
    norm_two = jnp.clip(1.0 + 0.1 * jax.random.normal(key_of[6], (D,), jnp.float32), 0.5, 1.5).astype(jnp.bfloat16)
    w_gateup = gaussian(key_of[7], (D, 2 * FF), D ** -0.5, 0.21875, ((0, 32),))
    w_down = gaussian(key_of[8], (FF, D), FF ** -0.5, 0.125, ((0, 32),))
    cotangent = gaussian(key_of[9], (ROWS, SEQ, D), 1.0, 6.0, ((0, 4), (1, 8)))
    row_qkv = jnp.clip(jnp.exp(math.log(4.0) - 2.7725887 * jax.random.uniform(key_of[10], (D,), jnp.float32) ** shard_levels(key_of[10], (D,), ((0, 32),), -0.2, 0.2)), 0.25, 4.0)
    col_qkv = jnp.clip(jnp.exp(jax.random.uniform(key_of[11], (3 * HD,), jnp.float32, math.log(0.25), math.log(4.0))), 0.25, 4.0)
    row_out = jnp.clip(jnp.exp(math.log(4.0) - 2.7725887 * jax.random.uniform(key_of[12], (HD,), jnp.float32) ** shard_levels(key_of[12], (HD,), ((0, 32),), -0.2, 0.2)), 0.25, 4.0)
    col_out = jnp.clip(jnp.exp(jax.random.uniform(key_of[13], (D,), jnp.float32, math.log(0.25), math.log(4.0))), 0.25, 4.0)
    row_gateup = jnp.clip(jnp.exp(math.log(4.0) - 2.7725887 * jax.random.uniform(key_of[14], (D,), jnp.float32) ** shard_levels(key_of[14], (D,), ((0, 32),), -0.2, 0.2)), 0.25, 4.0)
    col_gateup = jnp.clip(jnp.exp(jax.random.uniform(key_of[15], (2 * FF,), jnp.float32, math.log(0.25), math.log(4.0))), 0.25, 4.0)
    row_down = jnp.clip(jnp.exp(math.log(4.0) - 2.7725887 * jax.random.uniform(key_of[16], (FF,), jnp.float32) ** shard_levels(key_of[16], (FF,), ((0, 32),), -0.2, 0.2)), 0.25, 4.0)
    col_down = jnp.clip(jnp.exp(jax.random.uniform(key_of[17], (D,), jnp.float32, math.log(0.25), math.log(4.0))), 0.25, 4.0)
    return dict(tokens=tokens, lengths=lengths, norm_one=norm_one, w_qkv=w_qkv, rel_table=rel_table, w_out=w_out, norm_two=norm_two, w_gateup=w_gateup, w_down=w_down, cotangent=cotangent, row_qkv=row_qkv, col_qkv=col_qkv, row_out=row_out, col_out=col_out, row_gateup=row_gateup, col_gateup=col_gateup, row_down=row_down, col_down=col_down)


@jax.custom_vjp
def low(v):
    return lax.optimization_barrier(v.astype(jnp.bfloat16)).astype(jnp.float32)

@jax.custom_vjp
def low_back(v):
    return v

def low_keep(v):
    return (low(v), None)

def low_pass(kept, grad):
    return (grad,)

def back_keep(v):
    return (v, None)

def back_low(kept, grad):
    return (low(grad),)
low.defvjp(low_keep, low_pass)
low_back.defvjp(back_keep, back_low)
THRESHOLDS = (12, 16, 23, 32, 46, 64, 91)
EPSILON = 1e-06
DECAY_RATE = 0.5
NEGATIVE = -1000000000.0
GELU_SCALE = 0.7978845608028654
HIGHEST = lax.Precision.HIGHEST

def bucket_of(offset):
    distance = jnp.abs(offset)
    steps_up = 8 + sum(((distance >= limit).astype(jnp.int32) for limit in THRESHOLDS))
    within = jnp.where(distance < 8, distance, steps_up)
    return within + 16 * (offset > 0).astype(jnp.int32)

def documents(length_row, positions):
    ends = jnp.cumsum(length_row).astype(jnp.int32)
    segment = lax.optimization_barrier(jnp.sum((positions[:, None] >= ends[None, :]).astype(jnp.int32), axis=1))
    return (segment, positions >= ends[-1])

def rms_scale(values, gain):
    return values * lax.rsqrt(lax.optimization_barrier(jnp.mean(values * values, axis=-1, keepdims=True)) + EPSILON) * gain

def gelu_tanh(values):
    return 0.5 * values * (1.0 + jnp.tanh(GELU_SCALE * (values + 0.044715 * values * values * values)))

def attention(queries, keys, values, table, length_row):
    positions = jnp.arange(SEQ, dtype=jnp.int32)
    segment, padding = documents(length_row, positions)
    width = math.gcd(SEQ, 128)
    blocks = SEQ // width

    @jax.checkpoint
    def one_block(pieces):
        query_block, query_pos, query_seg = pieces
        scores = jnp.einsum('qhd,khd->hqk', query_block, keys, precision=HIGHEST)
        bucket = bucket_of(positions[None, :] - query_pos[:, None])
        scores = scores + jnp.transpose(table[bucket], (2, 0, 1))
        allowed = (query_seg[:, None] == segment[None, :]) & ~padding[None, :] | (query_pos[:, None] == positions[None, :])
        scores = low_back(scores)
        scores = jnp.where(allowed[None], scores, NEGATIVE)
        row_max = lax.optimization_barrier(jnp.max(scores, axis=-1, keepdims=True))
        unnorm = jnp.exp(scores - row_max)
        weights = unnorm / lax.optimization_barrier(jnp.sum(unnorm, axis=-1, keepdims=True))
        return jnp.einsum('hqk,khd->qhd', low(weights), values, precision=HIGHEST)
    result = lax.map(one_block, (queries.reshape(blocks, width, HEADS, DK), positions.reshape(blocks, width), segment.reshape(blocks, width)))
    return result.reshape(SEQ, HEADS, DK)

def layer_forward(inputs, gain_one, w_qkv, table, w_out, gain_two, w_gateup, w_down, lengths):
    width = HEADS * DK

    def one_row(pieces):
        row_values, length_row = pieces
        normed = low(rms_scale(row_values, gain_one))
        qkv = low_back(low(jnp.dot(normed, w_qkv, precision=HIGHEST)))
        shaped = qkv.reshape(SEQ, 3, HEADS, DK)
        context = attention(shaped[:, 0], shaped[:, 1], shaped[:, 2], table, length_row).reshape(SEQ, width)
        context = low_back(low(context))
        mixed = row_values + low_back(jnp.dot(context, w_out, precision=HIGHEST))
        normed_two = low(rms_scale(mixed, gain_two))
        gate_up = low_back(jnp.dot(normed_two, w_gateup, precision=HIGHEST))
        hidden = low(gelu_tanh(gate_up[:, :FF]) * gate_up[:, FF:])
        return mixed + low_back(jnp.dot(hidden, w_down, precision=HIGHEST))
    return lax.map(one_row, (inputs, lengths))

def factored(grad, row_old, column_old):
    squares = grad * grad
    mean_square = jnp.mean(squares) + EPSILON
    row_new = DECAY_RATE * row_old + (1.0 - DECAY_RATE) * lax.optimization_barrier(jnp.mean(squares, axis=1)) / mean_square
    column_new = DECAY_RATE * column_old + (1.0 - DECAY_RATE) * lax.optimization_barrier(jnp.mean(squares, axis=0)) / mean_square
    return (row_new, column_new)

def reference(tokens, lengths, norm_one, w_qkv, rel_table, w_out, norm_two, w_gateup, w_down, cotangent, row_qkv, col_qkv, row_out, col_out, row_gateup, col_gateup, row_down, col_down):

    def forward(inputs, gain_one, proj_qkv, table, proj_out, gain_two, proj_gateup, proj_down):
        return layer_forward(inputs, gain_one, proj_qkv, table, proj_out, gain_two, proj_gateup, proj_down, lengths)
    result, pullback = jax.vjp(forward, tokens.astype(jnp.float32), norm_one.astype(jnp.float32), w_qkv.astype(jnp.float32), rel_table.astype(jnp.float32), w_out.astype(jnp.float32), norm_two.astype(jnp.float32), w_gateup.astype(jnp.float32), w_down.astype(jnp.float32))
    grads = pullback(cotangent.astype(jnp.float32))
    new_row_qkv, new_col_qkv = factored(grads[2], row_qkv, col_qkv)
    new_row_out, new_col_out = factored(grads[4], row_out, col_out)
    new_row_gateup, new_col_gateup = factored(grads[6], row_gateup, col_gateup)
    new_row_down, new_col_down = factored(grads[7], row_down, col_down)
    return (result.astype(jnp.bfloat16), grads[0].astype(jnp.bfloat16), grads[1], grads[2], grads[3], grads[4], grads[5], grads[6], grads[7], new_row_qkv, new_col_qkv, new_row_out, new_col_out, new_row_gateup, new_col_gateup, new_row_down, new_col_down)
```

```python
import functools
import math

import jax
import jax.numpy as jnp
from jax import lax
from jax.experimental import pallas as pl
from jax.experimental.pallas import tpu as pltpu
from jax.sharding import PartitionSpec as P

THRESHOLDS = (12, 16, 23, 32, 46, 64, 91)
EPSILON = 1e-06
DECAY_RATE = 0.5
GELU_SCALE = 0.7978845608028654
MASKED = -1e9
ALL = ("batch", "blk")
LANES = 128
TILE = 256
GROUP = 4
VMEM = 56 * 2**20
F32 = jnp.float32
BF16 = jnp.bfloat16


def bucket_of(offset):
    distance = jnp.abs(offset)
    steps_up = 8 + sum(((distance >= limit).astype(jnp.int32) for limit in THRESHOLDS))
    within = jnp.where(distance < 8, distance, steps_up)
    return within + 16 * (offset > 0).astype(jnp.int32)


def rms_scale(values, gain):
    return values * lax.rsqrt(jnp.mean(values * values, axis=-1, keepdims=True) + EPSILON) * gain


def rms_back(values, gain, grad):
    scale = lax.rsqrt(jnp.mean(values * values, axis=-1, keepdims=True) + EPSILON)
    scaled = grad * gain
    return scale * scaled - values * scale**3 * jnp.mean(scaled * values, axis=-1, keepdims=True)


def gelu_tanh(values):
    return (
        0.5 * values * (1.0 + jnp.tanh(GELU_SCALE * (values + 0.044715 * values * values * values)))
    )


def gated(gate, upward):
    return gelu_tanh(gate) * upward


def dot_nn(left, right):
    return jnp.dot(left, right, preferred_element_type=F32)


def dot_tn(left, right):
    return lax.dot_general(left, right, (((0,), (0,)), ((), ())), preferred_element_type=F32)


def dot_nt(left, right):
    return lax.dot_general(left, right, (((1,), (1,)), ((), ())), preferred_element_type=F32)


def dot_tt(left, right):
    return lax.dot_general(left, right, (((0,), (1,)), ((), ())), preferred_element_type=F32)


class Layout:
    def __init__(self, tokens, groups, splits, ints):
        self.tokens, self.groups, self.splits = tokens, groups, splits
        self.blocks = groups * splits
        self.seq = tokens * self.blocks
        self.near = tokens + 2 * LANES
        self.subs = tokens // LANES
        self.group, self.split = ints[0], ints[1]
        self.ends = (ints[2], ints[3], ints[4])
        slot = pl.program_id(0)
        self.block = self.block_of(slot, 0)
        self.first = pl.multiple_of(self.block * tokens, LANES)
        self.lefts = jnp.maximum(0, self.block * (tokens // TILE) - 1)
        self.loops = (self.seq // TILE - 2 - tokens // TILE) // GROUP
        self.edge = jnp.logical_or(self.block == 0, self.block == self.blocks - 1)

    def block_of(self, slot, other):
        return lax.rem(self.group - slot + self.groups, self.groups) * self.splits + lax.rem(
            self.split + other, self.splits
        )

    def keys_of(self, tile):
        before = 2 * LANES + TILE * tile
        after = self.first + self.near + TILE * (tile - self.lefts)
        return pl.ds(pl.multiple_of(jnp.where(tile < self.lefts, before, after), LANES), TILE)

    def rows_of(self, tile):
        return pl.ds(pl.multiple_of(self.near + TILE * tile, LANES), TILE)

    def segment(self, positions):
        return sum((positions >= end).astype(jnp.int32) for end in self.ends)


def iota(shape, dim):
    return lax.broadcasted_iota(jnp.int32, shape, dim)


def fold(values):
    return values.reshape(values.shape[0] // 8, 8, values.shape[1])


def forward_kernel(tokens, groups, splits, ints, table, query, *refs):
    kvs, (probs, context, stats, k_aug, v_t, scores, biases, best) = refs[:splits], refs[splits:]
    lay = Layout(tokens, groups, splits, ints)
    half = query.shape[1] // 2
    buckets = table.shape[1]

    @pl.when(pl.program_id(0) == 0)
    def prepare():
        lane = iota((tokens, LANES), 1)
        for slot in range(groups):
            for other in range(splits):
                start = lay.block_of(slot, other) * tokens
                rows = pl.ds(pl.multiple_of(LANES + start, LANES), tokens)
                kv = kvs[other][slot * tokens : (slot + 1) * tokens, :].astype(F32)
                seg = lay.segment(start + iota((tokens, LANES), 0))
                k_aug[rows, :] = jnp.where(lane < half, kv, (lane - half == seg).astype(F32)).astype(BF16)
                turned = jnp.transpose(kv)
                ones = (iota((16, tokens), 0) == 0).astype(F32)
                v_t[:, rows] = jnp.concatenate([turned[half:], ones], axis=0).astype(BF16)
        outside = (iota((LANES, LANES), 1) == half + 3).astype(BF16)
        for start in (0, lay.seq + LANES):
            k_aug[start : start + LANES, :] = outside
            v_t[:, start : start + LANES] = jnp.zeros((half + 16, LANES), BF16)
        for place in range(3):
            bucket = bucket_of(
                LANES * (place - 1) + iota((LANES, LANES), 0) - iota((LANES, LANES), 1)
            )
            bias = jnp.zeros((LANES, LANES), F32)
            for label in range(buckets):
                bias = jnp.where(bucket == label, table[0, label], bias)
            biases[place] = bias

    far_left, far_right = table[0, buckets // 2 - 1], table[0, buckets - 1]
    positions = lay.block * tokens + iota((1, tokens), 1)
    seg_q = lay.segment(positions)
    row = iota((2 * half, tokens), 0)
    apart = jnp.logical_or(row - half != seg_q, row == half + 3)
    q_aug = jnp.where(
        row < half, jnp.transpose(query[...].astype(F32)), jnp.where(apart, MASKED, 0.0)
    ).astype(BF16)

    near = dot_nn(k_aug[pl.ds(lay.first, lay.near), :], q_aug)
    eye = iota((LANES, LANES), 0) == iota((LANES, LANES), 1)
    for sub_q in range(lay.subs):
        lanes = slice(LANES * sub_q, LANES * (sub_q + 1))
        top = None
        for sub_k in range(lay.subs + 2):
            rows = slice(LANES * sub_k, LANES * (sub_k + 1))
            place = sub_k - sub_q
            piece = near[rows, lanes] + (
                far_left if place < 0 else far_right if place > 2 else biases[place]
            )
            if place == 1:
                alone = jnp.logical_and(eye, positions[:, lanes] >= lay.ends[2])
                piece = jnp.where(alone, 0.0, piece)
            scores[rows, lanes] = piece
            high = jnp.max(fold(piece), axis=0)
            top = high if top is None else jnp.maximum(top, high)
        best[:, lanes] = top

    def score(tile):
        piece = dot_nn(k_aug[lay.keys_of(tile), :], q_aug)
        scores[lay.rows_of(tile), :] = piece
        const = jnp.where(tile < lay.lefts, far_left, far_right)
        return jnp.max(fold(piece), axis=0) + const

    def score_group(index, top):
        for step in range(GROUP):
            top = jnp.maximum(top, score(index * GROUP + step))
        return top

    best[...] = lax.fori_loop(0, lay.loops, score_group, best[...])

    @pl.when(lay.edge)
    def _():
        best[...] = jnp.maximum(best[...], score(lay.loops * GROUP))

    peak = jnp.max(best[...], axis=0, keepdims=True)
    weights = jnp.exp(scores[: lay.near, :] - peak).astype(BF16)
    probs[: lay.near, :] = weights
    total = dot_nn(v_t[:, pl.ds(lay.first, lay.near)], weights)

    def weigh(tile):
        const = jnp.where(tile < lay.lefts, far_left, far_right)
        rows = lay.rows_of(tile)
        part = jnp.exp(scores[rows, :] - (peak - const)).astype(BF16)
        probs[rows, :] = part
        return dot_nn(v_t[:, lay.keys_of(tile)], part)

    def weigh_group(index, total):
        return total + sum(weigh(index * GROUP + step) for step in range(GROUP))

    stats[...] = lax.fori_loop(0, lay.loops, weigh_group, total)

    @pl.when(lay.edge)
    def _():
        stats[...] += weigh(lay.loops * GROUP)

    inverse = 1.0 / stats[half : half + 1, :]
    result = stats[:half, :] * inverse
    context[...] = result.astype(BF16)
    stats[:half, :] = result
    stats[half : half + 1, :] = inverse


def backward_kernel(tokens, groups, splits, ints, query, d_context, stats, probs, *refs):
    kvs, d_query, d_kvs = refs[:splits], refs[splits], refs[splits + 1 : 2 * splits + 1]
    d_table, v_aug, k_t, d_kv, bands, sides, d_q = refs[2 * splits + 1 :]
    lay = Layout(tokens, groups, splits, ints)
    half = query.shape[1] // 2
    buckets = d_table.shape[0]

    @pl.when(pl.program_id(0) == 0)
    def prepare():
        lane = iota((tokens, LANES), 1)
        for slot in range(groups):
            for other in range(splits):
                start = lay.block_of(slot, other) * tokens
                rows = pl.ds(pl.multiple_of(LANES + start, LANES), tokens)
                kv = kvs[other][slot * tokens : (slot + 1) * tokens, :].astype(F32)
                v_aug[rows, :] = jnp.where(lane >= half, kv, (lane < 3).astype(F32)).astype(BF16)
                ones = (iota((16, tokens), 0) == 0).astype(F32)
                k_t[:, rows] = jnp.concatenate([jnp.transpose(kv)[:half], ones], axis=0).astype(BF16)
        for start in (0, lay.seq + LANES):
            v_aug[start : start + LANES, :] = jnp.zeros((LANES, LANES), BF16)
            k_t[:, start : start + LANES] = jnp.zeros((half + 16, LANES), BF16)
        d_kv[...] = jnp.zeros_like(d_kv)
        bands[...] = jnp.zeros_like(bands)
        sides[...] = jnp.zeros_like(sides)

    inverse = stats[half : half + 1, :]
    upstream = d_context[...].astype(F32)
    delta = jnp.sum(upstream * stats[:half, :], axis=0, keepdims=True) * inverse
    scaled = upstream * inverse
    high = delta.astype(BF16).astype(F32)
    middle = (delta - high).astype(BF16).astype(F32)
    low = delta - high - middle
    row = iota((half, tokens), 0)
    shift = jnp.where(row == 0, high, jnp.where(row == 1, middle, jnp.where(row == 2, low, 0.0)))
    up_aug = jnp.concatenate([-shift, scaled], axis=0).astype(BF16)
    up_rows = jnp.transpose(jnp.concatenate([jnp.zeros_like(scaled), scaled], axis=0)).astype(BF16)
    both = jnp.concatenate([query[...], up_rows], axis=0)

    def grads(keys, rows):
        part = probs[rows, :]
        d_scores = part.astype(F32) * dot_nn(v_aug[keys, :], up_aug)
        rounded = d_scores.astype(BF16)
        d_kv[keys, :] += dot_nn(jnp.concatenate([rounded, part], axis=1), both)
        return d_scores, dot_nn(k_t[:, keys], rounded)

    near, total = grads(pl.ds(lay.first, lay.near), pl.ds(0, lay.near))
    for sub_q in range(lay.subs):
        lanes = slice(LANES * sub_q, LANES * (sub_q + 1))
        for sub_k in range(lay.subs + 2):
            piece = near[LANES * sub_k : LANES * (sub_k + 1), lanes]
            place = sub_k - sub_q
            if 0 <= place <= 2:
                bands[place] += piece
            else:
                sides[int(place > 2), :, lanes] += jnp.sum(fold(piece), axis=0)
    d_q[...] = total
    near_sum = total[half : half + 8, :]

    def far(tile):
        part = grads(lay.keys_of(tile), lay.rows_of(tile))[1]
        return part, jnp.where(tile < lay.lefts, part[half : half + 8, :], 0.0)

    def far_group(index, left):
        parts = [far(index * GROUP + step) for step in range(GROUP)]
        d_q[...] += sum(part for part, _ in parts)
        return left + sum(side for _, side in parts)

    left_sum = lax.fori_loop(0, lay.loops, far_group, jnp.zeros((8, tokens), F32))
    sides[0] += left_sum

    @pl.when(lay.edge)
    def _():
        part, side = far(lay.loops * GROUP)
        d_q[...] += part
        sides[0] += side
        sides[1] -= side

    sides[1] += d_q[half : half + 8, :] - near_sum - left_sum
    d_query[...] = d_q[:half, :].astype(BF16)

    @pl.when(pl.program_id(0) == groups - 1)
    def finish():
        for slot in range(groups):
            for other in range(splits):
                start = lay.block_of(slot, other) * tokens
                rows = pl.ds(pl.multiple_of(LANES + start, LANES), tokens)
                d_kvs[other][slot * tokens : (slot + 1) * tokens, :] = d_kv[rows, :].astype(BF16)
        labels = [
            bucket_of(LANES * (place - 1) + iota((LANES, LANES), 0) - iota((LANES, LANES), 1))
            for place in range(3)
        ]
        for label in range(buckets):
            found = jnp.zeros((8, LANES), F32)
            for place in range(3):
                kept = jnp.where(labels[place] == label, bands[place], 0.0)
                found += jnp.sum(fold(kept), axis=0)
            if label in (buckets // 2 - 1, buckets - 1):
                side = sides[int(label == buckets - 1)]
                for sub in range(lay.subs):
                    found += side[:, LANES * sub : LANES * (sub + 1)]
            d_table[label : label + 1, :] = jnp.sum(found, axis=0, keepdims=True)


def smem():
    return pl.BlockSpec(memory_space=pltpu.SMEM)


def attend(head, tokens, groups, splits, ints, table, query, kvs):
    seq, rows = tokens * groups * splits, tokens * groups
    half = LANES // 2
    column = lambda slot: (0, slot)
    whole = pl.BlockSpec((rows, LANES), lambda slot: (0, head))
    return pl.pallas_call(
        functools.partial(forward_kernel, tokens, groups, splits),
        grid=(groups,),
        in_specs=[smem(), smem(), pl.BlockSpec((tokens, LANES), lambda slot: (slot, head))]
        + [whole] * splits,
        out_specs=[
            pl.BlockSpec((seq, tokens), lambda slot: (slot, 0)),
            pl.BlockSpec((half, tokens), column),
            pl.BlockSpec((half + 16, tokens), column),
        ],
        out_shape=[
            jax.ShapeDtypeStruct((groups * seq, tokens), BF16),
            jax.ShapeDtypeStruct((half, rows), BF16),
            jax.ShapeDtypeStruct((half + 16, rows), F32),
        ],
        scratch_shapes=[
            pltpu.VMEM((seq + 2 * LANES, LANES), BF16),
            pltpu.VMEM((half + 16, seq + 2 * LANES), BF16),
            pltpu.VMEM((seq, tokens), F32),
            pltpu.VMEM((3, LANES, LANES), F32),
            pltpu.VMEM((8, tokens), F32),
        ],
        compiler_params=pltpu.CompilerParams(vmem_limit_bytes=VMEM),
        cost_estimate=pl.CostEstimate(
            flops=16 * seq * rows * half, bytes_accessed=2 * seq * rows, transcendentals=seq * rows
        ),
        name="attend",
    )(ints, table, query, *kvs)


def attend_back(head, tokens, groups, splits, ints, buckets, query, d_context, stats, probs, kvs):
    seq, rows = tokens * groups * splits, tokens * groups
    half = LANES // 2
    column = lambda slot: (0, slot)
    whole = pl.BlockSpec((rows, LANES), lambda slot: (0, head))
    kept = pl.BlockSpec((rows, LANES), lambda slot: (0, 0))
    return pl.pallas_call(
        functools.partial(backward_kernel, tokens, groups, splits),
        grid=(groups,),
        in_specs=[
            smem(),
            pl.BlockSpec((tokens, LANES), lambda slot: (slot, head)),
            pl.BlockSpec((half, tokens), column),
            pl.BlockSpec((half + 16, tokens), column),
            pl.BlockSpec((seq, tokens), lambda slot: (slot, 0)),
        ]
        + [whole] * splits,
        out_specs=[pl.BlockSpec((half, tokens), column)]
        + [kept] * splits
        + [pl.BlockSpec((buckets, LANES), lambda slot: (0, 0))],
        out_shape=[jax.ShapeDtypeStruct((half, rows), BF16)]
        + [jax.ShapeDtypeStruct((rows, LANES), BF16)] * splits
        + [jax.ShapeDtypeStruct((buckets, LANES), F32)],
        scratch_shapes=[
            pltpu.VMEM((seq + 2 * LANES, LANES), BF16),
            pltpu.VMEM((half + 16, seq + 2 * LANES), BF16),
            pltpu.VMEM((seq + 2 * LANES, LANES), F32),
            pltpu.VMEM((3, LANES, LANES), F32),
            pltpu.VMEM((2, 8, tokens), F32),
            pltpu.VMEM((half + 16, tokens), F32),
        ],
        compiler_params=pltpu.CompilerParams(vmem_limit_bytes=VMEM),
        cost_estimate=pl.CostEstimate(
            flops=32 * seq * rows * half, bytes_accessed=2 * seq * rows, transcendentals=0
        ),
        name="attend_back",
    )(ints, query, d_context, stats, probs, *kvs)


def factored(grad_shard, column_total, row_old, column_old, row_total):
    columns = grad_shard.shape[1]
    mean_square = jnp.sum(column_total) / (row_total * columns) + EPSILON
    row_new = (
        DECAY_RATE * row_old
        + (1.0 - DECAY_RATE) * (jnp.sum(grad_shard * grad_shard, axis=1) / columns) / mean_square
    )
    column_new = (
        DECAY_RATE * column_old + (1.0 - DECAY_RATE) * (column_total / row_total) / mean_square
    )
    return (row_new, column_new)


def rolled(array, axis, by):
    size = array.shape[axis]
    return lax.dynamic_slice_in_dim(jnp.concatenate([array, array], axis=axis), by, size, axis)


def shards(
    tokens,
    lengths,
    norm_one,
    w_qkv,
    rel_table,
    w_out,
    norm_two,
    w_gateup,
    w_down,
    cotangent,
    row_qkv,
    col_qkv,
    row_out,
    col_out,
    row_gateup,
    col_gateup,
    row_down,
    col_down,
):
    own = tokens[0]
    tok_rows, width = own.shape
    heads = rel_table.shape[1]
    buckets = rel_table.shape[0]
    ring = lax.axis_size("blk")
    rows_apart = lax.axis_size("batch")
    groups = math.gcd(ring, heads)
    splits = ring // groups
    group_heads = heads // groups
    place = lax.axis_index("blk")
    group, split = place // splits, place % splits
    batch = lax.axis_index("batch")
    group_width = width // groups

    def line(array, by):
        step = by * splits
        return lax.ppermute(
            array, "blk", [(i, i + step) for i in range(ring) if 0 <= i + step < ring]
        )

    def from_group(array, ahead):
        step = ahead * splits
        return lax.ppermute(array, "blk", [(i, (i - step) % ring) for i in range(ring)])

    def from_split(array, ahead):
        pairs = []
        for i in range(ring):
            base = i // splits * splits
            pairs.append((base + (i - base + ahead) % splits, i))
        return lax.ppermute(array, "blk", pairs)

    ahead, behind = [own], [own]
    for _ in range(groups - 1):
        ahead.append(line(ahead[-1], 1))
        behind.append(line(behind[-1], -1))
    gathered = [own] + [ahead[s] + behind[groups - s] for s in range(1, groups)]

    gains = jnp.pad(jnp.stack([norm_one, norm_two], axis=1), ((0, 0), (0, LANES - 2)))
    full_qkv = lax.all_gather(jnp.concatenate([w_qkv, gains], axis=1), ALL, axis=0, tiled=True)
    full_out = lax.all_gather(w_out, ALL, axis=0, tiled=True)
    full_gateup = lax.all_gather(w_gateup, ALL, axis=0, tiled=True)
    full_down = lax.all_gather(w_down, ALL, axis=0, tiled=True)
    gain_one = full_qkv[:, 3 * width].astype(F32)
    gain_two = full_qkv[:, 3 * width + 1].astype(F32)

    split_qkv = rolled(
        full_qkv[:, : 3 * width].reshape(width, 3, groups, group_width), 2, group
    ).reshape(width, 3, groups, group_heads, LANES // 2)
    w_query = split_qkv[:, 0].reshape(width, width)
    w_kv = jnp.moveaxis(split_qkv[:, 1:], 1, 3).reshape(width, 2 * width)
    out_rel = rolled(full_out, 0, group * group_width)
    w_query_own = jnp.pad(
        split_qkv[:, 0, 0], ((0, 0), (0, 0), (0, LANES // 2))
    ).reshape(width, group_heads * LANES)

    normed = rms_scale(
        jnp.concatenate(gathered, axis=0).astype(F32), gain_one
    ).astype(BF16)
    query = dot_nn(normed, w_query_own).astype(BF16)
    kv = dot_nn(normed, w_kv[:, : 2 * group_width]).astype(BF16)
    kvs = [kv] + [from_split(kv, other) for other in range(1, splits)]

    ends = jnp.cumsum(lengths[0])
    ints = jnp.concatenate([jnp.stack([group, split]).astype(jnp.int32), ends.astype(jnp.int32)])
    table_own = lax.dynamic_slice_in_dim(rel_table.T, group * group_heads, group_heads, 0)

    contexts, stats, probs = [], [], []
    for head in range(group_heads):
        prob, context, stat = attend(
            head, tok_rows, groups, splits, ints, table_own[head : head + 1], query, kvs
        )
        contexts.append(context)
        stats.append(stat)
        probs.append(prob)

    def slot_of(array, slot, axis):
        return lax.slice_in_dim(array, slot * tok_rows, (slot + 1) * tok_rows, axis=axis)

    context_t = jnp.concatenate(
        [
            from_group(slot_of(contexts[head], s, 1), s) if s else slot_of(contexts[head], 0, 1)
            for s in range(groups)
            for head in range(group_heads)
        ],
        axis=0,
    )

    inputs = own.astype(F32)
    mixed = inputs + dot_tn(context_t, out_rel)
    normed_two = rms_scale(mixed, gain_two).astype(BF16)
    gate_up = dot_nn(normed_two, full_gateup)
    hidden_units = gate_up.shape[1] // 2
    gate = gate_up[:, :hidden_units]
    upward = gate_up[:, hidden_units:]
    hidden = gated(gate, upward).astype(BF16)
    result = (mixed + dot_nn(hidden, full_down)).astype(BF16)
    upstream = cotangent[0]
    d_hidden = dot_nt(upstream, full_down)
    grad_down = dot_tn(hidden, upstream)
    d_gate, d_upward = jax.vjp(gated, gate, upward)[1](d_hidden)
    grad_act = jnp.concatenate([d_gate, d_upward], axis=1).astype(BF16)
    grad_gateup = dot_tn(normed_two, grad_act)
    d_normed_two = dot_nt(grad_act, full_gateup)
    d_mixed = upstream.astype(F32) + rms_back(mixed, gain_two, d_normed_two)
    d_branch = d_mixed.astype(BF16)
    grad_out = rolled(dot_nn(context_t, d_branch), 0, (groups - group) % groups * group_width)
    d_context_t = dot_nt(out_rel, d_branch).astype(BF16)

    def scattered(grad):
        return lax.psum_scatter(grad.astype(BF16), ALL, scatter_dimension=0, tiled=True).astype(F32)

    shard_down = scattered(grad_down)
    shard_gateup = scattered(grad_gateup)
    shard_out = scattered(grad_out)

    head_size = LANES // 2
    d_queries, d_kvs, d_tables = [], [], []
    for head in range(group_heads):
        pieces = []
        for s in range(groups):
            piece = d_context_t[(s * group_heads + head) * head_size :][:head_size]
            pieces.append((s, piece))
        slots = [None] * groups
        for s, piece in pieces:
            slots[s] = from_group(piece, groups - s) if s else piece
        outs = attend_back(
            head,
            tok_rows,
            groups,
            splits,
            ints,
            buckets,
            query,
            jnp.concatenate(slots, axis=1),
            stats[head],
            probs[head],
            kvs,
        )
        d_queries.append(outs[0])
        d_kv = outs[1].astype(F32)
        for other in range(1, splits):
            d_kv = d_kv + from_split(outs[1 + other], splits - other).astype(F32)
        d_kvs.append(d_kv.astype(BF16))
        d_tables.append(jnp.sum(outs[-1], axis=1))

    d_query_t = jnp.concatenate(
        [
            from_group(slot_of(d_queries[head], s, 1), s) if s else slot_of(d_queries[head], 0, 1)
            for s in range(groups)
            for head in range(group_heads)
        ],
        axis=0,
    )
    d_kv_rows = jnp.concatenate(
        [
            from_group(slot_of(d_kvs[head], s, 0), s) if s else slot_of(d_kvs[head], 0, 0)
            for s in range(groups)
            for head in range(group_heads)
        ],
        axis=1,
    )
    d_normed = dot_tt(d_query_t, w_query) + dot_nt(d_kv_rows, w_kv)
    d_inputs = (d_mixed + rms_back(inputs, gain_one, d_normed)).astype(BF16)

    grad_group = jnp.concatenate(
        [dot_tt(normed, d) for d in d_queries] + [dot_tn(normed, d) for d in d_kvs], axis=1
    )
    shard_rows = width // (rows_apart * ring)
    grad_group = grad_group.reshape(rows_apart, groups, splits, shard_rows, 3 * group_width)
    held = lax.dynamic_index_in_dim(grad_group, split, 2, keepdims=False)
    for other in range(1, splits):
        target = (split + splits - other) % splits
        held = held + from_split(
            lax.dynamic_index_in_dim(grad_group, target, 2, keepdims=False), other
        )
    total = lax.dynamic_index_in_dim(held, batch, 0, keepdims=False)
    for step in range(1, rows_apart):
        total = total + lax.ppermute(
            lax.dynamic_index_in_dim(held, batch ^ step, 0, keepdims=False),
            "batch",
            [(i, i ^ step) for i in range(rows_apart)],
        )
    squares_group = jnp.sum(total * total, axis=(0, 1))
    columns = [lax.dynamic_index_in_dim(total, group, 0, keepdims=False)]
    for s in range(1, groups):
        columns.append(
            from_group(
                lax.dynamic_index_in_dim(total, (group + groups - s) % groups, 0, keepdims=False), s
            )
        )

    def unrolled(rel):
        absolute = rolled(rel, rel.ndim - 2, (groups - group) % groups)
        lead = absolute.shape[:-2]
        query_part = absolute[..., :group_width].reshape(*lead, 1, width)
        kv_part = absolute[..., group_width:].reshape(*lead, groups * group_heads, 2, head_size)
        kv_part = jnp.moveaxis(kv_part, -2, -3).reshape(*lead, 2, width)
        return jnp.concatenate([query_part, kv_part], axis=-2).reshape(*lead, 3 * width)

    shard_qkv = unrolled(jnp.stack(columns, axis=1))
    own_slot = (jnp.arange(groups) == 0).astype(F32)[:, None]
    squares_qkv = unrolled(own_slot * squares_group[None, :])
    table_local = jnp.stack(d_tables, axis=0)
    table_sum = lax.dynamic_update_slice_in_dim(
        jnp.zeros((heads, buckets), F32), table_local, group * group_heads, 0
    )
    table_total, column_qkv, column_out, column_gateup, column_down = lax.psum(
        (
            table_sum,
            squares_qkv,
            jnp.sum(shard_out * shard_out, axis=0),
            jnp.sum(shard_gateup * shard_gateup, axis=0),
            jnp.sum(shard_down * shard_down, axis=0),
        ),
        ALL,
    )
    shard_gain_one = jnp.sum(w_qkv.astype(F32) * shard_qkv, axis=1) / norm_one.astype(F32)
    shard_gain_two = jnp.sum(w_gateup.astype(F32) * shard_gateup, axis=1) / norm_two.astype(F32)
    new_row_qkv, new_col_qkv = factored(shard_qkv, column_qkv, row_qkv, col_qkv, width)
    new_row_out, new_col_out = factored(shard_out, column_out, row_out, col_out, width)
    new_row_gateup, new_col_gateup = factored(
        shard_gateup, column_gateup, row_gateup, col_gateup, width
    )
    new_row_down, new_col_down = factored(
        shard_down, column_down, row_down, col_down, full_down.shape[0]
    )
    return (
        result[None],
        d_inputs[None],
        shard_gain_one,
        shard_qkv,
        table_total.T,
        shard_out,
        shard_gain_two,
        shard_gateup,
        shard_down,
        new_row_qkv,
        new_col_qkv,
        new_row_out,
        new_col_out,
        new_row_gateup,
        new_col_gateup,
        new_row_down,
        new_col_down,
    )


def solution(mesh):
    split_rows = P(ALL, None)
    split_row = P(ALL)
    return jax.shard_map(
        shards,
        mesh=mesh,
        in_specs=(
            P("batch", "blk", None),
            P("batch", None),
            split_row,
            split_rows,
            P(),
            split_rows,
            split_row,
            split_rows,
            split_rows,
            P("batch", "blk", None),
            split_row,
            P(),
            split_row,
            P(),
            split_row,
            P(),
            split_row,
            P(),
        ),
        out_specs=(
            P("batch", "blk", None),
            P("batch", "blk", None),
            split_row,
            split_rows,
            P(),
            split_rows,
            split_row,
            split_rows,
            split_rows,
            split_row,
            P(),
            split_row,
            P(),
            split_row,
            P(),
            split_row,
            P(),
        ),
        check_vma=False,
    )
```

```python
import functools
import math

import jax
import jax.numpy as jnp
from jax import lax
from jax.experimental import pallas as pl
from jax.experimental.pallas import tpu as pltpu
from jax.sharding import Mesh
from jax.sharding import PartitionSpec as P

THRESHOLDS = (12, 16, 23, 32, 46, 64, 91)
EPSILON = 1e-06
DECAY_RATE = 0.5
GELU_SCALE = 0.7978845608028654
MASKED = -1e9
ALL = ("batch", "group", "split")
LANES = 128
TILE = 256
GROUP = 4
VMEM = 56 * 2**20
F32 = jnp.float32
BF16 = jnp.bfloat16


def bucket_of(offset):
    distance = jnp.abs(offset)
    steps_up = 8 + sum(((distance >= limit).astype(jnp.int32) for limit in THRESHOLDS))
    within = jnp.where(distance < 8, distance, steps_up)
    return within + 16 * (offset > 0).astype(jnp.int32)


def after(value, *others):
    return lax.optimization_barrier((value, *others))[0]


def rms_scale(values, gain):
    return values * lax.rsqrt(jnp.mean(values * values, axis=-1, keepdims=True) + EPSILON) * gain


def rms_back(values, gain, grad):
    scale = lax.rsqrt(jnp.mean(values * values, axis=-1, keepdims=True) + EPSILON)
    scaled = grad * gain
    return scale * scaled - values * scale**3 * jnp.mean(scaled * values, axis=-1, keepdims=True)


def dot_nn(left, right):
    return jnp.dot(left, right, preferred_element_type=F32)


def dot_nt(left, right):
    return lax.dot_general(left, right, (((1,), (1,)), ((), ())), preferred_element_type=F32)


def dot_tt(left, right):
    return lax.dot_general(left, right, (((0,), (1,)), ((), ())), preferred_element_type=F32)


class Layout:
    def __init__(self, tokens, groups, splits, ints):
        self.tokens, self.groups, self.splits = tokens, groups, splits
        self.blocks = groups * splits
        self.seq = tokens * self.blocks
        self.near = tokens + 2 * LANES
        self.subs = tokens // LANES
        self.split = ints[0]
        self.ends = (ints[1], ints[2], ints[3])
        slot = pl.program_id(0)
        self.block = self.block_of(slot, 0)
        self.first = pl.multiple_of(self.block * tokens, LANES)
        self.lefts = jnp.maximum(0, self.block * (tokens // TILE) - 1)
        self.loops = (self.seq // TILE - 2 - tokens // TILE) // GROUP
        self.edge = jnp.logical_or(self.block == 0, self.block == self.blocks - 1)

    def block_of(self, slot, other):
        return slot * self.splits + lax.rem(self.split + other, self.splits)

    def keys_of(self, tile):
        before = 2 * LANES + TILE * tile
        after = self.first + self.near + TILE * (tile - self.lefts)
        return pl.ds(pl.multiple_of(jnp.where(tile < self.lefts, before, after), LANES), TILE)

    def rows_of(self, tile):
        return pl.ds(pl.multiple_of(self.near + TILE * tile, LANES), TILE)

    def segment(self, positions):
        return sum((positions >= end).astype(jnp.int32) for end in self.ends)


def iota(shape, dim):
    return lax.broadcasted_iota(jnp.int32, shape, dim)


def fold(values):
    return values.reshape(values.shape[0] // 8, 8, values.shape[1])


def forward_kernel(tokens, groups, splits, ints, table, query, *refs):
    kvs, (probs, context, stats, k_aug, v_t, scores, biases, best) = refs[:splits], refs[splits:]
    lay = Layout(tokens, groups, splits, ints)
    half = query.shape[1] // 2
    buckets = table.shape[1]

    @pl.when(pl.program_id(0) == 0)
    def prepare():
        lane = iota((tokens, LANES), 1)
        for slot in range(groups):
            for other in range(splits):
                start = lay.block_of(slot, other) * tokens
                rows = pl.ds(pl.multiple_of(LANES + start, LANES), tokens)
                kv = kvs[other][slot * tokens : (slot + 1) * tokens, :].astype(F32)
                seg = lay.segment(start + iota((tokens, LANES), 0))
                k_aug[rows, :] = jnp.where(lane < half, kv, (lane - half == seg).astype(F32)).astype(BF16)
                turned = jnp.transpose(kv)
                ones = (iota((16, tokens), 0) == 0).astype(F32)
                v_t[:, rows] = jnp.concatenate([turned[half:], ones], axis=0).astype(BF16)
        outside = (iota((LANES, LANES), 1) == half + 3).astype(BF16)
        for start in (0, lay.seq + LANES):
            k_aug[start : start + LANES, :] = outside
            v_t[:, start : start + LANES] = jnp.zeros((half + 16, LANES), BF16)
        for place in range(3):
            bucket = bucket_of(
                LANES * (place - 1) + iota((LANES, LANES), 0) - iota((LANES, LANES), 1)
            )
            bias = jnp.zeros((LANES, LANES), F32)
            for label in range(buckets):
                bias = jnp.where(bucket == label, table[0, label], bias)
            biases[place] = bias

    far_left, far_right = table[0, buckets // 2 - 1], table[0, buckets - 1]
    positions = lay.block * tokens + iota((1, tokens), 1)
    seg_q = lay.segment(positions)
    row = iota((2 * half, tokens), 0)
    apart = jnp.logical_or(row - half != seg_q, row == half + 3)
    q_aug = jnp.where(
        row < half, jnp.transpose(query[...].astype(F32)), jnp.where(apart, MASKED, 0.0)
    ).astype(BF16)

    near = dot_nn(k_aug[pl.ds(lay.first, lay.near), :], q_aug)
    eye = iota((LANES, LANES), 0) == iota((LANES, LANES), 1)
    for sub_q in range(lay.subs):
        lanes = slice(LANES * sub_q, LANES * (sub_q + 1))
        top = None
        for sub_k in range(lay.subs + 2):
            rows = slice(LANES * sub_k, LANES * (sub_k + 1))
            place = sub_k - sub_q
            piece = near[rows, lanes] + (
                far_left if place < 0 else far_right if place > 2 else biases[place]
            )
            if place == 1:
                alone = jnp.logical_and(eye, positions[:, lanes] >= lay.ends[2])
                piece = jnp.where(alone, 0.0, piece)
            scores[rows, lanes] = piece
            high = jnp.max(fold(piece), axis=0)
            top = high if top is None else jnp.maximum(top, high)
        best[:, lanes] = top

    def score(tile):
        piece = dot_nn(k_aug[lay.keys_of(tile), :], q_aug)
        scores[lay.rows_of(tile), :] = piece
        const = jnp.where(tile < lay.lefts, far_left, far_right)
        return jnp.max(fold(piece), axis=0) + const

    def score_group(index, top):
        for step in range(GROUP):
            top = jnp.maximum(top, score(index * GROUP + step))
        return top

    best[...] = lax.fori_loop(0, lay.loops, score_group, best[...])

    @pl.when(lay.edge)
    def _():
        best[...] = jnp.maximum(best[...], score(lay.loops * GROUP))

    peak = jnp.max(best[...], axis=0, keepdims=True)
    weights = jnp.exp(scores[: lay.near, :] - peak).astype(BF16)
    probs[: lay.near, :] = weights
    total = dot_nn(v_t[:, pl.ds(lay.first, lay.near)], weights)

    def weigh(tile):
        const = jnp.where(tile < lay.lefts, far_left, far_right)
        rows = lay.rows_of(tile)
        part = jnp.exp(scores[rows, :] - (peak - const)).astype(BF16)
        probs[rows, :] = part
        return dot_nn(v_t[:, lay.keys_of(tile)], part)

    def weigh_group(index, total):
        return total + sum(weigh(index * GROUP + step) for step in range(GROUP))

    stats[...] = lax.fori_loop(0, lay.loops, weigh_group, total)

    @pl.when(lay.edge)
    def _():
        stats[...] += weigh(lay.loops * GROUP)

    inverse = 1.0 / stats[half : half + 1, :]
    result = stats[:half, :] * inverse
    context[...] = result.astype(BF16)
    stats[:half, :] = result
    stats[half : half + 1, :] = inverse


def backward_kernel(tokens, groups, splits, ints, query, d_context, stats, probs, *refs):
    kvs, d_query, d_kvs = refs[:splits], refs[splits], refs[splits + 1 : 2 * splits + 1]
    d_table, v_aug, k_t, d_kv, bands, sides, d_q = refs[2 * splits + 1 :]
    lay = Layout(tokens, groups, splits, ints)
    half = query.shape[1] // 2
    buckets = d_table.shape[0]

    @pl.when(pl.program_id(0) == 0)
    def prepare():
        lane = iota((tokens, LANES), 1)
        for slot in range(groups):
            for other in range(splits):
                start = lay.block_of(slot, other) * tokens
                rows = pl.ds(pl.multiple_of(LANES + start, LANES), tokens)
                kv = kvs[other][slot * tokens : (slot + 1) * tokens, :].astype(F32)
                v_aug[rows, :] = jnp.where(lane >= half, kv, (lane < 3).astype(F32)).astype(BF16)
                ones = (iota((16, tokens), 0) == 0).astype(F32)
                k_t[:, rows] = jnp.concatenate([jnp.transpose(kv)[:half], ones], axis=0).astype(BF16)
        for start in (0, lay.seq + LANES):
            v_aug[start : start + LANES, :] = jnp.zeros((LANES, LANES), BF16)
            k_t[:, start : start + LANES] = jnp.zeros((half + 16, LANES), BF16)
        d_kv[...] = jnp.zeros_like(d_kv)
        bands[...] = jnp.zeros_like(bands)
        sides[...] = jnp.zeros_like(sides)

    inverse = stats[half : half + 1, :]
    upstream = d_context[...].astype(F32)
    delta = jnp.sum(upstream * stats[:half, :], axis=0, keepdims=True) * inverse
    scaled = upstream * inverse
    high = delta.astype(BF16).astype(F32)
    middle = (delta - high).astype(BF16).astype(F32)
    low = delta - high - middle
    row = iota((half, tokens), 0)
    shift = jnp.where(row == 0, high, jnp.where(row == 1, middle, jnp.where(row == 2, low, 0.0)))
    up_aug = jnp.concatenate([-shift, scaled], axis=0).astype(BF16)
    up_rows = jnp.transpose(jnp.concatenate([jnp.zeros_like(scaled), scaled], axis=0)).astype(BF16)
    both = jnp.concatenate([query[...], up_rows], axis=0)

    def grads(keys, rows):
        part = probs[rows, :]
        d_scores = part.astype(F32) * dot_nn(v_aug[keys, :], up_aug)
        rounded = d_scores.astype(BF16)
        d_kv[keys, :] += dot_nn(jnp.concatenate([rounded, part], axis=1), both)
        return d_scores, dot_nn(k_t[:, keys], rounded)

    near, total = grads(pl.ds(lay.first, lay.near), pl.ds(0, lay.near))
    for sub_q in range(lay.subs):
        lanes = slice(LANES * sub_q, LANES * (sub_q + 1))
        for sub_k in range(lay.subs + 2):
            piece = near[LANES * sub_k : LANES * (sub_k + 1), lanes]
            place = sub_k - sub_q
            if 0 <= place <= 2:
                bands[place] += piece
            else:
                sides[int(place > 2), :, lanes] += jnp.sum(fold(piece), axis=0)
    d_q[...] = total
    near_sum = total[half : half + 8, :]

    def far(tile):
        part = grads(lay.keys_of(tile), lay.rows_of(tile))[1]
        return part, jnp.where(tile < lay.lefts, part[half : half + 8, :], 0.0)

    def far_group(index, left):
        parts = [far(index * GROUP + step) for step in range(GROUP)]
        d_q[...] += sum(part for part, _ in parts)
        return left + sum(side for _, side in parts)

    left_sum = lax.fori_loop(0, lay.loops, far_group, jnp.zeros((8, tokens), F32))
    sides[0] += left_sum

    @pl.when(lay.edge)
    def _():
        part, side = far(lay.loops * GROUP)
        d_q[...] += part
        sides[0] += side
        sides[1] -= side

    sides[1] += d_q[half : half + 8, :] - near_sum - left_sum
    d_query[...] = d_q[:half, :].astype(BF16)

    @pl.when(pl.program_id(0) == groups - 1)
    def finish():
        for slot in range(groups):
            for other in range(splits):
                start = lay.block_of(slot, other) * tokens
                rows = pl.ds(pl.multiple_of(LANES + start, LANES), tokens)
                d_kvs[other][slot] = jnp.transpose(d_kv[rows, :]).astype(BF16)
        labels = [
            bucket_of(LANES * (place - 1) + iota((LANES, LANES), 0) - iota((LANES, LANES), 1))
            for place in range(3)
        ]
        for label in range(buckets):
            found = jnp.zeros((8, LANES), F32)
            for place in range(3):
                kept = jnp.where(labels[place] == label, bands[place], 0.0)
                found += jnp.sum(fold(kept), axis=0)
            if label in (buckets // 2 - 1, buckets - 1):
                side = sides[int(label == buckets - 1)]
                for sub in range(lay.subs):
                    found += side[:, LANES * sub : LANES * (sub + 1)]
            d_table[label : label + 1, :] = jnp.sum(found, axis=0, keepdims=True)


def chosen(shape, source):
    return (source(iota((shape[0], 1), 0)) == iota(shape, 1)).astype(F32).astype(BF16)


def project_kernel(dims, ints, weights, own, *refs):
    rows_apart, groups, splits = dims
    others, (normed_t, query, kv, gains, values, order) = refs[:-6], refs[-6:]
    slot, split, group, batch = pl.program_id(0), ints[0], ints[4], ints[5]
    width, narrow = own.shape[1], kv.shape[1]
    unit = width // (rows_apart * groups * splits)

    @pl.when(slot == 0)
    def _():
        def source(index):
            within = lax.rem(index, unit)
            index = index // unit
            g = lax.rem(group + lax.rem(index, groups), groups)
            index = index // groups
            b = lax.rem(batch + lax.rem(index, rows_apart), rows_apart)
            r = lax.rem(split + index // rows_apart, splits)
            return ((b * groups + g) * splits + r) * unit + within

        order[...] = chosen((width, width), source)
        turned = jnp.transpose(weights[:, narrow : narrow + LANES].astype(F32))
        gains[...] = turned[LANES // 2 : LANES // 2 + 8]

    @pl.when(slot == group)
    def _():
        values[...] = own[...]

    for by in range(1, groups):

        @pl.when(slot == group - by)
        def _():
            values[...] = others[by - 1][...]

        @pl.when(slot == group + by)
        def _():
            values[...] = others[groups + by - 2][...]

    normed = rms_scale(values[...].astype(F32), gains[0:1, :]).astype(BF16)
    normed_t[...] = dot_nt(order[...], normed).astype(BF16)
    both = dot_nn(normed, weights[...])
    kv[...] = both[:, :narrow].astype(BF16)
    lane = lax.rem(iota((own.shape[0], narrow), 1), LANES)
    query[...] = jnp.where(lane < LANES // 2, both[:, narrow:], 0.0).astype(BF16)


def project(dims, ints, weights, own, others):
    tokens, width = own.shape
    groups = dims[1]
    narrow = width // 2
    whole = pl.BlockSpec((tokens, width), lambda slot, ints: (0, 0))
    by_row = pl.BlockSpec((tokens, narrow), lambda slot, ints: (slot, 0))
    return pl.pallas_call(
        functools.partial(project_kernel, dims),
        grid_spec=pltpu.PrefetchScalarGridSpec(
            num_scalar_prefetch=1,
            grid=(groups,),
            in_specs=[pl.BlockSpec((width, width), lambda slot, ints: (0, ints[4]))]
            + [whole] * (1 + len(others)),
            out_specs=[
                pl.BlockSpec((width, tokens), lambda slot, ints: (0, slot)),
                by_row,
                by_row,
                pl.BlockSpec((8, width), lambda slot, ints: (0, 0)),
            ],
            scratch_shapes=[pltpu.VMEM((tokens, width), BF16), pltpu.VMEM((width, width), BF16)],
        ),
        out_shape=[
            jax.ShapeDtypeStruct((width, groups * tokens), BF16),
            jax.ShapeDtypeStruct((groups * tokens, narrow), BF16),
            jax.ShapeDtypeStruct((groups * tokens, narrow), BF16),
            jax.ShapeDtypeStruct((8, width), F32),
        ],
        compiler_params=pltpu.CompilerParams(vmem_limit_bytes=VMEM),
        cost_estimate=pl.CostEstimate(
            flops=4 * groups * tokens * width * width,
            bytes_accessed=8 * groups * tokens * width,
            transcendentals=0,
        ),
        name="project",
    )(ints, weights, own, *others)


def split_order(split, splits, unit):
    def source_of(count):
        part = count // splits

        def source(index):
            r = lax.rem(split + index // part, splits)
            index = lax.rem(index, part)
            return (index // unit * splits + r) * unit + lax.rem(index, unit)

        return source

    return source_of


def block_kernel(
    dims, ints, tokens, most, last, w_out, gains, w_gate, w_up, w_down, upstream, *refs
):
    rows_apart, groups, splits = dims
    result, d_mixed, d_first, d_rest = refs[:4]
    grads_wide, grads_down = refs[4 : 4 + splits], refs[4 + splits : 4 + 2 * splits]
    (context_t, mixed, normed, normed_t, d_normed, total, order, order_hidden) = refs[4 + 2 * splits :]
    step, chunks = pl.program_id(0), pl.num_programs(0) - 1
    width, chunk = w_gate.shape
    devices = rows_apart * groups * splits
    hidden_unit = chunk * chunks // devices
    gain = gains[1:2, :]

    @pl.when(step == 0)
    def first():
        order[...] = chosen(
            (width, width), split_order(ints[0], splits, width // devices)(width)
        )
        order_hidden[...] = chosen((chunk, chunk), split_order(ints[0], splits, hidden_unit)(chunk))
        each = last.shape[1]
        size = width // groups
        for g in range(groups):
            context_t[size * g : size * (g + 1) - each, :] = most[g]
            context_t[size * (g + 1) - each : size * (g + 1), :] = last[g]
        context = jnp.transpose(context_t[...].astype(F32)).astype(BF16)
        values = tokens[...].astype(F32) + dot_nn(context, w_out[...])
        mixed[...] = values
        total[...] = values
        normed[...] = rms_scale(values, gain).astype(BF16)
        normed_t[...] = dot_nt(order[...], normed[...]).astype(BF16)
        d_normed[...] = jnp.zeros_like(d_normed)

    def stored(outs, rows, values):
        part = values.shape[0] // splits
        for other in range(splits):
            outs[other][:, rows] = values[part * other : part * (other + 1)].astype(BF16)

    @pl.when(step < chunks)
    def work():
        gate = dot_nn(normed[...], w_gate[...])
        upward = dot_nn(normed[...], w_up[...])
        d_hidden = dot_nt(upstream[...], w_down[...])
        square = gate * gate
        turn = jnp.tanh(GELU_SCALE * (gate + 0.044715 * gate * square))
        half = 0.5 * (1.0 + turn)
        active = gate * half
        slope = half + 0.5 * gate * (1.0 - turn * turn) * (GELU_SCALE * (1.0 + 0.134145 * square))
        hidden = (active * upward).astype(BF16)
        d_gate = (d_hidden * upward * slope).astype(BF16)
        d_up = (d_hidden * active).astype(BF16)
        total[...] += dot_nn(hidden, w_down[...])
        d_normed[...] += dot_nt(d_gate, w_gate[...]) + dot_nt(d_up, w_up[...])
        hidden_t = dot_nt(order_hidden[...], hidden).astype(BF16)

        stored(grads_down, slice(None), dot_nn(hidden_t, upstream[...]))
        stored(grads_wide, slice(0, chunk), dot_nn(normed_t[...], d_gate))
        stored(grads_wide, slice(chunk, 2 * chunk), dot_nn(normed_t[...], d_up))

    @pl.when(step == chunks)
    def finish():
        result[...] = total[...].astype(BF16)
        back = upstream[...].astype(F32) + rms_back(mixed[...], gain, d_normed[...])
        d_mixed[...] = back
        branch = back.astype(BF16)
        d_context = dot_nt(w_out[...], branch).astype(BF16)
        each = d_first.shape[1]
        size = width // groups
        for g in range(groups):
            d_first[g] = d_context[size * g : size * g + each]
            d_rest[g] = d_context[size * g + each : size * (g + 1)]
        ordered = dot_nn(order[...], context_t[...]).astype(BF16)
        stored(grads_wide, slice(0, width), dot_nn(ordered, branch))
        for out in grads_wide:
            out[:, width:] = jnp.zeros((out.shape[0], out.shape[1] - width), BF16)


def feed_forward(dims, ints, tokens, most, last, early, gains, late, w_down, upstream):
    groups, splits = dims[1:]
    rows, width = tokens.shape
    hidden = w_down.shape[0]
    chunk = 2 * TILE
    steps = hidden // chunk
    each = last.shape[1]
    full = lambda *shape: pl.BlockSpec(shape, lambda step: (0,) * len(shape))
    return pl.pallas_call(
        functools.partial(block_kernel, dims),
        grid=(steps + 1,),
        in_specs=[
            smem(),
            full(rows, width),
            full(*most.shape),
            full(*last.shape),
            pl.BlockSpec((width, width), lambda step: (0, groups)),
            full(8, width),
            pl.BlockSpec((width, chunk), lambda step: (0, jnp.minimum(step, steps - 1))),
            pl.BlockSpec((width, chunk), lambda step: (0, steps + jnp.minimum(step, steps - 1))),
            pl.BlockSpec((chunk, width), lambda step: (jnp.minimum(step, steps - 1), 0)),
            full(rows, width),
        ],
        out_specs=[
            full(rows, width),
            full(rows, width),
            full(groups, each, rows),
            full(groups, width // groups - each, rows),
        ]
        + [pl.BlockSpec((width // splits, 2 * chunk), lambda step: (0, step))] * splits
        + [pl.BlockSpec((chunk // splits, width), lambda step: (jnp.minimum(step, steps - 1), 0))]
        * splits,
        out_shape=[
            jax.ShapeDtypeStruct((rows, width), BF16),
            jax.ShapeDtypeStruct((rows, width), F32),
            jax.ShapeDtypeStruct((groups, each, rows), BF16),
            jax.ShapeDtypeStruct((groups, width // groups - each, rows), BF16),
        ]
        + [jax.ShapeDtypeStruct((width // splits, 2 * hidden + 2 * chunk), BF16)] * splits
        + [jax.ShapeDtypeStruct((hidden // splits, width), BF16)] * splits,
        scratch_shapes=[
            pltpu.VMEM((width, rows), BF16),
            pltpu.VMEM((rows, width), F32),
            pltpu.VMEM((rows, width), BF16),
            pltpu.VMEM((width, rows), BF16),
            pltpu.VMEM((rows, width), F32),
            pltpu.VMEM((rows, width), F32),
            pltpu.VMEM((width, width), BF16),
            pltpu.VMEM((chunk, chunk), BF16),
        ],
        compiler_params=pltpu.CompilerParams(vmem_limit_bytes=VMEM),
        cost_estimate=pl.CostEstimate(
            flops=18 * rows * width * hidden + 6 * rows * width * width,
            bytes_accessed=12 * width * hidden,
            transcendentals=rows * hidden,
        ),
        name="feed_forward",
    )(ints, tokens, most, last, early, gains, late, late, w_down, upstream)


def weight_kernel(splits, normed_t, *refs):
    d_heads, outs, total = refs[: -splits - 1], refs[-splits - 1 : -1], refs[-1]
    step = pl.program_id(0)
    added = dot_nt(normed_t[...], jnp.concatenate([d_head[...] for d_head in d_heads], axis=0))

    @pl.when(step == 0)
    def _():
        total[...] = added

    @pl.when(step > 0)
    def _():
        total[...] += added

    @pl.when(step == pl.num_programs(0) - 1)
    def _():
        part = total.shape[0] // splits
        for other in range(splits):
            outs[other][...] = total[part * other : part * (other + 1), :].astype(BF16)


def weight_grads(splits, normed_t, d_heads):
    groups, rows, tokens = d_heads[0].shape
    width = normed_t.shape[0]
    out = (width // splits, rows * len(d_heads))
    return pl.pallas_call(
        functools.partial(weight_kernel, splits),
        grid=(groups,),
        in_specs=[pl.BlockSpec((width, tokens), lambda step: (0, step))]
        + [by_slot(rows, tokens)] * len(d_heads),
        out_specs=[pl.BlockSpec(out, lambda step: (0, 0))] * splits,
        out_shape=[jax.ShapeDtypeStruct(out, BF16)] * splits,
        scratch_shapes=[pltpu.VMEM((width, out[1]), F32)],
        compiler_params=pltpu.CompilerParams(vmem_limit_bytes=VMEM),
        name="weight_grads",
    )(normed_t, *d_heads)


def added_kernel(count, *refs):
    held, outs = refs[:count], refs[count:]
    total = held[0][...].astype(F32)
    for piece in held[1:]:
        total += piece[...].astype(F32)
    part = total.shape[0] // len(outs)
    for index, out in enumerate(outs):
        out[...] = total[part * index : part * (index + 1)].astype(out.dtype)


def added(pieces, parts):
    rows, columns = pieces[0].shape
    return pl.pallas_call(
        functools.partial(added_kernel, len(pieces)),
        out_shape=[jax.ShapeDtypeStruct((rows // parts, columns), BF16)] * parts,
        compiler_params=pltpu.CompilerParams(vmem_limit_bytes=VMEM),
        name="added",
    )(*pieces)


def unpacked(pieces, heads, size):
    return jnp.concatenate(
        [
            piece[:, (3 * head + part) * size : (3 * head + part + 1) * size]
            for part in range(3)
            for piece in pieces
            for head in range(heads)
        ],
        axis=1,
    )


def count_kernel(groups, heads, size, count, ints, *refs):
    held, tables, (rest, down) = refs[:count], refs[count : count + heads], refs[count + heads :][:2]
    outs, counts = refs[count + heads + 2 : -1], refs[-1]
    total = held[0][...].astype(F32)
    for piece in held[1:]:
        total += piece[...].astype(F32)
    part = total.shape[0] // groups
    for index, out in enumerate(outs):
        out[...] = total[part * index : part * (index + 1)]
    squares = jnp.sum(total * total, axis=0, keepdims=True)
    table = jnp.concatenate(
        [jnp.sum(jnp.transpose(table[...]), axis=0, keepdims=True) for table in tables], axis=1
    )
    mine = [(ints[4] == g).astype(F32) for g in range(groups)]
    rest_values, down_values = rest[...].astype(F32), down[...].astype(F32)
    row = jnp.concatenate(
        [table * own for own in mine]
        + [unpacked([squares * own for own in mine], heads, size)]
        + [jnp.sum(rest_values * rest_values, axis=0, keepdims=True)]
        + [jnp.sum(down_values * down_values, axis=0, keepdims=True)],
        axis=1,
    )
    for index in range(counts.shape[0]):
        counts[index : index + 1, :] = row[:, LANES * index : LANES * (index + 1)]


def counted(groups, heads, size, ints, pieces, tables, rest, down):
    rows, columns = pieces[0].shape
    buckets = tables[0].shape[0]
    length = groups * (heads * buckets + columns) + rest.shape[1] + down.shape[1]
    vmem = pl.BlockSpec(memory_space=pltpu.VMEM)
    return pl.pallas_call(
        functools.partial(count_kernel, groups, heads, size, len(pieces)),
        in_specs=[smem()] + [vmem] * (len(pieces) + len(tables) + 2),
        out_shape=[jax.ShapeDtypeStruct((rows // groups, columns), F32)] * groups
        + [jax.ShapeDtypeStruct((length // LANES, LANES), F32)],
        compiler_params=pltpu.CompilerParams(vmem_limit_bytes=VMEM),
        name="counted",
    )(ints, *pieces, *tables, rest, down)


def input_kernel(heads, weights, own, gains, d_mixed, *refs):
    d_heads, (out, total) = refs[:heads], refs[heads:]
    step = pl.program_id(0)
    size = d_heads[0].shape[0] // 3
    blank = jnp.zeros((size, own.shape[0]), F32)
    pieces = [d_head[size:, :].astype(F32) for d_head in d_heads]
    for d_head in d_heads:
        pieces += [d_head[:size, :].astype(F32), blank]
    turned = jnp.transpose(jnp.concatenate(pieces, axis=0)).astype(BF16)
    added = dot_nt(turned, weights[...])

    @pl.when(step == 0)
    def _():
        total[...] = added

    @pl.when(step > 0)
    def _():
        total[...] += added

    @pl.when(step == pl.num_programs(0) - 1)
    def _():
        back = rms_back(own[...].astype(F32), gains[0:1, :], total[...])
        out[...] = (d_mixed[...] + back).astype(BF16)


def input_grads(groups, weights, own, gains, d_mixed, d_heads):
    tokens, width = own.shape
    full = lambda *shape: pl.BlockSpec(shape, lambda step: (0,) * len(shape))
    return pl.pallas_call(
        functools.partial(input_kernel, len(d_heads)),
        grid=(groups,),
        in_specs=[
            pl.BlockSpec((width, width), lambda step: (0, step)),
            full(tokens, width),
            full(8, width),
            full(tokens, width),
        ]
        + [by_slot(*d_heads[0].shape[1:])] * len(d_heads),
        out_specs=full(tokens, width),
        out_shape=jax.ShapeDtypeStruct((tokens, width), BF16),
        scratch_shapes=[pltpu.VMEM((tokens, width), F32)],
        compiler_params=pltpu.CompilerParams(vmem_limit_bytes=VMEM),
        name="input_grads",
    )(weights, own, gains, d_mixed, *d_heads)


def by_slot(rows, tokens):
    return pl.BlockSpec((None, rows, tokens), lambda slot: (slot, 0, 0))


def smem():
    return pl.BlockSpec(memory_space=pltpu.SMEM)


def attend(head, tokens, groups, splits, ints, table, query, kvs):
    seq, rows = tokens * groups * splits, tokens * groups
    half = LANES // 2
    whole = pl.BlockSpec((rows, LANES), lambda slot: (0, head))
    return pl.pallas_call(
        functools.partial(forward_kernel, tokens, groups, splits),
        grid=(groups,),
        in_specs=[smem(), smem(), pl.BlockSpec((tokens, LANES), lambda slot: (slot, head))]
        + [whole] * splits,
        out_specs=[
            pl.BlockSpec((seq, tokens), lambda slot: (slot, 0)),
            by_slot(half, tokens),
            by_slot(half + 16, tokens),
        ],
        out_shape=[
            jax.ShapeDtypeStruct((groups * seq, tokens), BF16),
            jax.ShapeDtypeStruct((groups, half, tokens), BF16),
            jax.ShapeDtypeStruct((groups, half + 16, tokens), F32),
        ],
        scratch_shapes=[
            pltpu.VMEM((seq + 2 * LANES, LANES), BF16),
            pltpu.VMEM((half + 16, seq + 2 * LANES), BF16),
            pltpu.VMEM((seq, tokens), F32),
            pltpu.VMEM((3, LANES, LANES), F32),
            pltpu.VMEM((8, tokens), F32),
        ],
        compiler_params=pltpu.CompilerParams(vmem_limit_bytes=VMEM),
        cost_estimate=pl.CostEstimate(
            flops=16 * seq * rows * half, bytes_accessed=2 * seq * rows, transcendentals=seq * rows
        ),
        name="attend",
    )(ints, table, query, *kvs)


def attend_back(
    head, tokens, groups, splits, ints, buckets, query, d_context, place, stats, probs, kvs
):
    seq, rows = tokens * groups * splits, tokens * groups
    half = LANES // 2
    whole = pl.BlockSpec((rows, LANES), lambda slot: (0, head))
    kept = pl.BlockSpec((groups, LANES, tokens), lambda slot: (0, 0, 0))
    return pl.pallas_call(
        functools.partial(backward_kernel, tokens, groups, splits),
        grid=(groups,),
        in_specs=[
            smem(),
            pl.BlockSpec((tokens, LANES), lambda slot: (slot, head)),
            pl.BlockSpec((None, None, half, tokens), lambda slot: (slot, place, 0, 0)),
            by_slot(half + 16, tokens),
            pl.BlockSpec((seq, tokens), lambda slot: (slot, 0)),
        ]
        + [whole] * splits,
        out_specs=[by_slot(half, tokens)]
        + [kept] * splits
        + [pl.BlockSpec((buckets, LANES), lambda slot: (0, 0))],
        out_shape=[jax.ShapeDtypeStruct((groups, half, tokens), BF16)]
        + [jax.ShapeDtypeStruct((groups, LANES, tokens), BF16)] * splits
        + [jax.ShapeDtypeStruct((buckets, LANES), F32)],
        scratch_shapes=[
            pltpu.VMEM((seq + 2 * LANES, LANES), BF16),
            pltpu.VMEM((half + 16, seq + 2 * LANES), BF16),
            pltpu.VMEM((seq + 2 * LANES, LANES), F32),
            pltpu.VMEM((3, LANES, LANES), F32),
            pltpu.VMEM((2, 8, tokens), F32),
            pltpu.VMEM((half + 16, tokens), F32),
        ],
        compiler_params=pltpu.CompilerParams(vmem_limit_bytes=VMEM),
        cost_estimate=pl.CostEstimate(
            flops=32 * seq * rows * half, bytes_accessed=2 * seq * rows, transcendentals=0
        ),
        name="attend_back",
    )(ints, query, d_context, stats, probs, *kvs)


def factored(grad_shard, column_total, row_old, column_old, row_total):
    columns = grad_shard.shape[1]
    mean_square = jnp.sum(column_total) / (row_total * columns) + EPSILON
    row_new = (
        DECAY_RATE * row_old
        + (1.0 - DECAY_RATE) * (jnp.sum(grad_shard * grad_shard, axis=1) / columns) / mean_square
    )
    column_new = (
        DECAY_RATE * column_old + (1.0 - DECAY_RATE) * (column_total / row_total) / mean_square
    )
    return (row_new, column_new)


def shards(
    tokens,
    lengths,
    norm_one,
    w_qkv,
    rel_table,
    w_out,
    norm_two,
    w_gateup,
    w_down,
    cotangent,
    row_qkv,
    col_qkv,
    row_out,
    col_out,
    row_gateup,
    col_gateup,
    row_down,
    col_down,
):
    own = tokens[0]
    tok_rows, width = own.shape
    heads = rel_table.shape[1]
    buckets = rel_table.shape[0]
    rows_apart, groups, splits = (lax.axis_size(name) for name in ALL)
    group_heads = heads // groups
    head_size = width // heads
    group, split = lax.axis_index("group"), lax.axis_index("split")
    group_width = width // groups

    def ahead(array, axis, by):
        size = lax.axis_size(axis)
        return lax.ppermute(array, axis, [((i + by) % size, i) for i in range(size)])

    def swap_groups(array):
        return lax.all_to_all(array, "group", 0, 0)

    def swap_rows(array):
        return lax.all_to_all(array, "batch", 0, 0)

    def all_sum(array, other):
        for axis in ALL:
            array = sum([ahead(array, axis, by) for by in range(1, lax.axis_size(axis))], array)
            if axis == "batch":
                array = after(array, other)
        return array

    def line(array, by):
        pairs = [(i, i + by) for i in range(groups) if 0 <= i + by < groups]
        return lax.ppermute(array, "group", pairs)

    before, behind = [own], [own]
    for _ in range(groups - 1):
        before.append(line(before[-1], 1))
        behind.append(line(behind[-1], -1))

    unit = w_qkv.shape[0]
    by_part = w_qkv.reshape(unit, 3, groups, group_heads, head_size)
    gains = jnp.pad(jnp.stack([norm_one, norm_two], axis=1), ((0, 0), (0, head_size - 2)))
    beside = jnp.pad(gains[:, None, None], ((0, 0), (0, 0), (0, group_heads - 1), (0, 0)))
    beside = jnp.broadcast_to(beside, (unit, groups, group_heads, head_size))
    packed = jnp.concatenate(
        [
            jnp.concatenate([by_part[:, 1], by_part[:, 2]], axis=-1),
            jnp.concatenate([by_part[:, 0], beside], axis=-1),
        ],
        axis=2,
    )
    early = lax.all_gather(
        jnp.concatenate([packed.reshape(unit, -1), w_out], axis=1), ALL, axis=0, tiled=True
    )
    late = lax.all_gather(
        after(
            jnp.concatenate([w_gateup, w_down.reshape(unit, -1)], axis=1),
            early,
            before[-1],
            behind[-1],
        ),
        ALL,
        axis=0,
        tiled=True,
    )
    full_down = late[:, w_gateup.shape[1] :].reshape(-1, width)

    dims = (rows_apart, groups, splits)
    ends = jnp.cumsum(lengths[0])
    ints = jnp.concatenate(
        [
            split.astype(jnp.int32)[None],
            ends.astype(jnp.int32),
            jnp.stack([group, lax.axis_index("batch")]).astype(jnp.int32),
        ]
    )
    normed_t, query, kv, gains = project(dims, ints, early, own, before[1:] + behind[1:])
    kvs = [kv] + [ahead(kv, "split", other) for other in range(1, splits)]

    table_own = lax.dynamic_slice_in_dim(rel_table.T, group * group_heads, group_heads, 0)

    contexts, stats, probs = [], [], []
    for head in range(group_heads):
        prob, context, stat = attend(
            head,
            tok_rows,
            groups,
            splits,
            after(ints, *contexts[-1:]),
            table_own[head : head + 1],
            query,
            kvs,
        )
        contexts.append(context)
        stats.append(stat)
        probs.append(prob)
    most = swap_groups(jnp.concatenate(contexts[:-1], axis=1))
    last = swap_groups(after(contexts[-1], most))

    outs = feed_forward(
        dims, ints, own, most, last, early, gains, late, full_down, cotangent[0]
    )
    result, d_mixed, d_first, d_rest = outs[:4]
    grads_wide, grads_down = outs[4 : 4 + splits], outs[4 + splits :]

    def split_sum(grads):
        held = grads[0].astype(F32)
        for by in range(1, splits):
            held = held + ahead(grads[by], "split", splits - by).astype(F32)
        return held.astype(BF16).reshape(rows_apart, groups, -1, held.shape[-1])

    d_first = swap_groups(d_first)
    d_rest = swap_groups(d_rest)
    d_contexts = [d_first[:, None], d_rest.reshape(groups, group_heads - 1, head_size, tok_rows)]
    held_rest = split_sum(grads_wide)
    held_down = split_sum(grads_down)
    rest = after(lax.psum_scatter(held_rest, "batch", scatter_dimension=0))
    down = after(lax.psum_scatter(held_down, "batch", scatter_dimension=0))
    rest_own = lax.psum_scatter(rest, "group", scatter_dimension=0)
    down_own = lax.psum_scatter(down, "group", scatter_dimension=0)

    d_heads, d_received, d_tables = [], [], []
    ready = [(held_rest,), (held_down,)] + [(rest, down)] * (group_heads - 2)
    for head in range(group_heads):
        outs = attend_back(
            head,
            tok_rows,
            groups,
            splits,
            ints,
            buckets,
            query,
            after(d_contexts[int(head > 0)], *ready[head], *d_heads[-1:]),
            head - int(head > 0),
            stats[head],
            probs[head],
            kvs,
        )
        beside = [d_received[-1] if head else d_contexts[1]]
        if head == group_heads - 1:
            beside += [rest_own, down_own]
        outs = lax.optimization_barrier((*outs, *beside))[: -len(beside)]
        d_kv = outs[1].astype(F32)
        for other in range(1, splits):
            d_kv = d_kv + ahead(outs[1 + other], "split", splits - other).astype(F32)
        d_head = jnp.concatenate([outs[0], d_kv.astype(BF16)], axis=1)
        d_heads.append(d_head)
        d_received.append(swap_groups(d_head))
        d_tables.append(outs[-1])

    d_inputs = input_grads(groups, early, own, gains, d_mixed, d_received)

    grads = weight_grads(splits, normed_t, d_heads)
    held = added(
        [grads[0]] + [ahead(grads[by], "split", splits - by) for by in range(1, splits)], rows_apart
    )
    held = [held[0]] + [ahead(held[by], "batch", rows_apart - by) for by in range(1, rows_apart)]
    *columns, counts = counted(
        groups, group_heads, head_size, ints, held, d_tables, rest_own, down_own
    )
    columns = [columns[0]] + [ahead(columns[by], "group", groups - by) for by in range(1, groups)]
    pieces = []
    for index in range(groups):
        piece = columns[0]
        for by in range(1, groups):
            piece = jnp.where((group + groups - by) % groups == index, columns[by], piece)
        pieces.append(piece)
    shard_qkv = unpacked(pieces, group_heads, head_size)
    steps = w_down.shape[0] * rows_apart * groups * splits // (2 * TILE)

    def in_order(array):
        array = array.reshape(*array.shape[:-1], steps, 2, -1)
        return jnp.swapaxes(array, -3, -2).reshape(*array.shape[:-3], -1)

    shard_rest = rest_own.astype(F32)
    shard_gateup = in_order(shard_rest[:, : w_gateup.shape[1]])
    shard_out = shard_rest[:, w_gateup.shape[1] :][:, :width]
    shard_down = down_own.astype(F32)
    summed = all_sum(counts, d_inputs).reshape(-1)
    extra = rest_own.shape[1] - w_gateup.shape[1] - width
    sizes = (heads * buckets, 3 * width, w_gateup.shape[1], width, extra, width)
    table_total, column_qkv, column_gateup, column_out, _, column_down = jnp.split(
        summed, [sum(sizes[: i + 1]) for i in range(len(sizes) - 1)]
    )
    table_total = table_total.reshape(heads, buckets)
    column_gateup = in_order(column_gateup)
    shard_gain_one = jnp.sum(w_qkv.astype(F32) * shard_qkv, axis=1) / norm_one.astype(F32)
    shard_gain_two = jnp.sum(w_gateup.astype(F32) * shard_gateup, axis=1) / norm_two.astype(F32)
    new_row_qkv, new_col_qkv = factored(shard_qkv, column_qkv, row_qkv, col_qkv, width)
    new_row_out, new_col_out = factored(shard_out, column_out, row_out, col_out, width)
    new_row_gateup, new_col_gateup = factored(
        shard_gateup, column_gateup, row_gateup, col_gateup, width
    )
    new_row_down, new_col_down = factored(
        shard_down, column_down, row_down, col_down, full_down.shape[0]
    )
    return (
        result[None],
        d_inputs[None],
        shard_gain_one,
        shard_qkv,
        table_total.T,
        shard_out,
        shard_gain_two,
        shard_gateup,
        shard_down,
        new_row_qkv,
        new_col_qkv,
        new_row_out,
        new_col_out,
        new_row_gateup,
        new_col_gateup,
        new_row_down,
        new_col_down,
    )


def solution(mesh):
    row_blocks = P("batch", ("group", "split"), None)
    split_rows = P(ALL, None)
    split_row = P(ALL)

    def run(*arrays):
        rows, ring = mesh.devices.shape
        groups = math.gcd(ring, arrays[4].shape[1])
        fine = Mesh(mesh.devices.reshape(rows, groups, ring // groups), ALL)
        return jax.shard_map(
            shards,
            mesh=fine,
            in_specs=(
                row_blocks,
                P("batch", None),
                split_row,
                split_rows,
                P(),
                split_rows,
                split_row,
                split_rows,
                split_rows,
                row_blocks,
            )
            + (split_row, P()) * 4,
            out_specs=(
                row_blocks,
                row_blocks,
                split_row,
                split_rows,
                P(),
                split_rows,
                split_row,
                split_rows,
                split_rows,
            )
            + (split_row, P()) * 4,
            check_vma=False,
        )(*arrays)

    return run
```

```python
import functools
import math

import jax
import jax.numpy as jnp
from jax import lax
from jax.experimental import pallas as pl
from jax.experimental.pallas import tpu as pltpu
from jax.sharding import Mesh
from jax.sharding import PartitionSpec as P

THRESHOLDS = (12, 16, 23, 32, 46, 64, 91)
EPSILON = 1e-06
DECAY_RATE = 0.5
GELU_SCALE = 0.7978845608028654
MASKED = -1e9
LEEWAY = 20.0
ALL = ("batch", "group", "split")
LANES = 128
TILE = 256
GROUP = 4
VMEM = 56 * 2**20
F32 = jnp.float32
BF16 = jnp.bfloat16


def bucket_of(offset):
    distance = jnp.abs(offset)
    steps_up = 8 + sum(((distance >= limit).astype(jnp.int32) for limit in THRESHOLDS))
    within = jnp.where(distance < 8, distance, steps_up)
    return within + 16 * (offset > 0).astype(jnp.int32)


def after(value, *others):
    return lax.optimization_barrier((value, *others))[0]


def rms_scale(values, gain):
    return values * lax.rsqrt(jnp.mean(values * values, axis=-1, keepdims=True) + EPSILON) * gain


def rms_back(values, gain, grad):
    scale = lax.rsqrt(jnp.mean(values * values, axis=-1, keepdims=True) + EPSILON)
    scaled = grad * gain
    return scale * scaled - values * scale**3 * jnp.mean(scaled * values, axis=-1, keepdims=True)


def dot_nn(left, right):
    return jnp.dot(left, right, preferred_element_type=F32)


def dot_nt(left, right):
    return lax.dot_general(left, right, (((1,), (1,)), ((), ())), preferred_element_type=F32)


def dot_tt(left, right):
    return lax.dot_general(left, right, (((0,), (1,)), ((), ())), preferred_element_type=F32)


class Layout:
    def __init__(self, tokens, groups, splits, ints):
        self.tokens, self.groups, self.splits = tokens, groups, splits
        self.blocks = groups * splits
        self.seq = tokens * self.blocks
        self.near = tokens + 2 * LANES
        self.subs = tokens // LANES
        self.split = ints[0]
        self.ends = (ints[1], ints[2], ints[3])
        slot = pl.program_id(0)
        self.block = self.block_of(slot, 0)
        self.first = pl.multiple_of(self.block * tokens, LANES)
        self.lefts = jnp.maximum(0, self.block * (tokens // TILE) - 1)
        self.loops = (self.seq // TILE - 2 - tokens // TILE) // GROUP
        self.edge = jnp.logical_or(self.block == 0, self.block == self.blocks - 1)

    def block_of(self, slot, other):
        return slot * self.splits + lax.rem(self.split + other, self.splits)

    def keys_of(self, tile):
        before = 2 * LANES + TILE * tile
        after = self.first + self.near + TILE * (tile - self.lefts)
        return pl.ds(pl.multiple_of(jnp.where(tile < self.lefts, before, after), LANES), TILE)

    def rows_of(self, tile):
        return pl.ds(pl.multiple_of(self.near + TILE * tile, LANES), TILE)

    def segment(self, positions):
        return sum((positions >= end).astype(jnp.int32) for end in self.ends)


def iota(shape, dim):
    return lax.broadcasted_iota(jnp.int32, shape, dim)


def fold(values):
    return values.reshape(values.shape[0] // 8, 8, values.shape[1])


def forward_kernel(tokens, groups, splits, ints, table, query, *refs):
    kvs, (probs, context, stats, k_aug, v_t, scores, biases, best) = refs[:splits], refs[splits:]
    lay = Layout(tokens, groups, splits, ints)
    half = query.shape[1] // 2
    buckets = table.shape[1]

    @pl.when(pl.program_id(0) == 0)
    def prepare():
        lane = iota((tokens, LANES), 1)
        for slot in range(groups):
            for other in range(splits):
                start = lay.block_of(slot, other) * tokens
                rows = pl.ds(pl.multiple_of(LANES + start, LANES), tokens)
                kv = kvs[other][slot * tokens : (slot + 1) * tokens, :].astype(F32)
                seg = lay.segment(start + iota((tokens, LANES), 0))
                k_aug[rows, :] = jnp.where(lane < half, kv, (lane - half == seg).astype(F32)).astype(BF16)
                turned = jnp.transpose(kv)
                ones = (iota((16, tokens), 0) == 0).astype(F32)
                v_t[:, rows] = jnp.concatenate([turned[half:], ones], axis=0).astype(BF16)
        outside = (iota((LANES, LANES), 1) == half + 3).astype(BF16)
        for start in (0, lay.seq + LANES):
            k_aug[start : start + LANES, :] = outside
            v_t[:, start : start + LANES] = jnp.zeros((half + 16, LANES), BF16)
        for place in range(3):
            bucket = bucket_of(
                LANES * (place - 1) + iota((LANES, LANES), 0) - iota((LANES, LANES), 1)
            )
            bias = jnp.zeros((LANES, LANES), F32)
            for label in range(buckets):
                bias = jnp.where(bucket == label, table[0, label], bias)
            biases[place] = bias

    far_left, far_right = table[0, buckets // 2 - 1], table[0, buckets - 1]
    positions = lay.block * tokens + iota((1, tokens), 1)
    seg_q = lay.segment(positions)
    row = iota((2 * half, tokens), 0)
    apart = jnp.logical_or(row - half != seg_q, row == half + 3)
    q_aug = jnp.where(
        row < half, jnp.transpose(query[...].astype(F32)), jnp.where(apart, MASKED, 0.0)
    ).astype(BF16)

    near = dot_nn(k_aug[pl.ds(lay.first, lay.near), :], q_aug)
    eye = iota((LANES, LANES), 0) == iota((LANES, LANES), 1)
    for sub_q in range(lay.subs):
        lanes = slice(LANES * sub_q, LANES * (sub_q + 1))
        top = None
        for sub_k in range(lay.subs + 2):
            rows = slice(LANES * sub_k, LANES * (sub_k + 1))
            place = sub_k - sub_q
            piece = near[rows, lanes] + (
                far_left if place < 0 else far_right if place > 2 else biases[place]
            )
            if place == 1:
                alone = jnp.logical_and(eye, positions[:, lanes] >= lay.ends[2])
                piece = jnp.where(alone, 0.0, piece)
            scores[rows, lanes] = piece
            high = jnp.max(fold(piece), axis=0)
            top = high if top is None else jnp.maximum(top, high)
        best[:, lanes] = top

    def sweep(peak):
        weights = jnp.exp(scores[...] - peak).astype(BF16)
        probs[: lay.near, :] = weights
        stats[...] = dot_nn(v_t[:, pl.ds(lay.first, lay.near)], weights)
        left_peak, right_peak = peak - far_left, peak - far_right

        def tiles(index, count):
            places = [lay.keys_of(index + step) for step in range(count)]
            piece = dot_nn(jnp.concatenate([k_aug[keys, :] for keys in places], axis=0), q_aug)
            parts, top = [], best[...]
            for step in range(count):
                score = piece[TILE * step : TILE * (step + 1)]
                is_left = index + step < lay.lefts
                top = jnp.maximum(
                    top,
                    jnp.max(fold(score), axis=0) + jnp.where(is_left, far_left, far_right),
                )
                part = jnp.exp(score - jnp.where(is_left, left_peak, right_peak)).astype(BF16)
                probs[lay.rows_of(index + step), :] = part
                parts.append(part)
            best[...] = top
            values = jnp.concatenate([v_t[:, keys] for keys in places], axis=1)
            stats[...] += dot_nn(values, jnp.concatenate(parts, axis=0))

        if lay.loops <= 3:
            for index in range(lay.loops):
                tiles(index * GROUP, GROUP)
        else:

            def group(index, carry):
                tiles(index * GROUP, GROUP)
                return carry

            lax.fori_loop(0, lay.loops, group, 0)

        @pl.when(lay.edge)
        def _():
            tiles(lay.loops * GROUP, 1)

    peak = jnp.max(best[...], axis=0, keepdims=True)
    sweep(peak)
    true_peak = jnp.max(best[...], axis=0, keepdims=True)

    @pl.when(jnp.max(true_peak - peak) > LEEWAY)
    def _():
        sweep(true_peak)

    inverse = 1.0 / stats[half : half + 1, :]
    result = stats[:half, :] * inverse
    context[...] = result.astype(BF16)
    stats[:half, :] = result
    stats[half : half + 1, :] = inverse


def backward_kernel(tokens, groups, splits, ints, query, d_context, stats, probs, *refs):
    kvs, d_kvs = refs[:splits], refs[splits : 2 * splits]
    d_table, v_aug, k_t, d_kv, bands, sides, d_q = refs[2 * splits :]
    lay = Layout(tokens, groups, splits, ints)
    half = query.shape[1] // 2
    buckets = d_table.shape[0]

    @pl.when(pl.program_id(0) == 0)
    def prepare():
        lane = iota((tokens, LANES), 1)
        for slot in range(groups):
            for other in range(splits):
                start = lay.block_of(slot, other) * tokens
                rows = pl.ds(pl.multiple_of(LANES + start, LANES), tokens)
                kv = kvs[other][slot * tokens : (slot + 1) * tokens, :].astype(F32)
                v_aug[rows, :] = jnp.where(lane >= half, kv, (lane < 3).astype(F32)).astype(BF16)
                ones = (iota((16, tokens), 0) == 0).astype(F32)
                k_t[:, rows] = jnp.concatenate([jnp.transpose(kv)[:half], ones], axis=0).astype(BF16)
        for start in (0, lay.seq + LANES):
            v_aug[start : start + LANES, :] = jnp.zeros((LANES, LANES), BF16)
            k_t[:, start : start + LANES] = jnp.zeros((half + 16, LANES), BF16)
        d_kv[...] = jnp.zeros_like(d_kv)
        bands[...] = jnp.zeros_like(bands)
        sides[...] = jnp.zeros_like(sides)

    inverse = stats[half : half + 1, :]
    upstream = d_context[...].astype(F32)
    delta = jnp.sum(upstream * stats[:half, :], axis=0, keepdims=True) * inverse
    scaled = upstream * inverse
    high = delta.astype(BF16).astype(F32)
    middle = (delta - high).astype(BF16).astype(F32)
    low = delta - high - middle
    row = iota((half, tokens), 0)
    shift = jnp.where(row == 0, high, jnp.where(row == 1, middle, jnp.where(row == 2, low, 0.0)))
    up_aug = jnp.concatenate([-shift, scaled], axis=0).astype(BF16)
    up_rows = jnp.transpose(jnp.concatenate([jnp.zeros_like(scaled), scaled], axis=0)).astype(BF16)
    both = jnp.concatenate([query[...], up_rows], axis=0)

    def grads(keys, rows):
        part = jnp.concatenate([probs[where, :] for where in rows], axis=0)
        values = jnp.concatenate([v_aug[where, :] for where in keys], axis=0)
        d_scores = part.astype(F32) * dot_nn(values, up_aug)
        rounded = d_scores.astype(BF16)
        added = dot_nn(jnp.concatenate([rounded, part], axis=1), both)
        size = part.shape[0] // len(keys)
        for index, where in enumerate(keys):
            d_kv[where, :] += added[size * index : size * (index + 1)]
        return d_scores, rounded

    near, rounded = grads([pl.ds(lay.first, lay.near)], [pl.ds(0, lay.near)])
    total = dot_nn(k_t[:, pl.ds(lay.first, lay.near)], rounded)
    for sub_q in range(lay.subs):
        lanes = slice(LANES * sub_q, LANES * (sub_q + 1))
        for sub_k in range(lay.subs + 2):
            piece = near[LANES * sub_k : LANES * (sub_k + 1), lanes]
            place = sub_k - sub_q
            if 0 <= place <= 2:
                bands[place] += piece
            else:
                sides[int(place > 2), :, lanes] += jnp.sum(fold(piece), axis=0)
    d_q[...] = total
    near_sum = total[half : half + 8, :]

    def far(index, count):
        places = [lay.keys_of(index + step) for step in range(count)]
        rounded = grads(places, [lay.rows_of(index + step) for step in range(count)])[1]
        keys = jnp.concatenate([k_t[:, where] for where in places], axis=1)
        lefts = jnp.clip(lay.lefts - index, 0, count) * TILE
        row = iota(keys.shape, 0)
        side = jnp.logical_and(row == half + 8, iota(keys.shape, 1) < lefts)
        keys = jnp.where(side, 1.0, keys.astype(F32)).astype(BF16)
        d_q[...] += dot_nn(keys, rounded)

    if lay.loops <= 3:
        for index in range(lay.loops):
            far(index * GROUP, GROUP)
    else:

        def group(index, carry):
            far(index * GROUP, GROUP)
            return carry

        lax.fori_loop(0, lay.loops, group, 0)

    @pl.when(lay.edge)
    def _():
        far(lay.loops * GROUP, 1)

    left_sum = d_q[half + 8 : half + 16, :]
    sides[0] += left_sum
    sides[1] += d_q[half : half + 8, :] - near_sum - left_sum
    d_kvs[0][pl.program_id(0), :half, :] = d_q[:half, :].astype(BF16)

    @pl.when(pl.program_id(0) == groups - 1)
    def finish():
        for slot in range(groups):
            for other in range(splits):
                start = lay.block_of(slot, other) * tokens
                rows = pl.ds(pl.multiple_of(LANES + start, LANES), tokens)
                turned = jnp.transpose(d_kv[rows, :]).astype(BF16)
                if other:
                    d_kvs[other][slot] = turned
                else:
                    d_kvs[0][slot, half:, :] = turned
        labels = [
            bucket_of(LANES * (place - 1) + iota((LANES, LANES), 0) - iota((LANES, LANES), 1))
            for place in range(3)
        ]
        for label in range(buckets):
            found = jnp.zeros((8, LANES), F32)
            for place in range(3):
                kept = jnp.where(labels[place] == label, bands[place], 0.0)
                found += jnp.sum(fold(kept), axis=0)
            if label in (buckets // 2 - 1, buckets - 1):
                side = sides[int(label == buckets - 1)]
                for sub in range(lay.subs):
                    found += side[:, LANES * sub : LANES * (sub + 1)]
            d_table[label : label + 1, :] = jnp.sum(found, axis=0, keepdims=True)


def chosen(shape, source):
    return (source(iota((shape[0], 1), 0)) == iota(shape, 1)).astype(F32).astype(BF16)


def project_kernel(dims, ints, weights, own, *refs):
    rows_apart, groups, splits = dims
    others, (normed_t, query, kv, gains, values, order) = refs[:-6], refs[-6:]
    slot, split, group, batch = pl.program_id(0), ints[0], ints[4], ints[5]
    width, narrow = own.shape[1], kv.shape[1]
    unit = width // (rows_apart * groups * splits)

    @pl.when(slot == 0)
    def _():
        def source(index):
            within = lax.rem(index, unit)
            index = index // unit
            g = lax.rem(group + lax.rem(index, groups), groups)
            index = index // groups
            b = lax.rem(batch + lax.rem(index, rows_apart), rows_apart)
            r = lax.rem(split + index // rows_apart, splits)
            return ((b * groups + g) * splits + r) * unit + within

        order[...] = chosen((width, width), source)
        turned = jnp.transpose(weights[:, narrow : narrow + LANES].astype(F32))
        gains[...] = turned[LANES // 2 : LANES // 2 + 8]

    @pl.when(slot == group)
    def _():
        values[...] = own[...]

    for by in range(1, groups):

        @pl.when(slot == group - by)
        def _():
            values[...] = others[by - 1][...]

        @pl.when(slot == group + by)
        def _():
            values[...] = others[groups + by - 2][...]

    normed = rms_scale(values[...].astype(F32), gains[0:1, :]).astype(BF16)
    normed_t[...] = dot_nt(order[...], normed).astype(BF16)
    both = dot_nn(normed, weights[...])
    kv[...] = both[:, :narrow].astype(BF16)
    lane = lax.rem(iota((own.shape[0], narrow), 1), LANES)
    query[...] = jnp.where(lane < LANES // 2, both[:, narrow:], 0.0).astype(BF16)


def project(dims, ints, weights, own, others):
    tokens, width = own.shape
    groups = dims[1]
    narrow = width // 2
    whole = pl.BlockSpec((tokens, width), lambda slot, ints: (0, 0))
    by_row = pl.BlockSpec((tokens, narrow), lambda slot, ints: (slot, 0))
    return pl.pallas_call(
        functools.partial(project_kernel, dims),
        grid_spec=pltpu.PrefetchScalarGridSpec(
            num_scalar_prefetch=1,
            grid=(groups,),
            in_specs=[pl.BlockSpec((width, width), lambda slot, ints: (0, ints[4]))]
            + [whole] * (1 + len(others)),
            out_specs=[
                pl.BlockSpec((width, tokens), lambda slot, ints: (0, slot)),
                by_row,
                by_row,
                pl.BlockSpec((8, width), lambda slot, ints: (0, 0)),
            ],
            scratch_shapes=[pltpu.VMEM((tokens, width), BF16), pltpu.VMEM((width, width), BF16)],
        ),
        out_shape=[
            jax.ShapeDtypeStruct((width, groups * tokens), BF16),
            jax.ShapeDtypeStruct((groups * tokens, narrow), BF16),
            jax.ShapeDtypeStruct((groups * tokens, narrow), BF16),
            jax.ShapeDtypeStruct((8, width), F32),
        ],
        compiler_params=pltpu.CompilerParams(vmem_limit_bytes=VMEM),
        cost_estimate=pl.CostEstimate(
            flops=4 * groups * tokens * width * width,
            bytes_accessed=8 * groups * tokens * width,
            transcendentals=0,
        ),
        name="project",
    )(ints, weights, own, *others)


def split_order(split, splits, unit):
    def source_of(count):
        part = count // splits

        def source(index):
            r = lax.rem(split + index // part, splits)
            index = lax.rem(index, part)
            return (index // unit * splits + r) * unit + lax.rem(index, unit)

        return source

    return source_of


def block_kernel(
    dims, heads, ints, tokens, w_out, gains, w_gate, w_up, w_down, upstream, *refs
):
    rows_apart, groups, splits = dims
    contexts, refs = refs[:heads], refs[heads:]
    result, d_mixed, d_first, d_rest = refs[:4]
    grads_wide, grads_down = refs[4 : 4 + splits], refs[4 + splits : 4 + 2 * splits]
    (context_t, mixed, normed, normed_t, d_normed, total, order, order_hidden) = refs[4 + 2 * splits :]
    step, chunks = pl.program_id(0), pl.num_programs(0) - 1
    width, chunk = w_gate.shape
    devices = rows_apart * groups * splits
    hidden_unit = chunk * chunks // devices
    gain = gains[1:2, :]

    @pl.when(step == 0)
    def first():
        order[...] = chosen(
            (width, width), split_order(ints[0], splits, width // devices)(width)
        )
        order_hidden[...] = chosen((chunk, chunk), split_order(ints[0], splits, hidden_unit)(chunk))
        each = width // groups // heads
        for g in range(groups):
            for head in range(heads):
                start = (g * heads + head) * each
                context_t[start : start + each, :] = contexts[head][g]
        context = jnp.transpose(context_t[...].astype(F32)).astype(BF16)
        values = tokens[...].astype(F32) + dot_nn(context, w_out[...])
        mixed[...] = values
        total[...] = values
        normed[...] = rms_scale(values, gain).astype(BF16)
        normed_t[...] = dot_nt(order[...], normed[...]).astype(BF16)
        d_normed[...] = jnp.zeros_like(d_normed)

    def stored(outs, rows, values):
        part = values.shape[0] // splits
        for other in range(splits):
            outs[other][:, rows] = values[part * other : part * (other + 1)].astype(BF16)

    @pl.when(step < chunks)
    def work():
        gate = dot_nn(normed[...], w_gate[...])
        upward = dot_nn(normed[...], w_up[...])
        d_hidden = dot_nt(upstream[...], w_down[...])
        square = gate * gate
        turn = jnp.tanh(GELU_SCALE * (gate + 0.044715 * gate * square))
        half = 0.5 * (1.0 + turn)
        active = gate * half
        slope = half + 0.5 * gate * (1.0 - turn * turn) * (GELU_SCALE * (1.0 + 0.134145 * square))
        hidden = (active * upward).astype(BF16)
        d_gate = (d_hidden * upward * slope).astype(BF16)
        d_up = (d_hidden * active).astype(BF16)
        total[...] += dot_nn(hidden, w_down[...])
        d_normed[...] += dot_nt(d_gate, w_gate[...]) + dot_nt(d_up, w_up[...])
        hidden_t = dot_nt(order_hidden[...], hidden).astype(BF16)

        stored(grads_down, slice(None), dot_nn(hidden_t, upstream[...]))
        stored(grads_wide, slice(0, chunk), dot_nn(normed_t[...], d_gate))
        stored(grads_wide, slice(chunk, 2 * chunk), dot_nn(normed_t[...], d_up))

    @pl.when(step == chunks)
    def finish():
        result[...] = total[...].astype(BF16)
        back = upstream[...].astype(F32) + rms_back(mixed[...], gain, d_normed[...])
        d_mixed[...] = back
        branch = back.astype(BF16)
        d_context = dot_nt(w_out[...], branch).astype(BF16)
        each = d_first.shape[1]
        size = width // groups
        for g in range(groups):
            d_first[g] = d_context[size * g : size * g + each]
            d_rest[g] = d_context[size * g + each : size * (g + 1)]
        ordered = dot_nn(order[...], context_t[...]).astype(BF16)
        stored(grads_wide, slice(0, width), dot_nn(ordered, branch))
        for out in grads_wide:
            out[:, width:] = jnp.zeros((out.shape[0], out.shape[1] - width), BF16)


def feed_forward(dims, ints, tokens, contexts, w_out, gains, late, w_down, upstream):
    groups, splits = dims[1:]
    rows, width = tokens.shape
    hidden = w_down.shape[0]
    chunk = 2 * TILE
    steps = hidden // chunk
    each = contexts[0].shape[1]
    full = lambda *shape: pl.BlockSpec(shape, lambda step: (0,) * len(shape))
    return pl.pallas_call(
        functools.partial(block_kernel, dims, len(contexts)),
        grid=(steps + 1,),
        in_specs=[
            smem(),
            full(rows, width),
            full(width, width),
            full(8, width),
            pl.BlockSpec((width, chunk), lambda step: (0, jnp.minimum(step, steps - 1))),
            pl.BlockSpec((width, chunk), lambda step: (0, steps + jnp.minimum(step, steps - 1))),
            pl.BlockSpec((chunk, width), lambda step: (jnp.minimum(step, steps - 1), 0)),
            full(rows, width),
        ]
        + [full(*context.shape) for context in contexts],
        out_specs=[
            full(rows, width),
            full(rows, width),
            full(groups, each, rows),
            full(groups, width // groups - each, rows),
        ]
        + [pl.BlockSpec((width // splits, 2 * chunk), lambda step: (0, step))] * splits
        + [pl.BlockSpec((chunk // splits, width), lambda step: (jnp.minimum(step, steps - 1), 0))]
        * splits,
        out_shape=[
            jax.ShapeDtypeStruct((rows, width), BF16),
            jax.ShapeDtypeStruct((rows, width), F32),
            jax.ShapeDtypeStruct((groups, each, rows), BF16),
            jax.ShapeDtypeStruct((groups, width // groups - each, rows), BF16),
        ]
        + [jax.ShapeDtypeStruct((width // splits, 2 * hidden + 2 * chunk), BF16)] * splits
        + [jax.ShapeDtypeStruct((hidden // splits, width), BF16)] * splits,
        scratch_shapes=[
            pltpu.VMEM((width, rows), BF16),
            pltpu.VMEM((rows, width), F32),
            pltpu.VMEM((rows, width), BF16),
            pltpu.VMEM((width, rows), BF16),
            pltpu.VMEM((rows, width), F32),
            pltpu.VMEM((rows, width), F32),
            pltpu.VMEM((width, width), BF16),
            pltpu.VMEM((chunk, chunk), BF16),
        ],
        compiler_params=pltpu.CompilerParams(vmem_limit_bytes=VMEM),
        cost_estimate=pl.CostEstimate(
            flops=18 * rows * width * hidden + 6 * rows * width * width,
            bytes_accessed=12 * width * hidden,
            transcendentals=rows * hidden,
        ),
        name="feed_forward",
    )(ints, tokens, w_out, gains, late, late, w_down, upstream, *contexts)


def weight_kernel(splits, normed_t, *refs):
    d_heads, outs, total = refs[: -splits - 1], refs[-splits - 1 : -1], refs[-1]
    step = pl.program_id(0)
    added = dot_nt(normed_t[...], jnp.concatenate([d_head[...] for d_head in d_heads], axis=0))

    @pl.when(step == 0)
    def _():
        total[...] = added

    @pl.when(step > 0)
    def _():
        total[...] += added

    @pl.when(step == pl.num_programs(0) - 1)
    def _():
        part = total.shape[0] // splits
        for other in range(splits):
            outs[other][...] = total[part * other : part * (other + 1), :].astype(BF16)


def weight_grads(splits, normed_t, d_heads):
    groups, rows, tokens = d_heads[0].shape
    width = normed_t.shape[0]
    out = (width // splits, rows * len(d_heads))
    return pl.pallas_call(
        functools.partial(weight_kernel, splits),
        grid=(groups,),
        in_specs=[pl.BlockSpec((width, tokens), lambda step: (0, step))]
        + [by_slot(rows, tokens)] * len(d_heads),
        out_specs=[pl.BlockSpec(out, lambda step: (0, 0))] * splits,
        out_shape=[jax.ShapeDtypeStruct(out, BF16)] * splits,
        scratch_shapes=[pltpu.VMEM((width, out[1]), F32)],
        compiler_params=pltpu.CompilerParams(vmem_limit_bytes=VMEM),
        name="weight_grads",
    )(normed_t, *d_heads)


def added_kernel(count, *refs):
    held, outs = refs[:count], refs[count:]
    total = held[0][...].astype(F32)
    for piece in held[1:]:
        total += piece[...].astype(F32)
    part = total.shape[0] // len(outs)
    for index, out in enumerate(outs):
        out[...] = total[part * index : part * (index + 1)].astype(out.dtype)


def added(pieces, parts):
    rows, columns = pieces[0].shape
    return pl.pallas_call(
        functools.partial(added_kernel, len(pieces)),
        out_shape=[jax.ShapeDtypeStruct((rows // parts, columns), BF16)] * parts,
        compiler_params=pltpu.CompilerParams(vmem_limit_bytes=VMEM),
        name="added",
    )(*pieces)


def total_of(pieces):
    rows, columns = pieces[0].shape
    block = pl.BlockSpec((rows // 4, columns), lambda step: (step, 0))
    return pl.pallas_call(
        functools.partial(added_kernel, len(pieces)),
        grid=(4,),
        in_specs=[block] * len(pieces),
        out_specs=[block],
        out_shape=[jax.ShapeDtypeStruct((rows, columns), BF16)],
        compiler_params=pltpu.CompilerParams(vmem_limit_bytes=VMEM),
        name="total_of",
    )(*pieces)[0]


def unpacked(pieces, heads, size):
    return jnp.concatenate(
        [
            piece[:, (3 * head + part) * size : (3 * head + part + 1) * size]
            for part in range(3)
            for piece in pieces
            for head in range(heads)
        ],
        axis=1,
    )


def count_kernel(groups, heads, size, count, ints, *refs):
    held, tables, (rest, down) = refs[:count], refs[count : count + heads], refs[count + heads :][:2]
    outs, counts = refs[count + heads + 2 : -1], refs[-1]
    total = held[0][...].astype(F32)
    for piece in held[1:]:
        total += piece[...].astype(F32)
    part = total.shape[0] // groups
    for index, out in enumerate(outs):
        out[...] = total[part * index : part * (index + 1)]
    squares = jnp.sum(total * total, axis=0, keepdims=True)
    table = jnp.concatenate(
        [jnp.sum(jnp.transpose(table[...]), axis=0, keepdims=True) for table in tables], axis=1
    )
    mine = [(ints[4] == g).astype(F32) for g in range(groups)]
    rest_values, down_values = rest[...].astype(F32), down[...].astype(F32)
    row = jnp.concatenate(
        [table * own for own in mine]
        + [unpacked([squares * own for own in mine], heads, size)]
        + [jnp.sum(rest_values * rest_values, axis=0, keepdims=True)]
        + [jnp.sum(down_values * down_values, axis=0, keepdims=True)],
        axis=1,
    )
    for index in range(counts.shape[0]):
        counts[index : index + 1, :] = row[:, LANES * index : LANES * (index + 1)]


def counted(groups, heads, size, ints, pieces, tables, rest, down):
    rows, columns = pieces[0].shape
    buckets = tables[0].shape[0]
    length = groups * (heads * buckets + columns) + rest.shape[1] + down.shape[1]
    vmem = pl.BlockSpec(memory_space=pltpu.VMEM)
    return pl.pallas_call(
        functools.partial(count_kernel, groups, heads, size, len(pieces)),
        in_specs=[smem()] + [vmem] * (len(pieces) + len(tables) + 2),
        out_shape=[jax.ShapeDtypeStruct((rows // groups, columns), F32)] * groups
        + [jax.ShapeDtypeStruct((length // LANES, LANES), F32)],
        compiler_params=pltpu.CompilerParams(vmem_limit_bytes=VMEM),
        name="counted",
    )(ints, *pieces, *tables, rest, down)


def input_kernel(heads, weights, own, gains, d_mixed, *refs):
    d_heads, (out, total) = refs[:heads], refs[heads:]
    step = pl.program_id(0)
    size = d_heads[0].shape[0] // 3
    blank = jnp.zeros((size, own.shape[0]), F32)
    pieces = [d_head[size:, :].astype(F32) for d_head in d_heads]
    for d_head in d_heads:
        pieces += [d_head[:size, :].astype(F32), blank]
    turned = jnp.transpose(jnp.concatenate(pieces, axis=0)).astype(BF16)
    added = dot_nt(turned, weights[...])

    @pl.when(step == 0)
    def _():
        total[...] = added

    @pl.when(step > 0)
    def _():
        total[...] += added

    @pl.when(step == pl.num_programs(0) - 1)
    def _():
        back = rms_back(own[...].astype(F32), gains[0:1, :], total[...])
        out[...] = (d_mixed[...] + back).astype(BF16)


def input_grads(groups, weights, own, gains, d_mixed, d_heads):
    tokens, width = own.shape
    full = lambda *shape: pl.BlockSpec(shape, lambda step: (0,) * len(shape))
    return pl.pallas_call(
        functools.partial(input_kernel, len(d_heads)),
        grid=(groups,),
        in_specs=[
            pl.BlockSpec((width, width), lambda step: (0, step)),
            full(tokens, width),
            full(8, width),
            full(tokens, width),
        ]
        + [by_slot(*d_heads[0].shape[1:])] * len(d_heads),
        out_specs=full(tokens, width),
        out_shape=jax.ShapeDtypeStruct((tokens, width), BF16),
        scratch_shapes=[pltpu.VMEM((tokens, width), F32)],
        compiler_params=pltpu.CompilerParams(vmem_limit_bytes=VMEM),
        name="input_grads",
    )(weights, own, gains, d_mixed, *d_heads)


def by_slot(rows, tokens):
    return pl.BlockSpec((None, rows, tokens), lambda slot: (slot, 0, 0))


def smem():
    return pl.BlockSpec(memory_space=pltpu.SMEM)


def attend(head, tokens, groups, splits, ints, table, query, kvs):
    seq, rows = tokens * groups * splits, tokens * groups
    half = LANES // 2
    whole = pl.BlockSpec((rows, LANES), lambda slot: (0, head))
    return pl.pallas_call(
        functools.partial(forward_kernel, tokens, groups, splits),
        grid=(groups,),
        in_specs=[smem(), smem(), pl.BlockSpec((tokens, LANES), lambda slot: (slot, head))]
        + [whole] * splits,
        out_specs=[
            pl.BlockSpec((seq, tokens), lambda slot: (slot, 0)),
            by_slot(half, tokens),
            by_slot(half + 16, tokens),
        ],
        out_shape=[
            jax.ShapeDtypeStruct((groups * seq, tokens), BF16),
            jax.ShapeDtypeStruct((groups, half, tokens), BF16),
            jax.ShapeDtypeStruct((groups, half + 16, tokens), F32),
        ],
        scratch_shapes=[
            pltpu.VMEM((seq + 2 * LANES, LANES), BF16),
            pltpu.VMEM((half + 16, seq + 2 * LANES), BF16),
            pltpu.VMEM((tokens + 2 * LANES, tokens), F32),
            pltpu.VMEM((3, LANES, LANES), F32),
            pltpu.VMEM((8, tokens), F32),
        ],
        compiler_params=pltpu.CompilerParams(vmem_limit_bytes=VMEM),
        cost_estimate=pl.CostEstimate(
            flops=16 * seq * rows * half, bytes_accessed=2 * seq * rows, transcendentals=seq * rows
        ),
        name="attend",
    )(ints, table, query, *kvs)


def attend_back(
    head, tokens, groups, splits, ints, buckets, query, d_context, place, stats, probs, kvs
):
    seq, rows = tokens * groups * splits, tokens * groups
    half = LANES // 2
    whole = pl.BlockSpec((rows, LANES), lambda slot: (0, head))
    kept = pl.BlockSpec((groups, LANES, tokens), lambda slot: (0, 0, 0))
    return pl.pallas_call(
        functools.partial(backward_kernel, tokens, groups, splits),
        grid=(groups,),
        in_specs=[
            smem(),
            pl.BlockSpec((tokens, LANES), lambda slot: (slot, head)),
            pl.BlockSpec((None, None, half, tokens), lambda slot: (slot, place, 0, 0)),
            by_slot(half + 16, tokens),
            pl.BlockSpec((seq, tokens), lambda slot: (slot, 0)),
        ]
        + [whole] * splits,
        out_specs=[pl.BlockSpec((groups, half + LANES, tokens), lambda slot: (0, 0, 0))]
        + [kept] * (splits - 1)
        + [pl.BlockSpec((buckets, LANES), lambda slot: (0, 0))],
        out_shape=[jax.ShapeDtypeStruct((groups, half + LANES, tokens), BF16)]
        + [jax.ShapeDtypeStruct((groups, LANES, tokens), BF16)] * (splits - 1)
        + [jax.ShapeDtypeStruct((buckets, LANES), F32)],
        scratch_shapes=[
            pltpu.VMEM((seq + 2 * LANES, LANES), BF16),
            pltpu.VMEM((half + 16, seq + 2 * LANES), BF16),
            pltpu.VMEM((seq + 2 * LANES, LANES), F32),
            pltpu.VMEM((3, LANES, LANES), F32),
            pltpu.VMEM((2, 8, tokens), F32),
            pltpu.VMEM((half + 16, tokens), F32),
        ],
        compiler_params=pltpu.CompilerParams(vmem_limit_bytes=VMEM),
        cost_estimate=pl.CostEstimate(
            flops=32 * seq * rows * half, bytes_accessed=2 * seq * rows, transcendentals=0
        ),
        name="attend_back",
    )(ints, query, d_context, stats, probs, *kvs)


def factored(grad_shard, column_total, row_old, column_old, row_total):
    columns = grad_shard.shape[1]
    mean_square = jnp.sum(column_total) / (row_total * columns) + EPSILON
    row_new = (
        DECAY_RATE * row_old
        + (1.0 - DECAY_RATE) * (jnp.sum(grad_shard * grad_shard, axis=1) / columns) / mean_square
    )
    column_new = (
        DECAY_RATE * column_old + (1.0 - DECAY_RATE) * (column_total / row_total) / mean_square
    )
    return (row_new, column_new)


def shards(
    tokens,
    lengths,
    norm_one,
    w_qkv,
    rel_table,
    w_out,
    norm_two,
    w_gateup,
    w_down,
    cotangent,
    row_qkv,
    col_qkv,
    row_out,
    col_out,
    row_gateup,
    col_gateup,
    row_down,
    col_down,
):
    own = tokens[0]
    tok_rows, width = own.shape
    heads = rel_table.shape[1]
    buckets = rel_table.shape[0]
    rows_apart, groups, splits = (lax.axis_size(name) for name in ALL)
    group_heads = heads // groups
    head_size = width // heads
    group, split = lax.axis_index("group"), lax.axis_index("split")
    group_width = width // groups

    def ahead(array, axis, by):
        size = lax.axis_size(axis)
        return lax.ppermute(array, axis, [((i + by) % size, i) for i in range(size)])

    def swap_groups(array):
        return lax.all_to_all(array, "group", 0, 0)

    def swap_rows(array):
        return lax.all_to_all(array, "batch", 0, 0)

    def all_sum(array, other):
        for axis in ALL:
            array = sum([ahead(array, axis, by) for by in range(1, lax.axis_size(axis))], array)
            if axis == "batch":
                array = after(array, other)
        return array

    def line(array, by):
        pairs = [(i, i + by) for i in range(groups) if 0 <= i + by < groups]
        return lax.ppermute(array, "group", pairs)

    before, behind = [own], [own]
    for _ in range(groups - 1):
        before.append(line(before[-1], 1))
        behind.append(line(behind[-1], -1))

    unit = w_qkv.shape[0]
    by_part = w_qkv.reshape(unit, 3, groups, group_heads, head_size)
    gains = jnp.pad(jnp.stack([norm_one, norm_two], axis=1), ((0, 0), (0, head_size - 2)))
    beside = jnp.pad(gains[:, None, None], ((0, 0), (0, 0), (0, group_heads - 1), (0, 0)))
    beside = jnp.broadcast_to(beside, (unit, groups, group_heads, head_size))
    packed = jnp.concatenate(
        [
            jnp.concatenate([by_part[:, 1], by_part[:, 2]], axis=-1),
            jnp.concatenate([by_part[:, 0], beside], axis=-1),
        ],
        axis=2,
    )
    early = lax.all_gather(packed.reshape(unit, -1), ALL, axis=0, tiled=True)
    late = lax.all_gather(
        after(
            jnp.concatenate([w_gateup, w_out, w_down.reshape(unit, -1)], axis=1),
            before[1],
            behind[1],
        ),
        ALL,
        axis=0,
        tiled=True,
    )
    full_down = late[:, w_gateup.shape[1] + width :].reshape(-1, width)
    full_out = late[:, w_gateup.shape[1] :][:, :width]

    dims = (rows_apart, groups, splits)
    ends = jnp.cumsum(lengths[0])
    ints = jnp.concatenate(
        [
            split.astype(jnp.int32)[None],
            ends.astype(jnp.int32),
            jnp.stack([group, lax.axis_index("batch")]).astype(jnp.int32),
        ]
    )
    normed_t, query, kv, gains = project(dims, ints, early, own, before[1:] + behind[1:])
    kvs = [kv] + [ahead(kv, "split", other) for other in range(1, splits)]

    table_own = lax.dynamic_slice_in_dim(rel_table.T, group * group_heads, group_heads, 0)

    contexts, moved, stats, probs = [], [], [], []
    for head in range(group_heads):
        prob, context, stat = attend(
            head,
            tok_rows,
            groups,
            splits,
            after(ints, *contexts[-1:]),
            table_own[head : head + 1],
            query,
            kvs,
        )
        contexts.append(context)
        moved.append(swap_groups(after(context, *moved[-1:])))
        stats.append(stat)
        probs.append(prob)

    outs = feed_forward(
        dims, ints, own, moved, full_out, gains, late, full_down, cotangent[0]
    )
    result, d_mixed, d_first, d_rest = outs[:4]
    grads_wide, grads_down = outs[4 : 4 + splits], outs[4 + splits :]

    def split_sum(grads, *waits):
        pieces = [grads[0]]
        for by in range(1, splits):
            pieces.append(after(ahead(grads[by], "split", splits - by), *waits))
        held = total_of(pieces)
        return held.reshape(rows_apart, groups, -1, held.shape[-1])

    held_down = split_sum(grads_down)
    d_first = swap_groups(after(d_first, held_down))
    d_rest = swap_groups(d_rest)
    d_contexts = [d_first[:, None], d_rest.reshape(groups, group_heads - 1, head_size, tok_rows)]
    grads_wide = [grads_wide[0]] + [after(grad, held_down) for grad in grads_wide[1:]]
    held_rest = split_sum(grads_wide, d_first)
    rest = after(lax.psum_scatter(held_rest, "batch", scatter_dimension=0))
    down = after(lax.psum_scatter(held_down, "batch", scatter_dimension=0))
    rest_own = lax.psum_scatter(rest, "group", scatter_dimension=0)
    down_own = lax.psum_scatter(down, "group", scatter_dimension=0)

    d_heads, d_received, d_tables = [], [], []
    ready = [(held_rest,), (held_down,)] + [(rest, down)] * (group_heads - 2)
    for head in range(group_heads):
        outs = attend_back(
            head,
            tok_rows,
            groups,
            splits,
            ints,
            buckets,
            query,
            after(d_contexts[int(head > 0)], *ready[head], *d_heads[-1:]),
            head - int(head > 0),
            stats[head],
            probs[head],
            kvs,
        )
        beside = d_received[-1] if head else d_contexts[1]
        outs = lax.optimization_barrier((*outs, beside))[:-1]
        d_head = outs[0].astype(F32)
        for other in range(1, splits):
            d_kv = ahead(outs[other], "split", splits - other).astype(F32)
            d_head = d_head + jnp.pad(d_kv, ((0, 0), (head_size, 0), (0, 0)))
        d_head = d_head.astype(BF16)
        d_heads.append(d_head)
        d_received.append(swap_groups(d_head))
        d_tables.append(outs[-1])

    grads = weight_grads(splits, normed_t, d_heads)
    held = added(
        [grads[0]] + [ahead(grads[by], "split", splits - by) for by in range(1, splits)], rows_apart
    )
    held = [held[0]] + [ahead(held[by], "batch", rows_apart - by) for by in range(1, rows_apart)]
    held[0] = after(held[0], d_received[-1])
    *columns, counts = counted(
        groups, group_heads, head_size, ints, held, d_tables, rest_own, down_own
    )
    d_received[-1] = after(d_received[-1], counts)
    d_inputs = input_grads(groups, early, own, gains, d_mixed, d_received)
    columns = [columns[0]] + [ahead(columns[by], "group", groups - by) for by in range(1, groups)]
    pieces = []
    for index in range(groups):
        piece = columns[0]
        for by in range(1, groups):
            piece = jnp.where((group + groups - by) % groups == index, columns[by], piece)
        pieces.append(piece)
    shard_qkv = unpacked(pieces, group_heads, head_size)
    steps = w_down.shape[0] * rows_apart * groups * splits // (2 * TILE)

    def in_order(array):
        array = array.reshape(*array.shape[:-1], steps, 2, -1)
        return jnp.swapaxes(array, -3, -2).reshape(*array.shape[:-3], -1)

    shard_rest = rest_own.astype(F32)
    shard_gateup = in_order(shard_rest[:, : w_gateup.shape[1]])
    shard_out = shard_rest[:, w_gateup.shape[1] :][:, :width]
    shard_down = down_own.astype(F32)
    summed = all_sum(counts, d_inputs).reshape(-1)
    extra = rest_own.shape[1] - w_gateup.shape[1] - width
    sizes = (heads * buckets, 3 * width, w_gateup.shape[1], width, extra, width)
    table_total, column_qkv, column_gateup, column_out, _, column_down = jnp.split(
        summed, [sum(sizes[: i + 1]) for i in range(len(sizes) - 1)]
    )
    table_total = table_total.reshape(heads, buckets)
    column_gateup = in_order(column_gateup)
    shard_gain_one = jnp.sum(w_qkv.astype(F32) * shard_qkv, axis=1) / norm_one.astype(F32)
    shard_gain_two = jnp.sum(w_gateup.astype(F32) * shard_gateup, axis=1) / norm_two.astype(F32)
    new_row_qkv, new_col_qkv = factored(shard_qkv, column_qkv, row_qkv, col_qkv, width)
    new_row_out, new_col_out = factored(shard_out, column_out, row_out, col_out, width)
    new_row_gateup, new_col_gateup = factored(
        shard_gateup, column_gateup, row_gateup, col_gateup, width
    )
    new_row_down, new_col_down = factored(
        shard_down, column_down, row_down, col_down, full_down.shape[0]
    )
    return (
        result[None],
        d_inputs[None],
        shard_gain_one,
        shard_qkv,
        table_total.T,
        shard_out,
        shard_gain_two,
        shard_gateup,
        shard_down,
        new_row_qkv,
        new_col_qkv,
        new_row_out,
        new_col_out,
        new_row_gateup,
        new_col_gateup,
        new_row_down,
        new_col_down,
    )


def solution(mesh):
    row_blocks = P("batch", ("group", "split"), None)
    split_rows = P(ALL, None)
    split_row = P(ALL)

    def run(*arrays):
        rows, ring = mesh.devices.shape
        groups = math.gcd(ring, arrays[4].shape[1])
        fine = Mesh(mesh.devices.reshape(rows, groups, ring // groups), ALL)
        return jax.shard_map(
            shards,
            mesh=fine,
            in_specs=(
                row_blocks,
                P("batch", None),
                split_row,
                split_rows,
                P(),
                split_rows,
                split_row,
                split_rows,
                split_rows,
                row_blocks,
            )
            + (split_row, P()) * 4,
            out_specs=(
                row_blocks,
                row_blocks,
                split_row,
                split_rows,
                P(),
                split_rows,
                split_row,
                split_rows,
                split_rows,
            )
            + (split_row, P()) * 4,
            check_vma=False,
        )(*arrays)

    return run
```

```python
import functools
import math

import jax
import jax.numpy as jnp
from jax import lax
from jax.experimental import pallas as pl
from jax.experimental.pallas import tpu as pltpu
from jax.sharding import Mesh
from jax.sharding import PartitionSpec as P

THRESHOLDS = (12, 16, 23, 32, 46, 64, 91)
EPSILON = 1e-06
DECAY_RATE = 0.5
GELU_SCALE = 0.7978845608028654
MASKED = -1e9
LEEWAY = 20.0
ALL = ("batch", "group", "split")
LANES = 128
TILE = 256
GROUP = 4
VMEM = 56 * 2**20
F32 = jnp.float32
BF16 = jnp.bfloat16


def bucket_of(offset):
    distance = jnp.abs(offset)
    steps_up = 8 + sum(((distance >= limit).astype(jnp.int32) for limit in THRESHOLDS))
    within = jnp.where(distance < 8, distance, steps_up)
    return within + 16 * (offset > 0).astype(jnp.int32)


def after(value, *others):
    return lax.optimization_barrier((value, *others))[0]


def rms_scale(values, gain):
    return values * lax.rsqrt(jnp.mean(values * values, axis=-1, keepdims=True) + EPSILON) * gain


def rms_back(values, gain, grad):
    scale = lax.rsqrt(jnp.mean(values * values, axis=-1, keepdims=True) + EPSILON)
    scaled = grad * gain
    return scale * scaled - values * scale**3 * jnp.mean(scaled * values, axis=-1, keepdims=True)


def dot_nn(left, right):
    return jnp.dot(left, right, preferred_element_type=F32)


def dot_nt(left, right):
    return lax.dot_general(left, right, (((1,), (1,)), ((), ())), preferred_element_type=F32)


def dot_tt(left, right):
    return lax.dot_general(left, right, (((0,), (1,)), ((), ())), preferred_element_type=F32)


class Layout:
    def __init__(self, tokens, groups, splits, ints):
        self.tokens, self.groups, self.splits = tokens, groups, splits
        self.blocks = groups * splits
        self.seq = tokens * self.blocks
        self.near = tokens + 2 * LANES
        self.subs = tokens // LANES
        self.split = ints[0]
        self.ends = (ints[1], ints[2], ints[3])
        slot = pl.program_id(0)
        self.block = self.block_of(slot, 0)
        self.first = pl.multiple_of(self.block * tokens, LANES)
        self.lefts = jnp.maximum(0, self.block * (tokens // TILE) - 1)
        self.loops = (self.seq // TILE - 2 - tokens // TILE) // GROUP
        self.edge = jnp.logical_or(self.block == 0, self.block == self.blocks - 1)

    def block_of(self, slot, other):
        return slot * self.splits + lax.rem(self.split + other, self.splits)

    def keys_of(self, tile):
        before = 2 * LANES + TILE * tile
        after = self.first + self.near + TILE * (tile - self.lefts)
        return pl.ds(pl.multiple_of(jnp.where(tile < self.lefts, before, after), LANES), TILE)

    def rows_of(self, tile):
        return pl.ds(pl.multiple_of(self.near + TILE * tile, LANES), TILE)

    def segment(self, positions):
        return sum((positions >= end).astype(jnp.int32) for end in self.ends)


def iota(shape, dim):
    return lax.broadcasted_iota(jnp.int32, shape, dim)


def fold(values):
    return values.reshape(values.shape[0] // 8, 8, values.shape[1])


def forward_kernel(tokens, groups, splits, ints, table, query, *refs):
    kvs, (probs, context, stats, k_aug, v_t, scores, biases, best) = refs[:splits], refs[splits:]
    lay = Layout(tokens, groups, splits, ints)
    half = query.shape[1] // 2
    buckets = table.shape[1]

    @pl.when(pl.program_id(0) == 0)
    def prepare():
        lane = iota((tokens, LANES), 1)
        for slot in range(groups):
            for other in range(splits):
                start = lay.block_of(slot, other) * tokens
                rows = pl.ds(pl.multiple_of(LANES + start, LANES), tokens)
                kv = kvs[other][slot * tokens : (slot + 1) * tokens, :].astype(F32)
                seg = lay.segment(start + iota((tokens, LANES), 0))
                k_aug[rows, :] = jnp.where(lane < half, kv, (lane - half == seg).astype(F32)).astype(BF16)
                turned = jnp.transpose(kv)
                ones = (iota((16, tokens), 0) == 0).astype(F32)
                v_t[:, rows] = jnp.concatenate([turned[half:], ones], axis=0).astype(BF16)
        outside = (iota((LANES, LANES), 1) == half + 3).astype(BF16)
        for start in (0, lay.seq + LANES):
            k_aug[start : start + LANES, :] = outside
            v_t[:, start : start + LANES] = jnp.zeros((half + 16, LANES), BF16)
        for place in range(3):
            bucket = bucket_of(
                LANES * (place - 1) + iota((LANES, LANES), 0) - iota((LANES, LANES), 1)
            )
            bias = jnp.zeros((LANES, LANES), F32)
            for label in range(buckets):
                bias = jnp.where(bucket == label, table[0, label], bias)
            biases[place] = bias

    far_left, far_right = table[0, buckets // 2 - 1], table[0, buckets - 1]
    positions = lay.block * tokens + iota((1, tokens), 1)
    seg_q = lay.segment(positions)
    row = iota((2 * half, tokens), 0)
    apart = jnp.logical_or(row - half != seg_q, row == half + 3)
    q_aug = jnp.where(
        row < half, jnp.transpose(query[...].astype(F32)), jnp.where(apart, MASKED, 0.0)
    ).astype(BF16)

    near = dot_nn(k_aug[pl.ds(lay.first, lay.near), :], q_aug)
    eye = iota((LANES, LANES), 0) == iota((LANES, LANES), 1)
    for sub_q in range(lay.subs):
        lanes = slice(LANES * sub_q, LANES * (sub_q + 1))
        top = None
        for sub_k in range(lay.subs + 2):
            rows = slice(LANES * sub_k, LANES * (sub_k + 1))
            place = sub_k - sub_q
            piece = near[rows, lanes] + (
                far_left if place < 0 else far_right if place > 2 else biases[place]
            )
            if place == 1:
                alone = jnp.logical_and(eye, positions[:, lanes] >= lay.ends[2])
                piece = jnp.where(alone, 0.0, piece)
            scores[rows, lanes] = piece
            high = jnp.max(fold(piece), axis=0)
            top = high if top is None else jnp.maximum(top, high)
        best[:, lanes] = top

    def sweep(peak):
        weights = jnp.exp(scores[...] - peak).astype(BF16)
        probs[: lay.near, :] = weights
        stats[...] = dot_nn(v_t[:, pl.ds(lay.first, lay.near)], weights)
        left_peak, right_peak = peak - far_left, peak - far_right

        def tiles(index, count):
            places = [lay.keys_of(index + step) for step in range(count)]
            piece = dot_nn(jnp.concatenate([k_aug[keys, :] for keys in places], axis=0), q_aug)
            parts, top = [], best[...]
            for step in range(count):
                score = piece[TILE * step : TILE * (step + 1)]
                is_left = index + step < lay.lefts
                top = jnp.maximum(
                    top,
                    jnp.max(fold(score), axis=0) + jnp.where(is_left, far_left, far_right),
                )
                part = jnp.exp(score - jnp.where(is_left, left_peak, right_peak)).astype(BF16)
                probs[lay.rows_of(index + step), :] = part
                parts.append(part)
            best[...] = top
            values = jnp.concatenate([v_t[:, keys] for keys in places], axis=1)
            stats[...] += dot_nn(values, jnp.concatenate(parts, axis=0))

        if lay.loops <= 3:
            for index in range(lay.loops):
                tiles(index * GROUP, GROUP)
        else:

            def group(index, carry):
                tiles(index * GROUP, GROUP)
                return carry

            lax.fori_loop(0, lay.loops, group, 0)

        @pl.when(lay.edge)
        def _():
            tiles(lay.loops * GROUP, 1)

    peak = jnp.max(best[...], axis=0, keepdims=True)
    sweep(peak)
    true_peak = jnp.max(best[...], axis=0, keepdims=True)

    @pl.when(jnp.max(true_peak - peak) > LEEWAY)
    def _():
        sweep(true_peak)

    inverse = 1.0 / stats[half : half + 1, :]
    result = stats[:half, :] * inverse
    context[...] = result.astype(BF16)
    stats[:half, :] = result
    stats[half : half + 1, :] = inverse


def backward_kernel(tokens, groups, splits, ints, query, d_context, stats, probs, *refs):
    kvs, d_kvs = refs[:splits], refs[splits : 2 * splits]
    d_table, v_aug, k_t, d_kv, bands, sides, d_q = refs[2 * splits :]
    lay = Layout(tokens, groups, splits, ints)
    half = query.shape[1] // 2
    buckets = d_table.shape[0]

    @pl.when(pl.program_id(0) == 0)
    def prepare():
        lane = iota((tokens, LANES), 1)
        for slot in range(groups):
            for other in range(splits):
                start = lay.block_of(slot, other) * tokens
                rows = pl.ds(pl.multiple_of(LANES + start, LANES), tokens)
                kv = kvs[other][slot * tokens : (slot + 1) * tokens, :].astype(F32)
                v_aug[rows, :] = jnp.where(lane >= half, kv, (lane < 3).astype(F32)).astype(BF16)
                ones = (iota((16, tokens), 0) == 0).astype(F32)
                k_t[:, rows] = jnp.concatenate([jnp.transpose(kv)[:half], ones], axis=0).astype(BF16)
        for start in (0, lay.seq + LANES):
            v_aug[start : start + LANES, :] = jnp.zeros((LANES, LANES), BF16)
            k_t[:, start : start + LANES] = jnp.zeros((half + 16, LANES), BF16)
        d_kv[...] = jnp.zeros_like(d_kv)
        bands[...] = jnp.zeros_like(bands)
        sides[...] = jnp.zeros_like(sides)

    inverse = stats[half : half + 1, :]
    upstream = d_context[...].astype(F32)
    delta = jnp.sum(upstream * stats[:half, :], axis=0, keepdims=True) * inverse
    scaled = upstream * inverse
    high = delta.astype(BF16).astype(F32)
    middle = (delta - high).astype(BF16).astype(F32)
    low = delta - high - middle
    row = iota((half, tokens), 0)
    shift = jnp.where(row == 0, high, jnp.where(row == 1, middle, jnp.where(row == 2, low, 0.0)))
    up_aug = jnp.concatenate([-shift, scaled], axis=0).astype(BF16)
    up_rows = jnp.transpose(jnp.concatenate([jnp.zeros_like(scaled), scaled], axis=0)).astype(BF16)
    both = jnp.concatenate([query[...], up_rows], axis=0)

    def grads(keys, rows):
        part = jnp.concatenate([probs[where, :] for where in rows], axis=0)
        values = jnp.concatenate([v_aug[where, :] for where in keys], axis=0)
        d_scores = part.astype(F32) * dot_nn(values, up_aug)
        rounded = d_scores.astype(BF16)
        added = dot_nn(jnp.concatenate([rounded, part], axis=1), both)
        size = part.shape[0] // len(keys)
        for index, where in enumerate(keys):
            d_kv[where, :] += added[size * index : size * (index + 1)]
        return d_scores, rounded

    near, rounded = grads([pl.ds(lay.first, lay.near)], [pl.ds(0, lay.near)])
    total = dot_nn(k_t[:, pl.ds(lay.first, lay.near)], rounded)
    for sub_q in range(lay.subs):
        lanes = slice(LANES * sub_q, LANES * (sub_q + 1))
        for sub_k in range(lay.subs + 2):
            piece = near[LANES * sub_k : LANES * (sub_k + 1), lanes]
            place = sub_k - sub_q
            if 0 <= place <= 2:
                bands[place] += piece
            else:
                sides[int(place > 2), :, lanes] += jnp.sum(fold(piece), axis=0)
    d_q[...] = total
    near_sum = total[half : half + 8, :]

    def far(index, count):
        places = [lay.keys_of(index + step) for step in range(count)]
        rounded = grads(places, [lay.rows_of(index + step) for step in range(count)])[1]
        keys = jnp.concatenate([k_t[:, where] for where in places], axis=1)
        lefts = jnp.clip(lay.lefts - index, 0, count) * TILE
        row = iota(keys.shape, 0)
        side = jnp.logical_and(row == half + 8, iota(keys.shape, 1) < lefts)
        keys = jnp.where(side, 1.0, keys.astype(F32)).astype(BF16)
        d_q[...] += dot_nn(keys, rounded)

    if lay.loops <= 3:
        for index in range(lay.loops):
            far(index * GROUP, GROUP)
    else:

        def group(index, carry):
            far(index * GROUP, GROUP)
            return carry

        lax.fori_loop(0, lay.loops, group, 0)

    @pl.when(lay.edge)
    def _():
        far(lay.loops * GROUP, 1)

    left_sum = d_q[half + 8 : half + 16, :]
    sides[0] += left_sum
    sides[1] += d_q[half : half + 8, :] - near_sum - left_sum
    d_kvs[0][pl.program_id(0), :half, :] = d_q[:half, :].astype(BF16)

    @pl.when(pl.program_id(0) == groups - 1)
    def finish():
        for slot in range(groups):
            for other in range(splits):
                start = lay.block_of(slot, other) * tokens
                rows = pl.ds(pl.multiple_of(LANES + start, LANES), tokens)
                turned = jnp.transpose(d_kv[rows, :]).astype(BF16)
                if other:
                    d_kvs[other][slot] = turned
                else:
                    d_kvs[0][slot, half:, :] = turned
        labels = [
            bucket_of(LANES * (place - 1) + iota((LANES, LANES), 0) - iota((LANES, LANES), 1))
            for place in range(3)
        ]
        for label in range(buckets):
            found = jnp.zeros((8, LANES), F32)
            for place in range(3):
                kept = jnp.where(labels[place] == label, bands[place], 0.0)
                found += jnp.sum(fold(kept), axis=0)
            if label in (buckets // 2 - 1, buckets - 1):
                side = sides[int(label == buckets - 1)]
                for sub in range(lay.subs):
                    found += side[:, LANES * sub : LANES * (sub + 1)]
            d_table[label : label + 1, :] = jnp.sum(found, axis=0, keepdims=True)


def chosen(shape, source):
    return (source(iota((shape[0], 1), 0)) == iota(shape, 1)).astype(F32).astype(BF16)


def project_block(values, weights, gains, order, normed_t, query, kv):
    normed = rms_scale(values.astype(F32), gains[0:1, :]).astype(BF16)
    normed_t[...] = dot_nt(order[...], normed).astype(BF16)
    both = dot_nn(normed, weights[...])
    narrow = kv.shape[1]
    kv[...] = both[:, :narrow].astype(BF16)
    size = LANES // 2
    blank = jnp.zeros((both.shape[0], size), F32)
    parts = []
    for start in range(narrow, narrow + narrow // 2, size):
        parts += [both[:, start : start + size], blank]
    query[...] = jnp.concatenate(parts, axis=1).astype(BF16)


def project_kernel(dims, ints, weights, own, *refs):
    rows_apart, groups, splits = dims
    others, (normed_t, query, kv, gains, order, values) = refs[:-6], refs[-6:]
    slot, split, group, batch = pl.program_id(0), ints[0], ints[4], ints[5]
    width, narrow = own.shape[1], kv.shape[1]
    unit = width // (rows_apart * groups * splits)

    @pl.when(slot == 0)
    def _():
        def source(index):
            within = lax.rem(index, unit)
            index = index // unit
            g = lax.rem(group + lax.rem(index, groups), groups)
            index = index // groups
            b = lax.rem(batch + lax.rem(index, rows_apart), rows_apart)
            r = lax.rem(split + index // rows_apart, splits)
            return ((b * groups + g) * splits + r) * unit + within

        order[...] = chosen((width, width), source)
        turned = jnp.transpose(weights[:, weights.shape[1] - LANES :].astype(F32))
        gains[...] = turned[LANES // 2 : LANES // 2 + 8]

    @pl.when(slot == group)
    def _():
        values[...] = own[...]

    for by in range(1, groups - 1):

        @pl.when(slot == group - by)
        def _():
            values[...] = others[by - 1][...]

        @pl.when(slot == group + by)
        def _():
            values[...] = others[groups + by - 3][...]

    @pl.when(jnp.abs(slot - group) < groups - 1)
    def _():
        project_block(values[...], weights, gains, order, normed_t, query, kv)


def project(dims, ints, weights, own, others):
    tokens, width = own.shape
    groups = dims[1]
    narrow = 2 * width // groups
    whole = pl.BlockSpec((tokens, width), lambda slot, ints: (0, 0))
    by_row = pl.BlockSpec((tokens, narrow), lambda slot, ints: (slot, 0))
    return pl.pallas_call(
        functools.partial(project_kernel, dims),
        grid_spec=pltpu.PrefetchScalarGridSpec(
            num_scalar_prefetch=1,
            grid=(groups,),
            in_specs=[pl.BlockSpec((width, weights.shape[1] // groups), lambda slot, ints: (0, ints[4]))]
            + [whole] * (1 + len(others)),
            out_specs=[
                pl.BlockSpec((width, tokens), lambda slot, ints: (0, slot)),
                by_row,
                by_row,
                pl.BlockSpec((8, width), lambda slot, ints: (0, 0)),
                pl.BlockSpec((width, width), lambda slot, ints: (0, 0)),
            ],
            scratch_shapes=[pltpu.VMEM((tokens, width), BF16)],
        ),
        out_shape=[
            jax.ShapeDtypeStruct((width, groups * tokens), BF16),
            jax.ShapeDtypeStruct((groups * tokens, narrow), BF16),
            jax.ShapeDtypeStruct((groups * tokens, narrow), BF16),
            jax.ShapeDtypeStruct((8, width), F32),
            jax.ShapeDtypeStruct((width, width), BF16),
        ],
        compiler_params=pltpu.CompilerParams(vmem_limit_bytes=VMEM),
        cost_estimate=pl.CostEstimate(
            flops=4 * groups * tokens * width * width,
            bytes_accessed=8 * groups * tokens * width,
            transcendentals=0,
        ),
        name="project",
    )(ints, weights, own, *others)


def project_last_kernel(groups, ints, weights, own, before, behind, order, gains, *refs):
    normed_t, query, kv, values = refs[3:]
    group = ints[4]
    values[...] = own[...]

    @pl.when(group == 0)
    def _():
        values[...] = behind[...]

    @pl.when(group == groups - 1)
    def _():
        values[...] = before[...]

    project_block(values[...], weights, gains, order, normed_t, query, kv)


def project_last(dims, ints, weights, own, before, behind, order, gains, normed_t, query, kv):
    tokens, width = own.shape
    narrow = kv.shape[1]
    whole = lambda array: pl.BlockSpec(array.shape, lambda step, ints: (0, 0))
    by_row = pl.BlockSpec((tokens, narrow), lambda step, ints: (ints[6], 0))
    return pl.pallas_call(
        functools.partial(project_last_kernel, dims[1]),
        grid_spec=pltpu.PrefetchScalarGridSpec(
            num_scalar_prefetch=1,
            grid=(1,),
            in_specs=[
                pl.BlockSpec((width, weights.shape[1] // dims[1]), lambda step, ints: (0, ints[4]))
            ]
            + [whole(array) for array in (own, before, behind, order, gains)]
            + [pl.BlockSpec(memory_space=pl.ANY)] * 3,
            out_specs=[
                pl.BlockSpec((width, tokens), lambda step, ints: (0, ints[6])),
                by_row,
                by_row,
            ],
            scratch_shapes=[pltpu.VMEM((tokens, width), BF16)],
        ),
        out_shape=[jax.ShapeDtypeStruct(x.shape, x.dtype) for x in (normed_t, query, kv)],
        input_output_aliases={7: 0, 8: 1, 9: 2},
        compiler_params=pltpu.CompilerParams(vmem_limit_bytes=VMEM),
        cost_estimate=pl.CostEstimate(
            flops=4 * tokens * width * width, bytes_accessed=8 * tokens * width, transcendentals=0
        ),
        name="project_last",
    )(ints, weights, own, before, behind, order, gains, normed_t, query, kv)


def split_order(split, splits, unit):
    def source_of(count):
        part = count // splits

        def source(index):
            r = lax.rem(split + index // part, splits)
            index = lax.rem(index, part)
            return (index // unit * splits + r) * unit + lax.rem(index, unit)

        return source

    return source_of


def packed_rows(values, tall, low):
    piece = math.gcd(tall, low)
    across, down = low // piece, tall // piece
    wide = values.shape[1] // across
    rows = []
    for start in range(0, values.shape[0], tall):
        for part in range(across):
            columns = slice(wide * part, wide * (part + 1))
            rows.append(
                jnp.concatenate(
                    [
                        values[start + piece * i : start + piece * (i + 1), columns]
                        for i in range(down)
                    ],
                    axis=1,
                )
            )
    return jnp.concatenate(rows, axis=0)


def unpacked_rows(values, tall, low, columns):
    piece = math.gcd(tall, low)
    across, down = low // piece, tall // piece
    wide = columns // across
    rows = []
    for start in range(0, values.shape[0], low):
        for index in range(down):
            lanes = slice(wide * index, wide * (index + 1))
            rows.append(
                jnp.concatenate(
                    [
                        values[start + piece * part : start + piece * (part + 1), lanes]
                        for part in range(across)
                    ],
                    axis=1,
                )
            )
    return jnp.concatenate(rows, axis=0)


def block_kernel(
    dims, heads, ints, tokens, w_out, gains, w_gate, w_up, w_packed, upstream, *refs
):
    rows_apart, groups, splits = dims
    contexts, refs = refs[:heads], refs[heads:]
    result, d_mixed, d_first, d_rest = refs[:4]
    grads_wide, grads_down = refs[4 : 4 + splits], refs[4 + splits : 4 + 2 * splits]
    (context_t, mixed, normed, normed_t, d_normed, total, order, order_hidden) = refs[4 + 2 * splits :]
    step, chunks = pl.program_id(0), pl.num_programs(0) - 1
    width, chunk = w_gate.shape
    devices = rows_apart * groups * splits
    hidden_unit = chunk * chunks // devices
    gain = gains[1:2, :]

    @pl.when(step == 0)
    def first():
        order[...] = chosen(
            (width, width), split_order(ints[0], splits, width // devices)(width)
        )
        order_hidden[...] = chosen((chunk, chunk), split_order(ints[0], splits, hidden_unit)(chunk))
        each = width // groups // heads
        for g in range(groups):
            for head in range(heads):
                start = (g * heads + head) * each
                context_t[start : start + each, :] = contexts[head][g]
        context = jnp.transpose(context_t[...].astype(F32)).astype(BF16)
        values = tokens[...].astype(F32) + dot_nn(context, w_out[...])
        mixed[...] = values
        total[...] = values
        normed[...] = rms_scale(values, gain).astype(BF16)
        normed_t[...] = dot_nt(order[...], normed[...]).astype(BF16)
        d_normed[...] = jnp.zeros_like(d_normed)

    def stored(outs, rows, values):
        part = values.shape[0] // splits
        for other in range(splits):
            outs[other][:, rows] = values[part * other : part * (other + 1)].astype(BF16)

    @pl.when(step < chunks)
    def work():
        w_down = unpacked_rows(
            w_packed[...].astype(F32), hidden_unit, width // devices, width
        ).astype(BF16)
        gate = dot_nn(normed[...], w_gate[...])
        upward = dot_nn(normed[...], w_up[...])
        d_hidden = dot_nt(upstream[...], w_down)
        square = gate * gate
        turn = jnp.tanh(GELU_SCALE * (gate + 0.044715 * gate * square))
        half = 0.5 * (1.0 + turn)
        active = gate * half
        slope = half + 0.5 * gate * (1.0 - turn * turn) * (GELU_SCALE * (1.0 + 0.134145 * square))
        hidden = (active * upward).astype(BF16)
        d_gate = (d_hidden * upward * slope).astype(BF16)
        d_up = (d_hidden * active).astype(BF16)
        total[...] += dot_nn(hidden, w_down)
        d_normed[...] += dot_nt(d_gate, w_gate[...]) + dot_nt(d_up, w_up[...])
        hidden_t = dot_nt(order_hidden[...], hidden).astype(BF16)

        down = dot_nn(hidden_t, upstream[...])
        part = chunk // splits
        for other in range(splits):
            grads_down[other][...] = packed_rows(
                down[part * other : part * (other + 1)], hidden_unit, width // devices
            ).astype(BF16)
        stored(grads_wide, slice(0, chunk), dot_nn(normed_t[...], d_gate))
        stored(grads_wide, slice(chunk, 2 * chunk), dot_nn(normed_t[...], d_up))

    @pl.when(step == chunks)
    def finish():
        result[...] = total[...].astype(BF16)
        back = upstream[...].astype(F32) + rms_back(mixed[...], gain, d_normed[...])
        d_mixed[...] = back
        branch = back.astype(BF16)
        d_context = dot_nt(w_out[...], branch).astype(BF16)
        each = d_first.shape[1]
        size = width // groups
        for g in range(groups):
            d_first[g] = d_context[size * g : size * g + each]
            d_rest[g] = d_context[size * g + each : size * (g + 1)]
        ordered = dot_nn(order[...], context_t[...]).astype(BF16)
        stored(grads_wide, slice(0, width), dot_nn(ordered, branch))
        for out in grads_wide:
            out[:, width:] = jnp.zeros((out.shape[0], out.shape[1] - width), BF16)


def feed_forward(dims, ints, tokens, contexts, gains, late, upstream):
    groups, splits = dims[1:]
    rows, width = tokens.shape
    hidden = (late.shape[1] - width) // 3
    chunk = 2 * TILE
    steps = hidden // chunk
    each = contexts[0].shape[1]
    full = lambda *shape: pl.BlockSpec(shape, lambda step: (0,) * len(shape))
    return pl.pallas_call(
        functools.partial(block_kernel, dims, len(contexts)),
        grid=(steps + 1,),
        in_specs=[
            smem(),
            full(rows, width),
            pl.BlockSpec((width, width), lambda step: (0, 3 * hidden // width)),
            full(8, width),
            pl.BlockSpec((width, chunk), lambda step: (0, steps + jnp.minimum(step, steps - 1))),
            pl.BlockSpec(
                (width, chunk), lambda step: (0, 2 * steps + jnp.minimum(step, steps - 1))
            ),
            pl.BlockSpec((width // steps, hidden), lambda step: (jnp.minimum(step, steps - 1), 0)),
            full(rows, width),
        ]
        + [full(*context.shape) for context in contexts],
        out_specs=[
            full(rows, width),
            full(rows, width),
            full(groups, each, rows),
            full(groups, width // groups - each, rows),
        ]
        + [pl.BlockSpec((width // splits, 2 * chunk), lambda step: (0, step))] * splits
        + [
            pl.BlockSpec(
                (width // splits // steps, hidden), lambda step: (jnp.minimum(step, steps - 1), 0)
            )
        ]
        * splits,
        out_shape=[
            jax.ShapeDtypeStruct((rows, width), BF16),
            jax.ShapeDtypeStruct((rows, width), F32),
            jax.ShapeDtypeStruct((groups, each, rows), BF16),
            jax.ShapeDtypeStruct((groups, width // groups - each, rows), BF16),
        ]
        + [jax.ShapeDtypeStruct((width // splits, 2 * hidden + 2 * chunk), BF16)] * splits
        + [jax.ShapeDtypeStruct((width // splits, hidden), BF16)] * splits,
        scratch_shapes=[
            pltpu.VMEM((width, rows), BF16),
            pltpu.VMEM((rows, width), F32),
            pltpu.VMEM((rows, width), BF16),
            pltpu.VMEM((width, rows), BF16),
            pltpu.VMEM((rows, width), F32),
            pltpu.VMEM((rows, width), F32),
            pltpu.VMEM((width, width), BF16),
            pltpu.VMEM((chunk, chunk), BF16),
        ],
        compiler_params=pltpu.CompilerParams(vmem_limit_bytes=VMEM),
        cost_estimate=pl.CostEstimate(
            flops=18 * rows * width * hidden + 6 * rows * width * width,
            bytes_accessed=12 * width * hidden,
            transcendentals=rows * hidden,
        ),
        name="feed_forward",
    )(ints, tokens, late, gains, late, late, late, upstream, *contexts)


def weight_kernel(splits, normed_t, *refs):
    d_heads, outs, total = refs[: -splits - 1], refs[-splits - 1 : -1], refs[-1]
    step = pl.program_id(0)
    added = dot_nt(normed_t[...], jnp.concatenate([d_head[...] for d_head in d_heads], axis=0))

    @pl.when(step == 0)
    def _():
        total[...] = added

    @pl.when(step > 0)
    def _():
        total[...] += added

    @pl.when(step == pl.num_programs(0) - 1)
    def _():
        part = total.shape[0] // splits
        for other in range(splits):
            outs[other][...] = total[part * other : part * (other + 1), :].astype(BF16)


def weight_grads(splits, normed_t, d_heads):
    groups, rows, tokens = d_heads[0].shape
    width = normed_t.shape[0]
    out = (width // splits, rows * len(d_heads))
    return pl.pallas_call(
        functools.partial(weight_kernel, splits),
        grid=(groups,),
        in_specs=[pl.BlockSpec((width, tokens), lambda step: (0, step))]
        + [by_slot(rows, tokens)] * len(d_heads),
        out_specs=[pl.BlockSpec(out, lambda step: (0, 0))] * splits,
        out_shape=[jax.ShapeDtypeStruct(out, BF16)] * splits,
        scratch_shapes=[pltpu.VMEM((width, out[1]), F32)],
        compiler_params=pltpu.CompilerParams(vmem_limit_bytes=VMEM),
        cost_estimate=pl.CostEstimate(
            flops=2 * width * out[1] * groups * tokens,
            bytes_accessed=2 * width * groups * tokens,
            transcendentals=0,
        ),
        name="weight_grads",
    )(normed_t, *d_heads)


def added_kernel(count, *refs):
    held, outs = refs[:count], refs[count:]
    total = held[0][...].astype(F32)
    for piece in held[1:]:
        total += piece[...].astype(F32)
    part = total.shape[0] // len(outs)
    for index, out in enumerate(outs):
        out[...] = total[part * index : part * (index + 1)].astype(out.dtype)


def added(pieces, parts):
    rows, columns = pieces[0].shape
    return pl.pallas_call(
        functools.partial(added_kernel, len(pieces)),
        out_shape=[jax.ShapeDtypeStruct((rows // parts, columns), BF16)] * parts,
        compiler_params=pltpu.CompilerParams(vmem_limit_bytes=VMEM),
        cost_estimate=pl.CostEstimate(flops=0, bytes_accessed=2**20, transcendentals=0),
        name="added",
    )(*pieces)


def joined_kernel(count, *refs):
    wide, down, out = refs[:count], refs[count : 2 * count], refs[-1]
    columns = wide[0].shape[1]
    for pieces, lanes in ((wide, slice(0, columns)), (down, slice(columns, out.shape[1]))):
        total = pieces[0][...].astype(F32)
        for piece in pieces[1:]:
            total += piece[...].astype(F32)
        out[:, lanes] = total.astype(BF16)


def joined(wide, down):
    rows, columns = wide[0].shape[0], wide[0].shape[1] + down[0].shape[1]
    block = lambda size: pl.BlockSpec((rows // 4, size), lambda step: (step, 0))
    return pl.pallas_call(
        functools.partial(joined_kernel, len(wide)),
        grid=(4,),
        in_specs=[block(piece.shape[1]) for piece in (*wide, *down)],
        out_specs=block(columns),
        out_shape=jax.ShapeDtypeStruct((rows, columns), BF16),
        compiler_params=pltpu.CompilerParams(vmem_limit_bytes=VMEM),
        cost_estimate=pl.CostEstimate(flops=0, bytes_accessed=2**20, transcendentals=0),
        name="joined",
    )(*wide, *down)


def unpacked(pieces, heads, size):
    return jnp.concatenate(
        [
            piece[:, (3 * head + part) * size : (3 * head + part + 1) * size]
            for part in range(3)
            for piece in pieces
            for head in range(heads)
        ],
        axis=1,
    )


def count_kernel(groups, heads, size, count, down, ints, *refs):
    held, tables, grads = refs[:count], refs[count : count + heads], refs[count + heads]
    outs, counts = refs[count + heads + 1 : -1], refs[-1]
    total = held[0][...].astype(F32)
    for piece in held[1:]:
        total += piece[...].astype(F32)
    part = total.shape[0] // groups
    blank = jnp.zeros((part, counts.shape[1] - total.shape[1]), F32)
    for index, out in enumerate(outs):
        rows = total[part * index : part * (index + 1)]
        out[...] = jnp.concatenate([rows, blank], axis=1)
    squares = jnp.sum(total * total, axis=0, keepdims=True)
    table = jnp.concatenate(
        [jnp.sum(jnp.transpose(table[...]), axis=0, keepdims=True) for table in tables], axis=1
    )
    mine = [(ints[4] == g).astype(F32) for g in range(groups)]
    values = grads[...].astype(F32)
    values = values * values
    wide = values.shape[1] - down[0]
    piece = math.gcd(*down[1:3])
    across = down[2] // piece
    each = down[0] * piece // down[1]
    packed = []
    for part in range(across):
        rows = jnp.sum(values[piece * part : piece * (part + 1), wide:], axis=0, keepdims=True)
        packed.append(sum(rows[:, start : start + each] for start in range(0, down[0], each)))
    row = jnp.concatenate(
        [table * own for own in mine]
        + [unpacked([squares * own for own in mine], heads, size)]
        + [jnp.sum(values[:, : wide - down[3]], axis=0, keepdims=True)]
        + packed,
        axis=1,
    )
    counts[...] = jnp.zeros_like(counts)
    each = counts.shape[1]
    for start in range(0, row.shape[1], each):
        held_row = row[:, start : start + each]
        counts[start // each : start // each + 1, : held_row.shape[1]] = held_row


def counted(groups, heads, size, ints, pieces, tables, grads, down):
    rows, columns = pieces[0].shape
    buckets = tables[0].shape[0]
    length = groups * (heads * buckets + columns) + grads.shape[1] - down[0] - down[3]
    length += down[0] * down[2] // down[1]
    across = -(-columns // LANES) * LANES
    counts = -(-length // (8 * across)) * 8
    vmem = pl.BlockSpec(memory_space=pltpu.VMEM)
    return pl.pallas_call(
        functools.partial(count_kernel, groups, heads, size, len(pieces), down),
        in_specs=[smem()] + [vmem] * (len(pieces) + len(tables) + 1),
        out_shape=[jax.ShapeDtypeStruct((rows // groups, across), F32)] * groups
        + [jax.ShapeDtypeStruct((counts, across), F32)],
        compiler_params=pltpu.CompilerParams(vmem_limit_bytes=VMEM),
        cost_estimate=pl.CostEstimate(flops=0, bytes_accessed=2**20, transcendentals=0),
        name="counted",
    )(ints, *pieces, *tables, grads)


def input_kernel(heads, weights, own, gains, d_mixed, *refs):
    d_heads, (out, total) = refs[:heads], refs[heads:]
    step = pl.program_id(0)
    size = d_heads[0].shape[0] // 3
    blank = jnp.zeros((size, own.shape[0]), BF16)
    pieces = [d_head[size:, :] for d_head in d_heads]
    pieces += [d_head[:size, :] for d_head in d_heads] + [blank]
    added = dot_nn(weights[...], jnp.concatenate(pieces, axis=0))

    @pl.when(step == 0)
    def _():
        total[...] = added

    @pl.when(step > 0)
    def _():
        total[...] += added

    @pl.when(step == pl.num_programs(0) - 1)
    def _():
        back = rms_back(own[...].astype(F32), gains[0:1, :], jnp.transpose(total[...]))
        out[...] = (d_mixed[...] + back).astype(BF16)


def input_grads(groups, weights, own, gains, d_mixed, d_heads):
    tokens, width = own.shape
    full = lambda *shape: pl.BlockSpec(shape, lambda step: (0,) * len(shape))
    return pl.pallas_call(
        functools.partial(input_kernel, len(d_heads)),
        grid=(groups,),
        in_specs=[
            pl.BlockSpec((width, weights.shape[1] // groups), lambda step: (0, step)),
            full(tokens, width),
            full(8, width),
            full(tokens, width),
        ]
        + [by_slot(*d_heads[0].shape[1:])] * len(d_heads),
        out_specs=full(tokens, width),
        out_shape=jax.ShapeDtypeStruct((tokens, width), BF16),
        scratch_shapes=[pltpu.VMEM((width, tokens), F32)],
        compiler_params=pltpu.CompilerParams(vmem_limit_bytes=VMEM),
        name="input_grads",
    )(weights, own, gains, d_mixed, *d_heads)


def by_slot(rows, tokens):
    return pl.BlockSpec((None, rows, tokens), lambda slot: (slot, 0, 0))


def smem():
    return pl.BlockSpec(memory_space=pltpu.SMEM)


def attend(head, tokens, groups, splits, ints, table, query, kvs):
    seq, rows = tokens * groups * splits, tokens * groups
    half = LANES // 2
    whole = pl.BlockSpec((rows, LANES), lambda slot: (0, head))
    return pl.pallas_call(
        functools.partial(forward_kernel, tokens, groups, splits),
        grid=(groups,),
        in_specs=[smem(), smem(), pl.BlockSpec((tokens, LANES), lambda slot: (slot, head))]
        + [whole] * splits,
        out_specs=[
            pl.BlockSpec((seq, tokens), lambda slot: (slot, 0)),
            by_slot(half, tokens),
            by_slot(half + 16, tokens),
        ],
        out_shape=[
            jax.ShapeDtypeStruct((groups * seq, tokens), BF16),
            jax.ShapeDtypeStruct((groups, half, tokens), BF16),
            jax.ShapeDtypeStruct((groups, half + 16, tokens), F32),
        ],
        scratch_shapes=[
            pltpu.VMEM((seq + 2 * LANES, LANES), BF16),
            pltpu.VMEM((half + 16, seq + 2 * LANES), BF16),
            pltpu.VMEM((tokens + 2 * LANES, tokens), F32),
            pltpu.VMEM((3, LANES, LANES), F32),
            pltpu.VMEM((8, tokens), F32),
        ],
        compiler_params=pltpu.CompilerParams(vmem_limit_bytes=VMEM),
        cost_estimate=pl.CostEstimate(
            flops=16 * seq * rows * half, bytes_accessed=2 * seq * rows, transcendentals=seq * rows
        ),
        name="attend",
    )(ints, table, query, *kvs)


def attend_back(
    head, tokens, groups, splits, ints, buckets, query, d_context, place, stats, probs, kvs
):
    seq, rows = tokens * groups * splits, tokens * groups
    half = LANES // 2
    whole = pl.BlockSpec((rows, LANES), lambda slot: (0, head))
    kept = pl.BlockSpec((groups, LANES, tokens), lambda slot: (0, 0, 0))
    return pl.pallas_call(
        functools.partial(backward_kernel, tokens, groups, splits),
        grid=(groups,),
        in_specs=[
            smem(),
            pl.BlockSpec((tokens, LANES), lambda slot: (slot, head)),
            pl.BlockSpec((None, None, half, tokens), lambda slot: (slot, place, 0, 0)),
            by_slot(half + 16, tokens),
            pl.BlockSpec((seq, tokens), lambda slot: (slot, 0)),
        ]
        + [whole] * splits,
        out_specs=[pl.BlockSpec((groups, half + LANES, tokens), lambda slot: (0, 0, 0))]
        + [kept] * (splits - 1)
        + [pl.BlockSpec((buckets, LANES), lambda slot: (0, 0))],
        out_shape=[jax.ShapeDtypeStruct((groups, half + LANES, tokens), BF16)]
        + [jax.ShapeDtypeStruct((groups, LANES, tokens), BF16)] * (splits - 1)
        + [jax.ShapeDtypeStruct((buckets, LANES), F32)],
        scratch_shapes=[
            pltpu.VMEM((seq + 2 * LANES, LANES), BF16),
            pltpu.VMEM((half + 16, seq + 2 * LANES), BF16),
            pltpu.VMEM((seq + 2 * LANES, LANES), F32),
            pltpu.VMEM((3, LANES, LANES), F32),
            pltpu.VMEM((2, 8, tokens), F32),
            pltpu.VMEM((half + 16, tokens), F32),
        ],
        compiler_params=pltpu.CompilerParams(vmem_limit_bytes=VMEM),
        cost_estimate=pl.CostEstimate(
            flops=32 * seq * rows * half, bytes_accessed=2 * seq * rows, transcendentals=0
        ),
        name="attend_back",
    )(ints, query, d_context, stats, probs, *kvs)


def factored(grad_shard, column_total, row_old, column_old, row_total):
    columns = grad_shard.shape[1]
    mean_square = jnp.sum(column_total) / (row_total * columns) + EPSILON
    row_new = (
        DECAY_RATE * row_old
        + (1.0 - DECAY_RATE) * (jnp.sum(grad_shard * grad_shard, axis=1) / columns) / mean_square
    )
    column_new = (
        DECAY_RATE * column_old + (1.0 - DECAY_RATE) * (column_total / row_total) / mean_square
    )
    return (row_new, column_new)


def shards(
    tokens,
    lengths,
    norm_one,
    w_qkv,
    rel_table,
    w_out,
    norm_two,
    w_gateup,
    w_down,
    cotangent,
    row_qkv,
    col_qkv,
    row_out,
    col_out,
    row_gateup,
    col_gateup,
    row_down,
    col_down,
):
    own = tokens[0]
    tok_rows, width = own.shape
    heads = rel_table.shape[1]
    buckets = rel_table.shape[0]
    rows_apart, groups, splits = (lax.axis_size(name) for name in ALL)
    group_heads = heads // groups
    head_size = width // heads
    group, split = lax.axis_index("group"), lax.axis_index("split")
    group_width = width // groups

    def ahead(array, axis, by):
        size = lax.axis_size(axis)
        return lax.ppermute(array, axis, [((i + by) % size, i) for i in range(size)])

    def swap_groups(array):
        return lax.all_to_all(array, "group", 0, 0)

    def swap_rows(array):
        return lax.all_to_all(array, "batch", 0, 0)

    def line(array, by):
        pairs = [(i, i + by) for i in range(groups) if 0 <= i + by < groups]
        return lax.ppermute(array, "group", pairs)

    before, behind = [own], [own]
    for _ in range(groups - 1):
        before.append(line(before[-1], 1))
        behind.append(line(behind[-1], -1))

    unit = w_qkv.shape[0]
    by_part = w_qkv.reshape(unit, 3, groups, group_heads, head_size)
    gains = jnp.pad(jnp.stack([norm_one, norm_two], axis=1), ((0, 0), (0, head_size - 2)))
    packed = jnp.concatenate(
        [
            jnp.concatenate([by_part[:, 1], by_part[:, 2]], axis=-1).reshape(unit, groups, -1),
            by_part[:, 0].reshape(unit, groups, -1),
            jnp.broadcast_to(gains[:, None], (unit, groups, head_size)),
        ],
        axis=2,
    )
    early = lax.all_gather(packed.reshape(unit, -1), ALL, axis=0, tiled=True)
    together = math.gcd(unit, w_down.shape[0])
    packed_down = w_down.reshape(w_down.shape[0] // together, together, unit // together, -1)
    packed_down = jnp.transpose(packed_down, (2, 1, 0, 3)).reshape(unit, -1)
    late = lax.all_gather(
        after(jnp.concatenate([packed_down, w_gateup, w_out], axis=1), before[1], behind[1]),
        ALL,
        axis=0,
        tiled=True,
    )

    dims = (rows_apart, groups, splits)
    far = jnp.where(group == 0, groups - 1, jnp.where(group == groups - 1, 0, group))
    ends = jnp.cumsum(lengths[0])
    ints = jnp.concatenate(
        [
            split.astype(jnp.int32)[None],
            ends.astype(jnp.int32),
            jnp.stack([group, lax.axis_index("batch"), far]).astype(jnp.int32),
        ]
    )
    *blocks, gains, order = project(dims, ints, early, own, before[1:-1] + behind[1:-1])
    normed_t, query, kv = project_last(
        dims, ints, early, own, before[-1], behind[-1], order, gains, *blocks
    )
    kvs = [kv] + [ahead(kv, "split", other) for other in range(1, splits)]

    table_own = lax.dynamic_slice_in_dim(rel_table.T, group * group_heads, group_heads, 0)

    contexts, moved, stats, probs = [], [], [], []
    for head in range(group_heads):
        prob, context, stat = attend(
            head,
            tok_rows,
            groups,
            splits,
            after(ints, *contexts[-1:]),
            table_own[head : head + 1],
            query,
            kvs,
        )
        contexts.append(context)
        moved.append(swap_groups(after(context, *moved[-1:])))
        stats.append(stat)
        probs.append(prob)

    outs = feed_forward(
        dims, ints, own, moved, gains, late, cotangent[0]
    )
    result, d_mixed, d_first, d_rest = outs[:4]
    grads_wide, grads_down = outs[4 : 4 + splits], outs[4 + splits :]

    def by_split(grads):
        return [grads[0]] + [ahead(grads[by], "split", splits - by) for by in range(1, splits)]

    d_first = swap_groups(d_first)
    d_rest = swap_groups(d_rest)
    d_contexts = [d_first[:, None], d_rest.reshape(groups, group_heads - 1, head_size, tok_rows)]
    wide, down = by_split(grads_wide), by_split(grads_down)
    wide[-1] = after(wide[-1], d_first)
    held = joined(wide, down)
    held = held.reshape(rows_apart, groups, -1, held.shape[-1])
    row_sum = after(lax.psum_scatter(held, "batch", scatter_dimension=0))
    grads_own = lax.psum_scatter(row_sum, "group", scatter_dimension=0)

    d_heads, d_received, d_tables = [], [], []
    ready = [(held,), ()] + [(row_sum,)] * (group_heads - 2)
    for head in range(group_heads):
        outs = attend_back(
            head,
            tok_rows,
            groups,
            splits,
            ints,
            buckets,
            query,
            after(d_contexts[int(head > 0)], *ready[head], *d_heads[-1:]),
            head - int(head > 0),
            stats[head],
            probs[head],
            kvs,
        )
        beside = d_received[-1] if head else d_contexts[1]
        if head < group_heads - 1:
            outs = lax.optimization_barrier((*outs, beside))[:-1]
        d_head = outs[0].astype(F32)
        for other in range(1, splits):
            d_kv = ahead(outs[other], "split", splits - other).astype(F32)
            d_head = d_head + jnp.pad(d_kv, ((0, 0), (head_size, 0), (0, 0)))
        d_head = d_head.astype(BF16)
        if head == group_heads - 1:
            d_head = after(d_head, beside)
        d_heads.append(d_head)
        d_received.append(swap_groups(d_head))
        d_tables.append(outs[-1])

    down_shape = (w_down.shape[0] * width // unit, w_down.shape[0], unit)
    down_start = grads_own.shape[1] - down_shape[0]
    down_shape += (down_start - w_gateup.shape[1] - width,)
    grads = weight_grads(splits, normed_t, d_heads)
    held = added(
        [grads[0]] + [ahead(grads[by], "split", splits - by) for by in range(1, splits)], rows_apart
    )
    held = [held[0]] + [ahead(held[by], "batch", rows_apart - by) for by in range(1, rows_apart)]
    held[0] = after(held[0], d_received[-1])
    *columns, counts = counted(
        groups, group_heads, head_size, ints, held, d_tables, grads_own, down_shape
    )
    d_received[-1] = after(d_received[-1], counts)
    d_inputs = input_grads(groups, early, own, gains, d_mixed, d_received)
    counts = sum([ahead(counts, "batch", by) for by in range(1, rows_apart)], counts)
    counts = after(counts, d_inputs)
    counts_rows = counts.shape[0]
    travelled = [jnp.concatenate([counts, columns[0]], axis=0)] + [
        ahead(jnp.concatenate([counts, columns[by]], axis=0), "group", groups - by)
        for by in range(1, groups)
    ]
    columns = [both[counts_rows:] for both in travelled]
    counts = sum([both[:counts_rows] for both in travelled[1:]], travelled[0][:counts_rows])
    counts = sum([ahead(counts, "split", by) for by in range(1, splits)], counts)
    pieces = []
    for index in range(groups):
        piece = columns[0]
        for by in range(1, groups):
            piece = jnp.where((group + groups - by) % groups == index, columns[by], piece)
        pieces.append(piece)
    shard_qkv = unpacked(pieces, group_heads, head_size)
    steps = w_down.shape[0] * rows_apart * groups * splits // (2 * TILE)

    def in_order(array):
        array = array.reshape(*array.shape[:-1], steps, 2, -1)
        return jnp.swapaxes(array, -3, -2).reshape(*array.shape[:-3], -1)

    shard_rest = grads_own.astype(F32)
    shard_gateup = in_order(shard_rest[:, : w_gateup.shape[1]])
    shard_out = shard_rest[:, w_gateup.shape[1] :][:, :width]
    shard_down = shard_rest[:, down_start:].reshape(
        unit // together, together, w_down.shape[0] // together, -1
    )
    shard_down = jnp.transpose(shard_down, (2, 1, 0, 3)).reshape(-1, width)
    summed = counts.reshape(-1)
    sizes = (heads * buckets, 3 * width, w_gateup.shape[1], width, width)
    table_total, column_qkv, column_gateup, column_out, column_down, _ = jnp.split(
        summed, [sum(sizes[: i + 1]) for i in range(len(sizes))]
    )
    table_total = table_total.reshape(heads, buckets)
    column_gateup = in_order(column_gateup)
    shard_gain_one = jnp.sum(w_qkv.astype(F32) * shard_qkv, axis=1) / norm_one.astype(F32)
    shard_gain_two = jnp.sum(w_gateup.astype(F32) * shard_gateup, axis=1) / norm_two.astype(F32)
    new_row_qkv, new_col_qkv = factored(shard_qkv, column_qkv, row_qkv, col_qkv, width)
    new_row_out, new_col_out = factored(shard_out, column_out, row_out, col_out, width)
    new_row_gateup, new_col_gateup = factored(
        shard_gateup, column_gateup, row_gateup, col_gateup, width
    )
    new_row_down, new_col_down = factored(
        shard_down, column_down, row_down, col_down, w_down.shape[0] * rows_apart * groups * splits
    )
    return (
        result[None],
        d_inputs[None],
        shard_gain_one,
        shard_qkv,
        table_total.T,
        shard_out,
        shard_gain_two,
        shard_gateup,
        shard_down,
        new_row_qkv,
        new_col_qkv,
        new_row_out,
        new_col_out,
        new_row_gateup,
        new_col_gateup,
        new_row_down,
        new_col_down,
    )


def solution(mesh):
    row_blocks = P("batch", ("group", "split"), None)
    split_rows = P(ALL, None)
    split_row = P(ALL)

    def run(*arrays):
        rows, ring = mesh.devices.shape
        groups = math.gcd(ring, arrays[4].shape[1])
        fine = Mesh(mesh.devices.reshape(rows, groups, ring // groups), ALL)
        return jax.shard_map(
            shards,
            mesh=fine,
            in_specs=(
                row_blocks,
                P("batch", None),
                split_row,
                split_rows,
                P(),
                split_rows,
                split_row,
                split_rows,
                split_rows,
                row_blocks,
            )
            + (split_row, P()) * 4,
            out_specs=(
                row_blocks,
                row_blocks,
                split_row,
                split_rows,
                P(),
                split_rows,
                split_row,
                split_rows,
                split_rows,
            )
            + (split_row, P()) * 4,
            check_vma=False,
        )(*arrays)

    return run
```

```python
import functools
import math

import jax
import jax.numpy as jnp
from jax import lax
from jax.experimental import pallas as pl
from jax.experimental.pallas import tpu as pltpu
from jax.sharding import Mesh
from jax.sharding import PartitionSpec as P

THRESHOLDS = (12, 16, 23, 32, 46, 64, 91)
EPSILON = 1e-06
DECAY_RATE = 0.5
GELU_SCALE = 0.7978845608028654
MASKED = -1e9
LEEWAY = 20.0
ALL = ("batch", "group", "split")
LANES = 128
TILE = 256
GROUP = 4
VMEM = 56 * 2**20
F32 = jnp.float32
BF16 = jnp.bfloat16


def bucket_of(offset):
    distance = jnp.abs(offset)
    steps_up = 8 + sum(((distance >= limit).astype(jnp.int32) for limit in THRESHOLDS))
    within = jnp.where(distance < 8, distance, steps_up)
    return within + 16 * (offset > 0).astype(jnp.int32)


def after(value, *others):
    return lax.optimization_barrier((value, *others))[0]


def rms_scale(values, gain):
    return values * lax.rsqrt(jnp.mean(values * values, axis=-1, keepdims=True) + EPSILON) * gain


def rms_back(values, gain, grad):
    scale = lax.rsqrt(jnp.mean(values * values, axis=-1, keepdims=True) + EPSILON)
    scaled = grad * gain
    return scale * scaled - values * scale**3 * jnp.mean(scaled * values, axis=-1, keepdims=True)


def dot_nn(left, right):
    return jnp.dot(left, right, preferred_element_type=F32)


def dot_nt(left, right):
    return lax.dot_general(left, right, (((1,), (1,)), ((), ())), preferred_element_type=F32)


def dot_tt(left, right):
    return lax.dot_general(left, right, (((0,), (1,)), ((), ())), preferred_element_type=F32)


class Layout:
    def __init__(self, tokens, groups, splits, ints):
        self.tokens, self.groups, self.splits = tokens, groups, splits
        self.blocks = groups * splits
        self.seq = tokens * self.blocks
        self.near = tokens + 2 * LANES
        self.subs = tokens // LANES
        self.split = ints[0]
        self.ends = (ints[1], ints[2], ints[3])
        slot = pl.program_id(0)
        self.block = self.block_of(slot, 0)
        self.first = pl.multiple_of(self.block * tokens, LANES)
        self.lefts = jnp.maximum(0, self.block * (tokens // TILE) - 1)
        self.loops = (self.seq // TILE - 2 - tokens // TILE) // GROUP
        self.edge = jnp.logical_or(self.block == 0, self.block == self.blocks - 1)

    def block_of(self, slot, other):
        return slot * self.splits + lax.rem(self.split + other, self.splits)

    def keys_of(self, tile):
        before = 2 * LANES + TILE * tile
        after = self.first + self.near + TILE * (tile - self.lefts)
        return pl.ds(pl.multiple_of(jnp.where(tile < self.lefts, before, after), LANES), TILE)

    def rows_of(self, tile):
        return pl.ds(pl.multiple_of(self.near + TILE * tile, LANES), TILE)

    def segment(self, positions):
        return sum((positions >= end).astype(jnp.int32) for end in self.ends)


def iota(shape, dim):
    return lax.broadcasted_iota(jnp.int32, shape, dim)


def fold(values):
    return values.reshape(values.shape[0] // 8, 8, values.shape[1])


def forward_kernel(tokens, groups, splits, ints, table, query, *refs):
    kvs, (probs, context, stats, k_aug, v_t, scores, biases, best) = refs[:splits], refs[splits:]
    lay = Layout(tokens, groups, splits, ints)
    half = query.shape[1] // 2
    buckets = table.shape[1]

    @pl.when(pl.program_id(0) == 0)
    def prepare():
        lane = iota((tokens, LANES), 1)
        for slot in range(groups):
            for other in range(splits):
                start = lay.block_of(slot, other) * tokens
                rows = pl.ds(pl.multiple_of(LANES + start, LANES), tokens)
                kv = kvs[other][slot * tokens : (slot + 1) * tokens, :].astype(F32)
                seg = lay.segment(start + iota((tokens, LANES), 0))
                k_aug[rows, :] = jnp.where(lane < half, kv, (lane - half == seg).astype(F32)).astype(BF16)
                turned = jnp.transpose(kv)
                ones = (iota((16, tokens), 0) == 0).astype(F32)
                v_t[:, rows] = jnp.concatenate([turned[half:], ones], axis=0).astype(BF16)
        outside = (iota((LANES, LANES), 1) == half + 3).astype(BF16)
        for start in (0, lay.seq + LANES):
            k_aug[start : start + LANES, :] = outside
            v_t[:, start : start + LANES] = jnp.zeros((half + 16, LANES), BF16)
        for place in range(3):
            bucket = bucket_of(
                LANES * (place - 1) + iota((LANES, LANES), 0) - iota((LANES, LANES), 1)
            )
            bias = jnp.zeros((LANES, LANES), F32)
            for label in range(buckets):
                bias = jnp.where(bucket == label, table[0, label], bias)
            biases[place] = bias

    far_left, far_right = table[0, buckets // 2 - 1], table[0, buckets - 1]
    positions = lay.block * tokens + iota((1, tokens), 1)
    seg_q = lay.segment(positions)
    row = iota((2 * half, tokens), 0)
    apart = jnp.logical_or(row - half != seg_q, row == half + 3)
    q_aug = jnp.where(
        row < half, jnp.transpose(query[...].astype(F32)), jnp.where(apart, MASKED, 0.0)
    ).astype(BF16)

    near = dot_nn(k_aug[pl.ds(lay.first, lay.near), :], q_aug)
    eye = iota((LANES, LANES), 0) == iota((LANES, LANES), 1)
    for sub_q in range(lay.subs):
        lanes = slice(LANES * sub_q, LANES * (sub_q + 1))
        top = None
        for sub_k in range(lay.subs + 2):
            rows = slice(LANES * sub_k, LANES * (sub_k + 1))
            place = sub_k - sub_q
            piece = near[rows, lanes] + (
                far_left if place < 0 else far_right if place > 2 else biases[place]
            )
            if place == 1:
                alone = jnp.logical_and(eye, positions[:, lanes] >= lay.ends[2])
                piece = jnp.where(alone, 0.0, piece)
            scores[rows, lanes] = piece
            high = jnp.max(fold(piece), axis=0)
            top = high if top is None else jnp.maximum(top, high)
        best[:, lanes] = top

    def sweep(peak):
        weights = jnp.exp(scores[...] - peak).astype(BF16)
        probs[: lay.near, :] = weights
        stats[...] = dot_nn(v_t[:, pl.ds(lay.first, lay.near)], weights)
        left_peak, right_peak = peak - far_left, peak - far_right

        def tiles(index, count):
            places = [lay.keys_of(index + step) for step in range(count)]
            piece = dot_nn(jnp.concatenate([k_aug[keys, :] for keys in places], axis=0), q_aug)
            parts, top = [], best[...]
            for step in range(count):
                score = piece[TILE * step : TILE * (step + 1)]
                is_left = index + step < lay.lefts
                top = jnp.maximum(
                    top,
                    jnp.max(fold(score), axis=0) + jnp.where(is_left, far_left, far_right),
                )
                part = jnp.exp(score - jnp.where(is_left, left_peak, right_peak)).astype(BF16)
                probs[lay.rows_of(index + step), :] = part
                parts.append(part)
            best[...] = top
            values = jnp.concatenate([v_t[:, keys] for keys in places], axis=1)
            stats[...] += dot_nn(values, jnp.concatenate(parts, axis=0))

        if lay.loops <= 3:
            for index in range(lay.loops):
                tiles(index * GROUP, GROUP)
        else:

            def group(index, carry):
                tiles(index * GROUP, GROUP)
                return carry

            lax.fori_loop(0, lay.loops, group, 0)

        @pl.when(lay.edge)
        def _():
            tiles(lay.loops * GROUP, 1)

    peak = jnp.max(best[...], axis=0, keepdims=True)
    sweep(peak)
    true_peak = jnp.max(best[...], axis=0, keepdims=True)

    @pl.when(jnp.max(true_peak - peak) > LEEWAY)
    def _():
        sweep(true_peak)

    inverse = 1.0 / stats[half : half + 1, :]
    result = stats[:half, :] * inverse
    context[...] = result.astype(BF16)
    stats[:half, :] = result
    stats[half : half + 1, :] = inverse


def backward_kernel(tokens, groups, splits, ints, query, d_context, stats, probs, *refs):
    kvs, d_kvs = refs[:splits], refs[splits : 2 * splits]
    d_table, v_aug, k_t, d_kv, bands, sides, d_q = refs[2 * splits :]
    lay = Layout(tokens, groups, splits, ints)
    half = query.shape[1] // 2
    buckets = d_table.shape[0]

    @pl.when(pl.program_id(0) == 0)
    def prepare():
        lane = iota((tokens, LANES), 1)
        for slot in range(groups):
            for other in range(splits):
                start = lay.block_of(slot, other) * tokens
                rows = pl.ds(pl.multiple_of(LANES + start, LANES), tokens)
                kv = kvs[other][slot * tokens : (slot + 1) * tokens, :].astype(F32)
                v_aug[rows, :] = jnp.where(lane >= half, kv, (lane < 3).astype(F32)).astype(BF16)
                ones = (iota((16, tokens), 0) == 0).astype(F32)
                k_t[:, rows] = jnp.concatenate([jnp.transpose(kv)[:half], ones], axis=0).astype(BF16)
        for start in (0, lay.seq + LANES):
            v_aug[start : start + LANES, :] = jnp.zeros((LANES, LANES), BF16)
            k_t[:, start : start + LANES] = jnp.zeros((half + 16, LANES), BF16)
        d_kv[...] = jnp.zeros_like(d_kv)
        bands[...] = jnp.zeros_like(bands)
        sides[...] = jnp.zeros_like(sides)

    inverse = stats[half : half + 1, :]
    upstream = d_context[...].astype(F32)
    delta = jnp.sum(upstream * stats[:half, :], axis=0, keepdims=True) * inverse
    scaled = upstream * inverse
    high = delta.astype(BF16).astype(F32)
    middle = (delta - high).astype(BF16).astype(F32)
    low = delta - high - middle
    row = iota((half, tokens), 0)
    shift = jnp.where(row == 0, high, jnp.where(row == 1, middle, jnp.where(row == 2, low, 0.0)))
    up_aug = jnp.concatenate([-shift, scaled], axis=0).astype(BF16)
    up_rows = jnp.transpose(jnp.concatenate([jnp.zeros_like(scaled), scaled], axis=0)).astype(BF16)
    both = jnp.concatenate([query[...], up_rows], axis=0)

    def grads(keys, rows):
        part = jnp.concatenate([probs[where, :] for where in rows], axis=0)
        values = jnp.concatenate([v_aug[where, :] for where in keys], axis=0)
        d_scores = part.astype(F32) * dot_nn(values, up_aug)
        rounded = d_scores.astype(BF16)
        added = dot_nn(jnp.concatenate([rounded, part], axis=1), both)
        size = part.shape[0] // len(keys)
        for index, where in enumerate(keys):
            d_kv[where, :] += added[size * index : size * (index + 1)]
        return d_scores, rounded

    near, rounded = grads([pl.ds(lay.first, lay.near)], [pl.ds(0, lay.near)])
    total = dot_nn(k_t[:, pl.ds(lay.first, lay.near)], rounded)
    for sub_q in range(lay.subs):
        lanes = slice(LANES * sub_q, LANES * (sub_q + 1))
        for sub_k in range(lay.subs + 2):
            piece = near[LANES * sub_k : LANES * (sub_k + 1), lanes]
            place = sub_k - sub_q
            if 0 <= place <= 2:
                bands[place] += piece
            else:
                sides[int(place > 2), :, lanes] += jnp.sum(fold(piece), axis=0)
    d_q[...] = total
    near_sum = total[half : half + 8, :]

    def far(index, count):
        places = [lay.keys_of(index + step) for step in range(count)]
        rounded = grads(places, [lay.rows_of(index + step) for step in range(count)])[1]
        keys = jnp.concatenate([k_t[:, where] for where in places], axis=1)
        lefts = jnp.clip(lay.lefts - index, 0, count) * TILE
        row = iota(keys.shape, 0)
        side = jnp.logical_and(row == half + 8, iota(keys.shape, 1) < lefts)
        keys = jnp.where(side, 1.0, keys.astype(F32)).astype(BF16)
        d_q[...] += dot_nn(keys, rounded)

    if lay.loops <= 3:
        for index in range(lay.loops):
            far(index * GROUP, GROUP)
    else:

        def group(index, carry):
            far(index * GROUP, GROUP)
            return carry

        lax.fori_loop(0, lay.loops, group, 0)

    @pl.when(lay.edge)
    def _():
        far(lay.loops * GROUP, 1)

    left_sum = d_q[half + 8 : half + 16, :]
    sides[0] += left_sum
    sides[1] += d_q[half : half + 8, :] - near_sum - left_sum
    d_kvs[0][pl.program_id(0), :half, :] = d_q[:half, :].astype(BF16)

    @pl.when(pl.program_id(0) == groups - 1)
    def finish():
        for slot in range(groups):
            for other in range(splits):
                start = lay.block_of(slot, other) * tokens
                rows = pl.ds(pl.multiple_of(LANES + start, LANES), tokens)
                turned = jnp.transpose(d_kv[rows, :]).astype(BF16)
                if other:
                    d_kvs[other][slot] = turned
                else:
                    d_kvs[0][slot, half:, :] = turned
        labels = [
            bucket_of(LANES * (place - 1) + iota((LANES, LANES), 0) - iota((LANES, LANES), 1))
            for place in range(3)
        ]
        for label in range(buckets):
            found = jnp.zeros((8, LANES), F32)
            for place in range(3):
                kept = jnp.where(labels[place] == label, bands[place], 0.0)
                found += jnp.sum(fold(kept), axis=0)
            if label in (buckets // 2 - 1, buckets - 1):
                side = sides[int(label == buckets - 1)]
                for sub in range(lay.subs):
                    found += side[:, LANES * sub : LANES * (sub + 1)]
            d_table[label : label + 1, :] = jnp.sum(found, axis=0, keepdims=True)


def chosen(shape, source):
    return (source(iota((shape[0], 1), 0)) == iota(shape, 1)).astype(F32).astype(BF16)


def project_block(values, weights, gains, order, normed_t, query, kv):
    normed = rms_scale(values.astype(F32), gains[0:1, :]).astype(BF16)
    normed_t[...] = dot_nt(order[...], normed).astype(BF16)
    both = dot_nn(normed, weights[...])
    narrow = kv.shape[1]
    kv[...] = both[:, :narrow].astype(BF16)
    size = LANES // 2
    blank = jnp.zeros((both.shape[0], size), F32)
    parts = []
    for start in range(narrow, narrow + narrow // 2, size):
        parts += [both[:, start : start + size], blank]
    query[...] = jnp.concatenate(parts, axis=1).astype(BF16)


def project_kernel(dims, ints, weights, own, *refs):
    rows_apart, groups, splits = dims
    others, (normed_t, query, kv, gains, order, values) = refs[:-6], refs[-6:]
    slot, split, group, batch = pl.program_id(0), ints[0], ints[4], ints[5]
    width, narrow = own.shape[1], kv.shape[1]
    unit = width // (rows_apart * groups * splits)

    @pl.when(slot == 0)
    def _():
        def source(index):
            within = lax.rem(index, unit)
            index = index // unit
            g = lax.rem(group + lax.rem(index, groups), groups)
            index = index // groups
            b = lax.rem(batch + lax.rem(index, rows_apart), rows_apart)
            r = lax.rem(split + index // rows_apart, splits)
            return ((b * groups + g) * splits + r) * unit + within

        order[...] = chosen((width, width), source)
        turned = jnp.transpose(weights[:, weights.shape[1] - LANES :].astype(F32))
        gains[...] = turned[LANES // 2 : LANES // 2 + 8]

    @pl.when(slot == group)
    def _():
        values[...] = own[...]

    for by in range(1, groups - 1):

        @pl.when(slot == group - by)
        def _():
            values[...] = others[by - 1][...]

        @pl.when(slot == group + by)
        def _():
            values[...] = others[groups + by - 3][...]

    @pl.when(jnp.abs(slot - group) < groups - 1)
    def _():
        project_block(values[...], weights, gains, order, normed_t, query, kv)


def project(dims, ints, weights, own, others):
    tokens, width = own.shape
    groups = dims[1]
    narrow = 2 * width // groups
    whole = pl.BlockSpec((tokens, width), lambda slot, ints: (0, 0))
    by_row = pl.BlockSpec((tokens, narrow), lambda slot, ints: (slot, 0))
    return pl.pallas_call(
        functools.partial(project_kernel, dims),
        grid_spec=pltpu.PrefetchScalarGridSpec(
            num_scalar_prefetch=1,
            grid=(groups,),
            in_specs=[pl.BlockSpec((width, weights.shape[1] // groups), lambda slot, ints: (0, ints[4]))]
            + [whole] * (1 + len(others)),
            out_specs=[
                pl.BlockSpec((width, tokens), lambda slot, ints: (0, slot)),
                by_row,
                by_row,
                pl.BlockSpec((8, width), lambda slot, ints: (0, 0)),
                pl.BlockSpec((width, width), lambda slot, ints: (0, 0)),
            ],
            scratch_shapes=[pltpu.VMEM((tokens, width), BF16)],
        ),
        out_shape=[
            jax.ShapeDtypeStruct((width, groups * tokens), BF16),
            jax.ShapeDtypeStruct((groups * tokens, narrow), BF16),
            jax.ShapeDtypeStruct((groups * tokens, narrow), BF16),
            jax.ShapeDtypeStruct((8, width), F32),
            jax.ShapeDtypeStruct((width, width), BF16),
        ],
        compiler_params=pltpu.CompilerParams(vmem_limit_bytes=VMEM),
        cost_estimate=pl.CostEstimate(
            flops=4 * groups * tokens * width * width,
            bytes_accessed=8 * groups * tokens * width,
            transcendentals=0,
        ),
        name="project",
    )(ints, weights, own, *others)


def project_last_kernel(groups, ints, weights, own, before, behind, order, gains, *refs):
    normed_t, query, kv, values = refs[3:]
    group = ints[4]
    values[...] = own[...]

    @pl.when(group == 0)
    def _():
        values[...] = behind[...]

    @pl.when(group == groups - 1)
    def _():
        values[...] = before[...]

    project_block(values[...], weights, gains, order, normed_t, query, kv)


def project_last(dims, ints, weights, own, before, behind, order, gains, normed_t, query, kv):
    tokens, width = own.shape
    narrow = kv.shape[1]
    whole = lambda array: pl.BlockSpec(array.shape, lambda step, ints: (0, 0))
    by_row = pl.BlockSpec((tokens, narrow), lambda step, ints: (ints[6], 0))
    return pl.pallas_call(
        functools.partial(project_last_kernel, dims[1]),
        grid_spec=pltpu.PrefetchScalarGridSpec(
            num_scalar_prefetch=1,
            grid=(1,),
            in_specs=[
                pl.BlockSpec((width, weights.shape[1] // dims[1]), lambda step, ints: (0, ints[4]))
            ]
            + [whole(array) for array in (own, before, behind, order, gains)]
            + [pl.BlockSpec(memory_space=pl.ANY)] * 3,
            out_specs=[
                pl.BlockSpec((width, tokens), lambda step, ints: (0, ints[6])),
                by_row,
                by_row,
            ],
            scratch_shapes=[pltpu.VMEM((tokens, width), BF16)],
        ),
        out_shape=[jax.ShapeDtypeStruct(x.shape, x.dtype) for x in (normed_t, query, kv)],
        input_output_aliases={7: 0, 8: 1, 9: 2},
        compiler_params=pltpu.CompilerParams(vmem_limit_bytes=VMEM),
        cost_estimate=pl.CostEstimate(
            flops=4 * tokens * width * width, bytes_accessed=8 * tokens * width, transcendentals=0
        ),
        name="project_last",
    )(ints, weights, own, before, behind, order, gains, normed_t, query, kv)


def scatter_order(groups, splits, unit):
    def source(index):
        within = lax.rem(index, unit)
        index = index // unit
        g = lax.rem(index, groups)
        index = index // groups
        r = lax.rem(index, splits)
        return ((index // splits * groups + g) * splits + r) * unit + within

    return source


def packed_rows(values, tall, low):
    piece = math.gcd(tall, low)
    across, down = low // piece, tall // piece
    wide = values.shape[1] // across
    rows = []
    for start in range(0, values.shape[0], tall):
        for part in range(across):
            columns = slice(wide * part, wide * (part + 1))
            rows.append(
                jnp.concatenate(
                    [
                        values[start + piece * i : start + piece * (i + 1), columns]
                        for i in range(down)
                    ],
                    axis=1,
                )
            )
    return jnp.concatenate(rows, axis=0)


def unpacked_rows(values, tall, low, columns):
    piece = math.gcd(tall, low)
    across, down = low // piece, tall // piece
    wide = columns // across
    rows = []
    for start in range(0, values.shape[0], low):
        for index in range(down):
            lanes = slice(wide * index, wide * (index + 1))
            rows.append(
                jnp.concatenate(
                    [
                        values[start + piece * part : start + piece * (part + 1), lanes]
                        for part in range(across)
                    ],
                    axis=1,
                )
            )
    return jnp.concatenate(rows, axis=0)


def block_kernel(
    dims, heads, ints, tokens, w_out, gains, w_gate, w_up, w_packed, upstream, *refs
):
    rows_apart, groups, splits = dims
    contexts, refs = refs[:heads], refs[heads:]
    result, d_mixed, d_first, d_rest, grads = refs[:5]
    (context_t, mixed, normed, normed_t, d_normed, total, order, order_hidden) = refs[5:13]
    wide, down, sems = refs[13:]
    step, chunks = pl.program_id(0), pl.num_programs(0) - 1
    width, chunk = w_gate.shape
    devices = rows_apart * groups * splits
    hidden_unit = chunk * chunks // devices
    gain = gains[1:2, :]

    @pl.when(step == 0)
    def first():
        order[...] = chosen((width, width), scatter_order(groups, splits, width // devices))
        order_hidden[...] = chosen((chunk, chunk), scatter_order(groups, splits, hidden_unit))
        each = width // groups // heads
        for g in range(groups):
            for head in range(heads):
                start = (g * heads + head) * each
                context_t[start : start + each, :] = contexts[head][g]
        context = jnp.transpose(context_t[...].astype(F32)).astype(BF16)
        values = tokens[...].astype(F32) + dot_nn(context, w_out[...])
        mixed[...] = values
        total[...] = values
        normed[...] = rms_scale(values, gain).astype(BF16)
        normed_t[...] = dot_nt(order[...], normed[...]).astype(BF16)
        d_normed[...] = jnp.zeros_like(d_normed)

    place = lax.rem(step, 2)
    tall = down.shape[1]

    def wide_copy(slot, index):
        columns = pl.ds(pl.multiple_of(index * 2 * chunk, 2 * chunk), 2 * chunk)
        return pltpu.make_async_copy(wide.at[slot], grads.at[:, columns], sems.at[0, slot])

    def down_copy(slot, index):
        rows = pl.ds(pl.multiple_of(index * tall, tall), tall)
        columns = pl.ds(grads.shape[1] - down.shape[2], down.shape[2])
        return pltpu.make_async_copy(down.at[slot], grads.at[rows, columns], sems.at[1, slot])

    @pl.when(step >= 2)
    def _():
        wide_copy(place, step - 2).wait()
        down_copy(place, step - 2).wait()

    @pl.when(step < chunks)
    def work():
        w_down = unpacked_rows(
            w_packed[...].astype(F32), hidden_unit, width // devices, width
        ).astype(BF16)
        gate = dot_nn(normed[...], w_gate[...])
        upward = dot_nn(normed[...], w_up[...])
        d_hidden = dot_nt(upstream[...], w_down)
        square = gate * gate
        turn = jnp.tanh(GELU_SCALE * (gate + 0.044715 * gate * square))
        half = 0.5 * (1.0 + turn)
        active = gate * half
        slope = half + 0.5 * gate * (1.0 - turn * turn) * (GELU_SCALE * (1.0 + 0.134145 * square))
        hidden = (active * upward).astype(BF16)
        d_gate = (d_hidden * upward * slope).astype(BF16)
        d_up = (d_hidden * active).astype(BF16)
        total[...] += dot_nn(hidden, w_down)
        d_normed[...] += dot_nt(d_gate, w_gate[...]) + dot_nt(d_up, w_up[...])
        hidden_t = dot_nt(order_hidden[...], hidden).astype(BF16)

        d_down = dot_nn(hidden_t, upstream[...])
        down[place] = packed_rows(d_down, hidden_unit, width // devices).astype(BF16)
        wide[place, :, :chunk] = dot_nn(normed_t[...], d_gate).astype(BF16)
        wide[place, :, chunk:] = dot_nn(normed_t[...], d_up).astype(BF16)
        wide_copy(place, step).start()
        down_copy(place, step).start()

    @pl.when(step == chunks)
    def finish():
        result[...] = total[...].astype(BF16)
        back = upstream[...].astype(F32) + rms_back(mixed[...], gain, d_normed[...])
        d_mixed[...] = back
        branch = back.astype(BF16)
        d_context = dot_nt(w_out[...], branch).astype(BF16)
        each = d_first.shape[1]
        size = width // groups
        for g in range(groups):
            d_first[g] = d_context[size * g : size * g + each]
            d_rest[g] = d_context[size * g + each : size * (g + 1)]
        ordered = dot_nn(order[...], context_t[...]).astype(BF16)
        wide[place, :, :width] = dot_nn(ordered, branch).astype(BF16)
        wide[place, :, width:] = jnp.zeros((width, 2 * chunk - width), BF16)
        wide_copy(place, step).start()
        wide_copy(1 - place, step - 1).wait()
        down_copy(1 - place, step - 1).wait()
        wide_copy(place, step).wait()


def feed_forward(dims, ints, tokens, contexts, gains, late, upstream):
    groups, splits = dims[1:]
    rows, width = tokens.shape
    hidden = (late.shape[1] - width) // 3
    chunk = 2 * TILE
    steps = hidden // chunk
    each = contexts[0].shape[1]
    full = lambda *shape: pl.BlockSpec(shape, lambda step: (0,) * len(shape))
    return pl.pallas_call(
        functools.partial(block_kernel, dims, len(contexts)),
        grid=(steps + 1,),
        in_specs=[
            smem(),
            full(rows, width),
            pl.BlockSpec((width, width), lambda step: (0, 3 * hidden // width)),
            full(8, width),
            pl.BlockSpec((width, chunk), lambda step: (0, steps + jnp.minimum(step, steps - 1))),
            pl.BlockSpec(
                (width, chunk), lambda step: (0, 2 * steps + jnp.minimum(step, steps - 1))
            ),
            pl.BlockSpec((width // steps, hidden), lambda step: (jnp.minimum(step, steps - 1), 0)),
            full(rows, width),
        ]
        + [full(*context.shape) for context in contexts],
        out_specs=[
            full(rows, width),
            full(rows, width),
            full(groups, each, rows),
            full(groups, width // groups - each, rows),
        ]
        + [pl.BlockSpec(memory_space=pl.ANY)],
        out_shape=[
            jax.ShapeDtypeStruct((rows, width), BF16),
            jax.ShapeDtypeStruct((rows, width), F32),
            jax.ShapeDtypeStruct((groups, each, rows), BF16),
            jax.ShapeDtypeStruct((groups, width // groups - each, rows), BF16),
        ]
        + [jax.ShapeDtypeStruct((width, 3 * hidden + 2 * chunk), BF16)],
        scratch_shapes=[
            pltpu.VMEM((width, rows), BF16),
            pltpu.VMEM((rows, width), F32),
            pltpu.VMEM((rows, width), BF16),
            pltpu.VMEM((width, rows), BF16),
            pltpu.VMEM((rows, width), F32),
            pltpu.VMEM((rows, width), F32),
            pltpu.VMEM((width, width), BF16),
            pltpu.VMEM((chunk, chunk), BF16),
            pltpu.VMEM((2, width, 2 * chunk), BF16),
            pltpu.VMEM((2, width // steps, hidden), BF16),
            pltpu.SemaphoreType.DMA((2, 2)),
        ],
        compiler_params=pltpu.CompilerParams(vmem_limit_bytes=VMEM),
        cost_estimate=pl.CostEstimate(
            flops=18 * rows * width * hidden + 6 * rows * width * width,
            bytes_accessed=12 * width * hidden,
            transcendentals=rows * hidden,
        ),
        name="feed_forward",
    )(ints, tokens, late, gains, late, late, late, upstream, *contexts)


def weight_kernel(splits, normed_t, *refs):
    d_heads, outs, total = refs[: -splits - 1], refs[-splits - 1 : -1], refs[-1]
    step = pl.program_id(0)
    added = dot_nt(normed_t[...], jnp.concatenate([d_head[...] for d_head in d_heads], axis=0))

    @pl.when(step == 0)
    def _():
        total[...] = added

    @pl.when(step > 0)
    def _():
        total[...] += added

    @pl.when(step == pl.num_programs(0) - 1)
    def _():
        part = total.shape[0] // splits
        for other in range(splits):
            outs[other][...] = total[part * other : part * (other + 1), :].astype(BF16)


def weight_grads(splits, normed_t, d_heads):
    groups, rows, tokens = d_heads[0].shape
    width = normed_t.shape[0]
    out = (width // splits, rows * len(d_heads))
    return pl.pallas_call(
        functools.partial(weight_kernel, splits),
        grid=(groups,),
        in_specs=[pl.BlockSpec((width, tokens), lambda step: (0, step))]
        + [by_slot(rows, tokens)] * len(d_heads),
        out_specs=[pl.BlockSpec(out, lambda step: (0, 0))] * splits,
        out_shape=[jax.ShapeDtypeStruct(out, BF16)] * splits,
        scratch_shapes=[pltpu.VMEM((width, out[1]), F32)],
        compiler_params=pltpu.CompilerParams(vmem_limit_bytes=VMEM),
        cost_estimate=pl.CostEstimate(
            flops=2 * width * out[1] * groups * tokens,
            bytes_accessed=2 * width * groups * tokens,
            transcendentals=0,
        ),
        name="weight_grads",
    )(normed_t, *d_heads)


def added_kernel(count, *refs):
    held, outs = refs[:count], refs[count:]
    total = held[0][...].astype(F32)
    for piece in held[1:]:
        total += piece[...].astype(F32)
    part = total.shape[0] // len(outs)
    for index, out in enumerate(outs):
        out[...] = total[part * index : part * (index + 1)].astype(out.dtype)


def added(pieces, parts):
    rows, columns = pieces[0].shape
    return pl.pallas_call(
        functools.partial(added_kernel, len(pieces)),
        out_shape=[jax.ShapeDtypeStruct((rows // parts, columns), BF16)] * parts,
        compiler_params=pltpu.CompilerParams(vmem_limit_bytes=VMEM),
        cost_estimate=pl.CostEstimate(flops=0, bytes_accessed=2**20, transcendentals=0),
        name="added",
    )(*pieces)


def unpacked(pieces, heads, size):
    return jnp.concatenate(
        [
            piece[:, (3 * head + part) * size : (3 * head + part + 1) * size]
            for part in range(3)
            for piece in pieces
            for head in range(heads)
        ],
        axis=1,
    )


def count_kernel(groups, heads, size, count, down, ints, *refs):
    held, tables, grads = refs[:count], refs[count : count + heads], refs[count + heads]
    outs, counts = refs[count + heads + 1 : -1], refs[-1]
    total = held[0][...].astype(F32)
    for piece in held[1:]:
        total += piece[...].astype(F32)
    part = total.shape[0] // groups
    blank = jnp.zeros((part, counts.shape[1] - total.shape[1]), F32)
    for index, out in enumerate(outs):
        rows = total[part * index : part * (index + 1)]
        out[...] = jnp.concatenate([rows, blank], axis=1)
    squares = jnp.sum(total * total, axis=0, keepdims=True)
    table = jnp.concatenate(
        [jnp.sum(jnp.transpose(table[...]), axis=0, keepdims=True) for table in tables], axis=1
    )
    mine = [(ints[4] == g).astype(F32) for g in range(groups)]
    values = grads[...].astype(F32)
    values = values * values
    wide = values.shape[1] - down[0]
    piece = math.gcd(*down[1:3])
    across = down[2] // piece
    each = down[0] * piece // down[1]
    packed = []
    for part in range(across):
        rows = jnp.sum(values[piece * part : piece * (part + 1), wide:], axis=0, keepdims=True)
        packed.append(sum(rows[:, start : start + each] for start in range(0, down[0], each)))
    row = jnp.concatenate(
        [table * own for own in mine]
        + [unpacked([squares * own for own in mine], heads, size)]
        + [jnp.sum(values[:, : wide - down[3]], axis=0, keepdims=True)]
        + packed,
        axis=1,
    )
    counts[...] = jnp.zeros_like(counts)
    each = counts.shape[1]
    for start in range(0, row.shape[1], each):
        held_row = row[:, start : start + each]
        counts[start // each : start // each + 1, : held_row.shape[1]] = held_row


def counted(groups, heads, size, ints, pieces, tables, grads, down):
    rows, columns = pieces[0].shape
    buckets = tables[0].shape[0]
    length = groups * (heads * buckets + columns) + grads.shape[1] - down[0] - down[3]
    length += down[0] * down[2] // down[1]
    across = -(-columns // LANES) * LANES
    counts = -(-length // (8 * across)) * 8
    vmem = pl.BlockSpec(memory_space=pltpu.VMEM)
    return pl.pallas_call(
        functools.partial(count_kernel, groups, heads, size, len(pieces), down),
        in_specs=[smem()] + [vmem] * (len(pieces) + len(tables) + 1),
        out_shape=[jax.ShapeDtypeStruct((rows // groups, across), F32)] * groups
        + [jax.ShapeDtypeStruct((counts, across), F32)],
        compiler_params=pltpu.CompilerParams(vmem_limit_bytes=VMEM),
        cost_estimate=pl.CostEstimate(flops=0, bytes_accessed=2**20, transcendentals=0),
        name="counted",
    )(ints, *pieces, *tables, grads)


def input_kernel(heads, weights, own, gains, d_mixed, *refs):
    d_heads, (out, total) = refs[:heads], refs[heads:]
    step = pl.program_id(0)
    size = d_heads[0].shape[0] // 3
    blank = jnp.zeros((size, own.shape[0]), BF16)
    pieces = [d_head[size:, :] for d_head in d_heads]
    pieces += [d_head[:size, :] for d_head in d_heads] + [blank]
    added = dot_nn(weights[...], jnp.concatenate(pieces, axis=0))

    @pl.when(step == 0)
    def _():
        total[...] = added

    @pl.when(step > 0)
    def _():
        total[...] += added

    @pl.when(step == pl.num_programs(0) - 1)
    def _():
        back = rms_back(own[...].astype(F32), gains[0:1, :], jnp.transpose(total[...]))
        out[...] = (d_mixed[...] + back).astype(BF16)


def input_grads(groups, weights, own, gains, d_mixed, d_heads):
    tokens, width = own.shape
    full = lambda *shape: pl.BlockSpec(shape, lambda step: (0,) * len(shape))
    return pl.pallas_call(
        functools.partial(input_kernel, len(d_heads)),
        grid=(groups,),
        in_specs=[
            pl.BlockSpec((width, weights.shape[1] // groups), lambda step: (0, step)),
            full(tokens, width),
            full(8, width),
            full(tokens, width),
        ]
        + [by_slot(*d_heads[0].shape[1:])] * len(d_heads),
        out_specs=full(tokens, width),
        out_shape=jax.ShapeDtypeStruct((tokens, width), BF16),
        scratch_shapes=[pltpu.VMEM((width, tokens), F32)],
        compiler_params=pltpu.CompilerParams(vmem_limit_bytes=VMEM),
        name="input_grads",
    )(weights, own, gains, d_mixed, *d_heads)


def by_slot(rows, tokens):
    return pl.BlockSpec((None, rows, tokens), lambda slot: (slot, 0, 0))


def smem():
    return pl.BlockSpec(memory_space=pltpu.SMEM)


def attend(head, tokens, groups, splits, ints, table, query, kvs):
    seq, rows = tokens * groups * splits, tokens * groups
    half = LANES // 2
    whole = pl.BlockSpec((rows, LANES), lambda slot: (0, head))
    return pl.pallas_call(
        functools.partial(forward_kernel, tokens, groups, splits),
        grid=(groups,),
        in_specs=[smem(), smem(), pl.BlockSpec((tokens, LANES), lambda slot: (slot, head))]
        + [whole] * splits,
        out_specs=[
            pl.BlockSpec((seq, tokens), lambda slot: (slot, 0)),
            by_slot(half, tokens),
            by_slot(half + 16, tokens),
        ],
        out_shape=[
            jax.ShapeDtypeStruct((groups * seq, tokens), BF16),
            jax.ShapeDtypeStruct((groups, half, tokens), BF16),
            jax.ShapeDtypeStruct((groups, half + 16, tokens), F32),
        ],
        scratch_shapes=[
            pltpu.VMEM((seq + 2 * LANES, LANES), BF16),
            pltpu.VMEM((half + 16, seq + 2 * LANES), BF16),
            pltpu.VMEM((tokens + 2 * LANES, tokens), F32),
            pltpu.VMEM((3, LANES, LANES), F32),
            pltpu.VMEM((8, tokens), F32),
        ],
        compiler_params=pltpu.CompilerParams(vmem_limit_bytes=VMEM),
        cost_estimate=pl.CostEstimate(
            flops=16 * seq * rows * half, bytes_accessed=2 * seq * rows, transcendentals=seq * rows
        ),
        name="attend",
    )(ints, table, query, *kvs)


def attend_back(
    head, tokens, groups, splits, ints, buckets, query, d_context, place, stats, probs, kvs
):
    seq, rows = tokens * groups * splits, tokens * groups
    half = LANES // 2
    whole = pl.BlockSpec((rows, LANES), lambda slot: (0, head))
    kept = pl.BlockSpec((groups, LANES, tokens), lambda slot: (0, 0, 0))
    return pl.pallas_call(
        functools.partial(backward_kernel, tokens, groups, splits),
        grid=(groups,),
        in_specs=[
            smem(),
            pl.BlockSpec((tokens, LANES), lambda slot: (slot, head)),
            pl.BlockSpec((None, None, half, tokens), lambda slot: (slot, place, 0, 0)),
            by_slot(half + 16, tokens),
            pl.BlockSpec((seq, tokens), lambda slot: (slot, 0)),
        ]
        + [whole] * splits,
        out_specs=[pl.BlockSpec((groups, half + LANES, tokens), lambda slot: (0, 0, 0))]
        + [kept] * (splits - 1)
        + [pl.BlockSpec((buckets, LANES), lambda slot: (0, 0))],
        out_shape=[jax.ShapeDtypeStruct((groups, half + LANES, tokens), BF16)]
        + [jax.ShapeDtypeStruct((groups, LANES, tokens), BF16)] * (splits - 1)
        + [jax.ShapeDtypeStruct((buckets, LANES), F32)],
        scratch_shapes=[
            pltpu.VMEM((seq + 2 * LANES, LANES), BF16),
            pltpu.VMEM((half + 16, seq + 2 * LANES), BF16),
            pltpu.VMEM((seq + 2 * LANES, LANES), F32),
            pltpu.VMEM((3, LANES, LANES), F32),
            pltpu.VMEM((2, 8, tokens), F32),
            pltpu.VMEM((half + 16, tokens), F32),
        ],
        compiler_params=pltpu.CompilerParams(vmem_limit_bytes=VMEM),
        cost_estimate=pl.CostEstimate(
            flops=32 * seq * rows * half, bytes_accessed=2 * seq * rows, transcendentals=0
        ),
        name="attend_back",
    )(ints, query, d_context, stats, probs, *kvs)


def factored(grad_shard, column_total, row_old, column_old, row_total):
    columns = grad_shard.shape[1]
    mean_square = jnp.sum(column_total) / (row_total * columns) + EPSILON
    row_new = (
        DECAY_RATE * row_old
        + (1.0 - DECAY_RATE) * (jnp.sum(grad_shard * grad_shard, axis=1) / columns) / mean_square
    )
    column_new = (
        DECAY_RATE * column_old + (1.0 - DECAY_RATE) * (column_total / row_total) / mean_square
    )
    return (row_new, column_new)


def shards(
    tokens,
    lengths,
    norm_one,
    w_qkv,
    rel_table,
    w_out,
    norm_two,
    w_gateup,
    w_down,
    cotangent,
    row_qkv,
    col_qkv,
    row_out,
    col_out,
    row_gateup,
    col_gateup,
    row_down,
    col_down,
):
    own = tokens[0]
    tok_rows, width = own.shape
    heads = rel_table.shape[1]
    buckets = rel_table.shape[0]
    rows_apart, groups, splits = (lax.axis_size(name) for name in ALL)
    group_heads = heads // groups
    head_size = width // heads
    group, split = lax.axis_index("group"), lax.axis_index("split")
    group_width = width // groups

    def ahead(array, axis, by):
        size = lax.axis_size(axis)
        return lax.ppermute(array, axis, [((i + by) % size, i) for i in range(size)])

    def swap_groups(array):
        return lax.all_to_all(array, "group", 0, 0)

    def swap_rows(array):
        return lax.all_to_all(array, "batch", 0, 0)

    def line(array, by):
        pairs = [(i, i + by) for i in range(groups) if 0 <= i + by < groups]
        return lax.ppermute(array, "group", pairs)

    before, behind = [own], [own]
    for _ in range(groups - 1):
        before.append(line(before[-1], 1))
        behind.append(line(behind[-1], -1))

    unit = w_qkv.shape[0]
    by_part = w_qkv.reshape(unit, 3, groups, group_heads, head_size)
    gains = jnp.pad(jnp.stack([norm_one, norm_two], axis=1), ((0, 0), (0, head_size - 2)))
    packed = jnp.concatenate(
        [
            jnp.concatenate([by_part[:, 1], by_part[:, 2]], axis=-1).reshape(unit, groups, -1),
            by_part[:, 0].reshape(unit, groups, -1),
            jnp.broadcast_to(gains[:, None], (unit, groups, head_size)),
        ],
        axis=2,
    )
    early = lax.all_gather(packed.reshape(unit, -1), ALL, axis=0, tiled=True)
    together = math.gcd(unit, w_down.shape[0])
    packed_down = w_down.reshape(w_down.shape[0] // together, together, unit // together, -1)
    packed_down = jnp.transpose(packed_down, (2, 1, 0, 3)).reshape(unit, -1)
    late = lax.all_gather(
        after(jnp.concatenate([packed_down, w_gateup, w_out], axis=1), before[1], behind[1]),
        ALL,
        axis=0,
        tiled=True,
    )

    dims = (rows_apart, groups, splits)
    far = jnp.where(group == 0, groups - 1, jnp.where(group == groups - 1, 0, group))
    ends = jnp.cumsum(lengths[0])
    ints = jnp.concatenate(
        [
            split.astype(jnp.int32)[None],
            ends.astype(jnp.int32),
            jnp.stack([group, lax.axis_index("batch"), far]).astype(jnp.int32),
        ]
    )
    *blocks, gains, order = project(dims, ints, early, own, before[1:-1] + behind[1:-1])
    normed_t, query, kv = project_last(
        dims, ints, early, own, before[-1], behind[-1], order, gains, *blocks
    )
    kvs = [kv] + [ahead(kv, "split", other) for other in range(1, splits)]

    table_own = lax.dynamic_slice_in_dim(rel_table.T, group * group_heads, group_heads, 0)

    contexts, moved, stats, probs = [], [], [], []
    for head in range(group_heads):
        prob, context, stat = attend(
            head,
            tok_rows,
            groups,
            splits,
            after(ints, *contexts[-1:]),
            table_own[head : head + 1],
            query,
            kvs,
        )
        contexts.append(context)
        moved.append(swap_groups(after(context, *moved[-1:])))
        stats.append(stat)
        probs.append(prob)

    outs = feed_forward(
        dims, ints, own, moved, gains, late, cotangent[0]
    )
    result, d_mixed, d_first, d_rest, held = outs

    d_first = swap_groups(d_first)
    d_rest = swap_groups(d_rest)
    d_contexts = [d_first[:, None], d_rest.reshape(groups, group_heads - 1, head_size, tok_rows)]
    row_sum = lax.psum_scatter(held, ("batch", "split"), scatter_dimension=0, tiled=True)
    row_sum = after(row_sum)
    grads_own = lax.psum_scatter(row_sum, "group", scatter_dimension=0, tiled=True)

    d_heads, d_received, d_tables = [], [], []
    ready = [(), ()] + [(row_sum,)] * (group_heads - 2)
    for head in range(group_heads):
        outs = attend_back(
            head,
            tok_rows,
            groups,
            splits,
            ints,
            buckets,
            query,
            after(d_contexts[int(head > 0)], *ready[head], *d_heads[-1:]),
            head - int(head > 0),
            stats[head],
            probs[head],
            kvs,
        )
        beside = d_received[-1] if head else d_contexts[1]
        if head < group_heads - 1:
            outs = lax.optimization_barrier((*outs, beside))[:-1]
        d_head = outs[0].astype(F32)
        for other in range(1, splits):
            d_kv = ahead(outs[other], "split", splits - other).astype(F32)
            d_head = d_head + jnp.pad(d_kv, ((0, 0), (head_size, 0), (0, 0)))
        d_head = d_head.astype(BF16)
        if head == group_heads - 1:
            d_head = after(d_head, beside)
        d_heads.append(d_head)
        d_received.append(swap_groups(d_head))
        d_tables.append(outs[-1])

    down_shape = (w_down.shape[0] * width // unit, w_down.shape[0], unit)
    down_start = grads_own.shape[1] - down_shape[0]
    down_shape += (down_start - w_gateup.shape[1] - width,)
    grads = weight_grads(splits, normed_t, d_heads)
    held = added(
        [grads[0]] + [ahead(grads[by], "split", splits - by) for by in range(1, splits)], rows_apart
    )
    held = [held[0]] + [ahead(held[by], "batch", rows_apart - by) for by in range(1, rows_apart)]
    held[0] = after(held[0], d_received[-1])
    *columns, counts = counted(
        groups, group_heads, head_size, ints, held, d_tables, grads_own, down_shape
    )
    d_received[-1] = after(d_received[-1], counts)
    d_inputs = input_grads(groups, early, own, gains, d_mixed, d_received)
    counts = sum([ahead(counts, "batch", by) for by in range(1, rows_apart)], counts)
    counts = after(counts, d_inputs)
    counts_rows = counts.shape[0]
    travelled = [jnp.concatenate([counts, columns[0]], axis=0)] + [
        ahead(jnp.concatenate([counts, columns[by]], axis=0), "group", groups - by)
        for by in range(1, groups)
    ]
    columns = [both[counts_rows:] for both in travelled]
    counts = sum([both[:counts_rows] for both in travelled[1:]], travelled[0][:counts_rows])
    counts = sum([ahead(counts, "split", by) for by in range(1, splits)], counts)
    pieces = []
    for index in range(groups):
        piece = columns[0]
        for by in range(1, groups):
            piece = jnp.where((group + groups - by) % groups == index, columns[by], piece)
        pieces.append(piece)
    shard_qkv = unpacked(pieces, group_heads, head_size)
    steps = w_down.shape[0] * rows_apart * groups * splits // (2 * TILE)

    def in_order(array):
        array = array.reshape(*array.shape[:-1], steps, 2, -1)
        return jnp.swapaxes(array, -3, -2).reshape(*array.shape[:-3], -1)

    shard_rest = grads_own.astype(F32)
    shard_gateup = in_order(shard_rest[:, : w_gateup.shape[1]])
    shard_out = shard_rest[:, w_gateup.shape[1] :][:, :width]
    shard_down = shard_rest[:, down_start:].reshape(
        unit // together, together, w_down.shape[0] // together, -1
    )
    shard_down = jnp.transpose(shard_down, (2, 1, 0, 3)).reshape(-1, width)
    summed = counts.reshape(-1)
    sizes = (heads * buckets, 3 * width, w_gateup.shape[1], width, width)
    table_total, column_qkv, column_gateup, column_out, column_down, _ = jnp.split(
        summed, [sum(sizes[: i + 1]) for i in range(len(sizes))]
    )
    table_total = table_total.reshape(heads, buckets)
    column_gateup = in_order(column_gateup)
    shard_gain_one = jnp.sum(w_qkv.astype(F32) * shard_qkv, axis=1) / norm_one.astype(F32)
    shard_gain_two = jnp.sum(w_gateup.astype(F32) * shard_gateup, axis=1) / norm_two.astype(F32)
    new_row_qkv, new_col_qkv = factored(shard_qkv, column_qkv, row_qkv, col_qkv, width)
    new_row_out, new_col_out = factored(shard_out, column_out, row_out, col_out, width)
    new_row_gateup, new_col_gateup = factored(
        shard_gateup, column_gateup, row_gateup, col_gateup, width
    )
    new_row_down, new_col_down = factored(
        shard_down, column_down, row_down, col_down, w_down.shape[0] * rows_apart * groups * splits
    )
    return (
        result[None],
        d_inputs[None],
        shard_gain_one,
        shard_qkv,
        table_total.T,
        shard_out,
        shard_gain_two,
        shard_gateup,
        shard_down,
        new_row_qkv,
        new_col_qkv,
        new_row_out,
        new_col_out,
        new_row_gateup,
        new_col_gateup,
        new_row_down,
        new_col_down,
    )


def solution(mesh):
    row_blocks = P("batch", ("group", "split"), None)
    split_rows = P(ALL, None)
    split_row = P(ALL)

    def run(*arrays):
        rows, ring = mesh.devices.shape
        groups = math.gcd(ring, arrays[4].shape[1])
        fine = Mesh(mesh.devices.reshape(rows, groups, ring // groups), ALL)
        return jax.shard_map(
            shards,
            mesh=fine,
            in_specs=(
                row_blocks,
                P("batch", None),
                split_row,
                split_rows,
                P(),
                split_rows,
                split_row,
                split_rows,
                split_rows,
                row_blocks,
            )
            + (split_row, P()) * 4,
            out_specs=(
                row_blocks,
                row_blocks,
                split_row,
                split_rows,
                P(),
                split_rows,
                split_row,
                split_rows,
                split_rows,
            )
            + (split_row, P()) * 4,
            check_vma=False,
        )(*arrays)

    return run
```

```python
import functools
import math

import jax
import jax.numpy as jnp
from jax import lax
from jax.experimental import pallas as pl
from jax.experimental.pallas import tpu as pltpu
from jax.sharding import Mesh
from jax.sharding import PartitionSpec as P

THRESHOLDS = (12, 16, 23, 32, 46, 64, 91)
EPSILON = 1e-06
DECAY_RATE = 0.5
GELU_SCALE = 0.7978845608028654
MASKED = -1e9
LEEWAY = 20.0
ALL = ("batch", "group", "split")
LANES = 128
TILE = 256
GROUP = 4
VMEM = 60 * 2**20
F32 = jnp.float32
BF16 = jnp.bfloat16


def bucket_of(offset):
    distance = jnp.abs(offset)
    steps_up = 8 + sum(((distance >= limit).astype(jnp.int32) for limit in THRESHOLDS))
    within = jnp.where(distance < 8, distance, steps_up)
    return within + 16 * (offset > 0).astype(jnp.int32)


def after(value, *others):
    return lax.optimization_barrier((value, *others))[0]


def rms_scale(values, gain):
    return values * lax.rsqrt(jnp.mean(values * values, axis=-1, keepdims=True) + EPSILON) * gain


def rms_back(values, gain, grad):
    scale = lax.rsqrt(jnp.mean(values * values, axis=-1, keepdims=True) + EPSILON)
    scaled = grad * gain
    return scale * scaled - values * scale**3 * jnp.mean(scaled * values, axis=-1, keepdims=True)


def dot_nn(left, right):
    return jnp.dot(left, right, preferred_element_type=F32)


def dot_nt(left, right):
    return lax.dot_general(left, right, (((1,), (1,)), ((), ())), preferred_element_type=F32)


def dot_tt(left, right):
    return lax.dot_general(left, right, (((0,), (1,)), ((), ())), preferred_element_type=F32)


class Layout:
    def __init__(self, tokens, groups, splits, ints):
        self.tokens, self.groups, self.splits = tokens, groups, splits
        self.blocks = groups * splits
        self.seq = tokens * self.blocks
        self.near = tokens + 2 * LANES
        self.subs = tokens // LANES
        self.split = ints[0]
        self.ends = (ints[1], ints[2], ints[3])
        slot = pl.program_id(0)
        self.block = self.block_of(slot, 0)
        self.first = pl.multiple_of(self.block * tokens, LANES)
        self.lefts = jnp.maximum(0, self.block * (tokens // TILE) - 1)
        self.loops = (self.seq // TILE - 2 - tokens // TILE) // GROUP
        self.edge = jnp.logical_or(self.block == 0, self.block == self.blocks - 1)

    def block_of(self, slot, other):
        return slot * self.splits + lax.rem(self.split + other, self.splits)

    def keys_of(self, tile):
        before = 2 * LANES + TILE * tile
        after = self.first + self.near + TILE * (tile - self.lefts)
        return pl.ds(pl.multiple_of(jnp.where(tile < self.lefts, before, after), LANES), TILE)

    def rows_of(self, tile):
        return pl.ds(pl.multiple_of(self.near + TILE * tile, LANES), TILE)

    def segment(self, positions):
        return sum((positions >= end).astype(jnp.int32) for end in self.ends)


def iota(shape, dim):
    return lax.broadcasted_iota(jnp.int32, shape, dim)


def fold(values):
    return values.reshape(values.shape[0] // 8, 8, values.shape[1])


def forward_kernel(tokens, groups, splits, ints, table, query, *refs):
    kvs, (probs, context, stats, k_aug, v_t, scores, biases, best) = refs[:splits], refs[splits:]
    lay = Layout(tokens, groups, splits, ints)
    half = query.shape[1] // 2
    buckets = table.shape[1]

    @pl.when(pl.program_id(0) == 0)
    def prepare():
        lane = iota((tokens, LANES), 1)
        for slot in range(groups):
            for other in range(splits):
                start = lay.block_of(slot, other) * tokens
                rows = pl.ds(pl.multiple_of(LANES + start, LANES), tokens)
                kv = kvs[other][slot * tokens : (slot + 1) * tokens, :].astype(F32)
                seg = lay.segment(start + iota((tokens, LANES), 0))
                k_aug[rows, :] = jnp.where(lane < half, kv, (lane - half == seg).astype(F32)).astype(BF16)
                turned = jnp.transpose(kv)
                ones = (iota((16, tokens), 0) == 0).astype(F32)
                v_t[:, rows] = jnp.concatenate([turned[half:], ones], axis=0).astype(BF16)
        outside = (iota((LANES, LANES), 1) == half + 3).astype(BF16)
        for start in (0, lay.seq + LANES):
            k_aug[start : start + LANES, :] = outside
            v_t[:, start : start + LANES] = jnp.zeros((half + 16, LANES), BF16)
        for place in range(3):
            bucket = bucket_of(
                LANES * (place - 1) + iota((LANES, LANES), 0) - iota((LANES, LANES), 1)
            )
            bias = jnp.zeros((LANES, LANES), F32)
            for label in range(buckets):
                bias = jnp.where(bucket == label, table[0, label], bias)
            biases[place] = bias

    far_left, far_right = table[0, buckets // 2 - 1], table[0, buckets - 1]
    positions = lay.block * tokens + iota((1, tokens), 1)
    seg_q = lay.segment(positions)
    row = iota((2 * half, tokens), 0)
    apart = jnp.logical_or(row - half != seg_q, row == half + 3)
    q_aug = jnp.where(
        row < half, jnp.transpose(query[...].astype(F32)), jnp.where(apart, MASKED, 0.0)
    ).astype(BF16)

    near = dot_nn(k_aug[pl.ds(lay.first, lay.near), :], q_aug)
    eye = iota((LANES, LANES), 0) == iota((LANES, LANES), 1)
    for sub_q in range(lay.subs):
        lanes = slice(LANES * sub_q, LANES * (sub_q + 1))
        top = None
        for sub_k in range(lay.subs + 2):
            rows = slice(LANES * sub_k, LANES * (sub_k + 1))
            place = sub_k - sub_q
            piece = near[rows, lanes] + (
                far_left if place < 0 else far_right if place > 2 else biases[place]
            )
            if place == 1:
                alone = jnp.logical_and(eye, positions[:, lanes] >= lay.ends[2])
                piece = jnp.where(alone, 0.0, piece)
            scores[rows, lanes] = piece
            high = jnp.max(fold(piece), axis=0)
            top = high if top is None else jnp.maximum(top, high)
        best[:, lanes] = top

    def sweep(peak):
        weights = jnp.exp(scores[...] - peak).astype(BF16)
        probs[: lay.near, :] = weights
        stats[...] = dot_nn(v_t[:, pl.ds(lay.first, lay.near)], weights)
        left_peak, right_peak = peak - far_left, peak - far_right

        def tiles(index, count):
            places = [lay.keys_of(index + step) for step in range(count)]
            piece = dot_nn(jnp.concatenate([k_aug[keys, :] for keys in places], axis=0), q_aug)
            parts, top = [], best[...]
            for step in range(count):
                score = piece[TILE * step : TILE * (step + 1)]
                is_left = index + step < lay.lefts
                top = jnp.maximum(
                    top,
                    jnp.max(fold(score), axis=0) + jnp.where(is_left, far_left, far_right),
                )
                part = jnp.exp(score - jnp.where(is_left, left_peak, right_peak)).astype(BF16)
                probs[lay.rows_of(index + step), :] = part
                parts.append(part)
            best[...] = top
            values = jnp.concatenate([v_t[:, keys] for keys in places], axis=1)
            stats[...] += dot_nn(values, jnp.concatenate(parts, axis=0))

        if lay.loops <= 3:
            for index in range(lay.loops):
                tiles(index * GROUP, GROUP)
        else:

            def group(index, carry):
                tiles(index * GROUP, GROUP)
                return carry

            lax.fori_loop(0, lay.loops, group, 0)

        @pl.when(lay.edge)
        def _():
            tiles(lay.loops * GROUP, 1)

    peak = jnp.max(best[...], axis=0, keepdims=True)
    sweep(peak)
    true_peak = jnp.max(best[...], axis=0, keepdims=True)

    @pl.when(jnp.max(true_peak - peak) > LEEWAY)
    def _():
        sweep(true_peak)

    inverse = 1.0 / stats[half : half + 1, :]
    result = stats[:half, :] * inverse
    context[...] = result.astype(BF16)
    stats[:half, :] = result
    stats[half : half + 1, :] = inverse


def backward_kernel(tokens, groups, splits, ints, query, d_context, stats, probs, *refs):
    kvs, d_kvs = refs[:splits], refs[splits : 2 * splits]
    d_table, v_aug, k_t, d_kv, bands, sides, d_q = refs[2 * splits :]
    lay = Layout(tokens, groups, splits, ints)
    half = query.shape[1] // 2
    buckets = d_table.shape[0]

    @pl.when(pl.program_id(0) == 0)
    def prepare():
        lane = iota((tokens, LANES), 1)
        for slot in range(groups):
            for other in range(splits):
                start = lay.block_of(slot, other) * tokens
                rows = pl.ds(pl.multiple_of(LANES + start, LANES), tokens)
                kv = kvs[other][slot * tokens : (slot + 1) * tokens, :].astype(F32)
                v_aug[rows, :] = jnp.where(lane >= half, kv, (lane < 3).astype(F32)).astype(BF16)
                ones = (iota((16, tokens), 0) == 0).astype(F32)
                k_t[:, rows] = jnp.concatenate([jnp.transpose(kv)[:half], ones], axis=0).astype(BF16)
        for start in (0, lay.seq + LANES):
            v_aug[start : start + LANES, :] = jnp.zeros((LANES, LANES), BF16)
            k_t[:, start : start + LANES] = jnp.zeros((half + 16, LANES), BF16)
        d_kv[...] = jnp.zeros_like(d_kv)
        bands[...] = jnp.zeros_like(bands)
        sides[...] = jnp.zeros_like(sides)

    inverse = stats[half : half + 1, :]
    upstream = d_context[...].astype(F32)
    delta = jnp.sum(upstream * stats[:half, :], axis=0, keepdims=True) * inverse
    scaled = upstream * inverse
    high = delta.astype(BF16).astype(F32)
    middle = (delta - high).astype(BF16).astype(F32)
    low = delta - high - middle
    row = iota((half, tokens), 0)
    shift = jnp.where(row == 0, high, jnp.where(row == 1, middle, jnp.where(row == 2, low, 0.0)))
    up_aug = jnp.concatenate([-shift, scaled], axis=0).astype(BF16)
    up_rows = jnp.transpose(jnp.concatenate([jnp.zeros_like(scaled), scaled], axis=0)).astype(BF16)
    both = jnp.concatenate([query[...], up_rows], axis=0)

    def grads(keys, rows):
        part = jnp.concatenate([probs[where, :] for where in rows], axis=0)
        values = jnp.concatenate([v_aug[where, :] for where in keys], axis=0)
        d_scores = part.astype(F32) * dot_nn(values, up_aug)
        rounded = d_scores.astype(BF16)
        added = dot_nn(jnp.concatenate([rounded, part], axis=1), both)
        size = part.shape[0] // len(keys)
        for index, where in enumerate(keys):
            d_kv[where, :] += added[size * index : size * (index + 1)]
        return d_scores, rounded

    near, rounded = grads([pl.ds(lay.first, lay.near)], [pl.ds(0, lay.near)])
    total = dot_nn(k_t[:, pl.ds(lay.first, lay.near)], rounded)
    for sub_q in range(lay.subs):
        lanes = slice(LANES * sub_q, LANES * (sub_q + 1))
        for sub_k in range(lay.subs + 2):
            piece = near[LANES * sub_k : LANES * (sub_k + 1), lanes]
            place = sub_k - sub_q
            if 0 <= place <= 2:
                bands[place] += piece
            else:
                sides[int(place > 2), :, lanes] += jnp.sum(fold(piece), axis=0)
    d_q[...] = total
    near_sum = total[half : half + 8, :]

    def far(index, count):
        places = [lay.keys_of(index + step) for step in range(count)]
        rounded = grads(places, [lay.rows_of(index + step) for step in range(count)])[1]
        keys = jnp.concatenate([k_t[:, where] for where in places], axis=1)
        lefts = jnp.clip(lay.lefts - index, 0, count) * TILE
        row = iota(keys.shape, 0)
        side = jnp.logical_and(row == half + 8, iota(keys.shape, 1) < lefts)
        keys = jnp.where(side, 1.0, keys.astype(F32)).astype(BF16)
        d_q[...] += dot_nn(keys, rounded)

    if lay.loops <= 3:
        for index in range(lay.loops):
            far(index * GROUP, GROUP)
    else:

        def group(index, carry):
            far(index * GROUP, GROUP)
            return carry

        lax.fori_loop(0, lay.loops, group, 0)

    @pl.when(lay.edge)
    def _():
        far(lay.loops * GROUP, 1)

    left_sum = d_q[half + 8 : half + 16, :]
    sides[0] += left_sum
    sides[1] += d_q[half : half + 8, :] - near_sum - left_sum
    d_kvs[0][pl.program_id(0), :half, :] = d_q[:half, :].astype(BF16)

    @pl.when(pl.program_id(0) == groups - 1)
    def finish():
        for slot in range(groups):
            for other in range(splits):
                start = lay.block_of(slot, other) * tokens
                rows = pl.ds(pl.multiple_of(LANES + start, LANES), tokens)
                turned = jnp.transpose(d_kv[rows, :]).astype(BF16)
                if other:
                    d_kvs[other][slot] = turned
                else:
                    d_kvs[0][slot, half:, :] = turned
        labels = [
            bucket_of(LANES * (place - 1) + iota((LANES, LANES), 0) - iota((LANES, LANES), 1))
            for place in range(3)
        ]
        for label in range(buckets):
            found = jnp.zeros((8, LANES), F32)
            for place in range(3):
                kept = jnp.where(labels[place] == label, bands[place], 0.0)
                found += jnp.sum(fold(kept), axis=0)
            if label in (buckets // 2 - 1, buckets - 1):
                side = sides[int(label == buckets - 1)]
                for sub in range(lay.subs):
                    found += side[:, LANES * sub : LANES * (sub + 1)]
            d_table[label : label + 1, :] = jnp.sum(found, axis=0, keepdims=True)


def chosen(shape, source):
    return (source(iota((shape[0], 1), 0)) == iota(shape, 1)).astype(F32).astype(BF16)


def project_block(values, weights, gains, order, normed_t, query, kv):
    normed = rms_scale(values.astype(F32), gains[0:1, :]).astype(BF16)
    normed_t[...] = dot_nt(order[...], normed).astype(BF16)
    both = dot_nn(normed, weights[...])
    narrow = kv.shape[1]
    kv[...] = both[:, :narrow].astype(BF16)
    size = LANES // 2
    blank = jnp.zeros((both.shape[0], size), F32)
    parts = []
    for start in range(narrow, narrow + narrow // 2, size):
        parts += [both[:, start : start + size], blank]
    query[...] = jnp.concatenate(parts, axis=1).astype(BF16)


def project_kernel(dims, ints, weights, own, *refs):
    rows_apart, groups, splits = dims
    others, (normed_t, query, kv, gains, order, values) = refs[:-6], refs[-6:]
    slot, split, group, batch = pl.program_id(0), ints[0], ints[4], ints[5]
    width, narrow = own.shape[1], kv.shape[1]
    unit = width // (rows_apart * groups * splits)

    @pl.when(slot == 0)
    def _():
        def source(index):
            within = lax.rem(index, unit)
            index = index // unit
            g = lax.rem(group + lax.rem(index, groups), groups)
            index = index // groups
            b = lax.rem(batch + lax.rem(index, rows_apart), rows_apart)
            r = lax.rem(split + index // rows_apart, splits)
            return ((b * groups + g) * splits + r) * unit + within

        order[...] = chosen((width, width), source)
        turned = jnp.transpose(weights[:, weights.shape[1] - LANES :].astype(F32))
        gains[...] = turned[LANES // 2 : LANES // 2 + 8]

    @pl.when(slot == group)
    def _():
        values[...] = own[...]

    for by in range(1, groups - 1):

        @pl.when(slot == group - by)
        def _():
            values[...] = others[by - 1][...]

        @pl.when(slot == group + by)
        def _():
            values[...] = others[groups + by - 3][...]

    @pl.when(jnp.abs(slot - group) < groups - 1)
    def _():
        project_block(values[...], weights, gains, order, normed_t, query, kv)


def project(dims, ints, weights, own, others):
    tokens, width = own.shape
    groups = dims[1]
    narrow = 2 * width // groups
    whole = pl.BlockSpec((tokens, width), lambda slot, ints: (0, 0))
    by_row = pl.BlockSpec((tokens, narrow), lambda slot, ints: (slot, 0))
    return pl.pallas_call(
        functools.partial(project_kernel, dims),
        grid_spec=pltpu.PrefetchScalarGridSpec(
            num_scalar_prefetch=1,
            grid=(groups,),
            in_specs=[pl.BlockSpec((width, weights.shape[1] // groups), lambda slot, ints: (0, ints[4]))]
            + [whole] * (1 + len(others)),
            out_specs=[
                pl.BlockSpec((width, tokens), lambda slot, ints: (0, slot)),
                by_row,
                by_row,
                pl.BlockSpec((8, width), lambda slot, ints: (0, 0)),
                pl.BlockSpec((width, width), lambda slot, ints: (0, 0)),
            ],
            scratch_shapes=[pltpu.VMEM((tokens, width), BF16)],
        ),
        out_shape=[
            jax.ShapeDtypeStruct((width, groups * tokens), BF16),
            jax.ShapeDtypeStruct((groups * tokens, narrow), BF16),
            jax.ShapeDtypeStruct((groups * tokens, narrow), BF16),
            jax.ShapeDtypeStruct((8, width), F32),
            jax.ShapeDtypeStruct((width, width), BF16),
        ],
        compiler_params=pltpu.CompilerParams(vmem_limit_bytes=VMEM),
        cost_estimate=pl.CostEstimate(
            flops=4 * groups * tokens * width * width,
            bytes_accessed=8 * groups * tokens * width,
            transcendentals=0,
        ),
        name="project",
    )(ints, weights, own, *others)


def project_last_kernel(groups, ints, weights, own, before, behind, order, gains, *refs):
    normed_t, query, kv, values = refs[3:]
    group = ints[4]
    values[...] = own[...]

    @pl.when(group == 0)
    def _():
        values[...] = behind[...]

    @pl.when(group == groups - 1)
    def _():
        values[...] = before[...]

    project_block(values[...], weights, gains, order, normed_t, query, kv)


def project_last(dims, ints, weights, own, before, behind, order, gains, normed_t, query, kv):
    tokens, width = own.shape
    narrow = kv.shape[1]
    whole = lambda array: pl.BlockSpec(array.shape, lambda step, ints: (0, 0))
    by_row = pl.BlockSpec((tokens, narrow), lambda step, ints: (ints[6], 0))
    return pl.pallas_call(
        functools.partial(project_last_kernel, dims[1]),
        grid_spec=pltpu.PrefetchScalarGridSpec(
            num_scalar_prefetch=1,
            grid=(1,),
            in_specs=[
                pl.BlockSpec((width, weights.shape[1] // dims[1]), lambda step, ints: (0, ints[4]))
            ]
            + [whole(array) for array in (own, before, behind, order, gains)]
            + [pl.BlockSpec(memory_space=pl.ANY)] * 3,
            out_specs=[
                pl.BlockSpec((width, tokens), lambda step, ints: (0, ints[6])),
                by_row,
                by_row,
            ],
            scratch_shapes=[pltpu.VMEM((tokens, width), BF16)],
        ),
        out_shape=[jax.ShapeDtypeStruct(x.shape, x.dtype) for x in (normed_t, query, kv)],
        input_output_aliases={7: 0, 8: 1, 9: 2},
        compiler_params=pltpu.CompilerParams(vmem_limit_bytes=VMEM),
        cost_estimate=pl.CostEstimate(
            flops=4 * tokens * width * width, bytes_accessed=8 * tokens * width, transcendentals=0
        ),
        name="project_last",
    )(ints, weights, own, before, behind, order, gains, normed_t, query, kv)


def scatter_order(groups, splits, unit):
    def source(index):
        within = index % unit
        index = index // unit
        g = index % groups
        index = index // groups
        return ((index // splits * groups + g) * splits + index % splits) * unit + within

    return source


def reordered(values, source, unit):
    return jnp.concatenate(
        [
            values[source(start) : source(start) + unit]
            for start in range(0, values.shape[0], unit)
        ],
        axis=0,
    )


def packed_rows(values, tall, low):
    piece = math.gcd(tall, low)
    across, down = low // piece, tall // piece
    wide = values.shape[1] // across
    rows = []
    for start in range(0, values.shape[0], tall):
        for part in range(across):
            columns = slice(wide * part, wide * (part + 1))
            rows.append(
                jnp.concatenate(
                    [
                        values[start + piece * i : start + piece * (i + 1), columns]
                        for i in range(down)
                    ],
                    axis=1,
                )
            )
    return jnp.concatenate(rows, axis=0)


def unpacked_rows(values, tall, low, columns):
    piece = math.gcd(tall, low)
    across, down = low // piece, tall // piece
    wide = columns // across
    rows = []
    for start in range(0, values.shape[0], low):
        for index in range(down):
            lanes = slice(wide * index, wide * (index + 1))
            rows.append(
                jnp.concatenate(
                    [
                        values[start + piece * part : start + piece * (part + 1), lanes]
                        for part in range(across)
                    ],
                    axis=1,
                )
            )
    return jnp.concatenate(rows, axis=0)


def block_kernel(
    dims, heads, ints, tokens, w_out, gains, w_gate, w_up, w_packed, upstream, *refs
):
    rows_apart, groups, splits = dims
    contexts, refs = refs[:heads], refs[heads:]
    result, d_mixed, d_first, d_rest, grads = refs[:5]
    (context_t, mixed, normed, normed_t, d_normed, total, order) = refs[5:12]
    wide, down, sems = refs[12:]
    step, chunks = pl.program_id(0), pl.num_programs(0) - 1
    width, chunk = w_gate.shape
    devices = rows_apart * groups * splits
    hidden_unit = chunk * chunks // devices
    gain = gains[1:2, :]
    unit = width // devices
    for_rows = scatter_order(groups, splits, unit)
    for_hidden = scatter_order(groups, splits, hidden_unit)
    whole_rows = unit % 8 == 0

    @pl.when(step == 0)
    def first():
        if not whole_rows:
            order[...] = chosen((width, width), for_rows)
        each = width // groups // heads
        for g in range(groups):
            for head in range(heads):
                start = (g * heads + head) * each
                context_t[start : start + each, :] = contexts[head][g]
        context = jnp.transpose(context_t[...].astype(F32)).astype(BF16)
        values = tokens[...].astype(F32) + dot_nn(context, w_out[...])
        mixed[...] = values
        total[...] = values
        wide_values = rms_scale(values, gain)
        normed[...] = wide_values.astype(BF16)
        if whole_rows:
            turned = reordered(jnp.transpose(wide_values), for_rows, unit)
        else:
            turned = dot_nt(order[...], normed[...])
        normed_t[...] = turned.astype(BF16)
        d_normed[...] = jnp.zeros_like(d_normed)

    place = lax.rem(step, 2)
    tall = down.shape[1]

    def wide_copy(slot, index):
        columns = pl.ds(pl.multiple_of(index * 2 * chunk, 2 * chunk), 2 * chunk)
        return pltpu.make_async_copy(wide.at[slot], grads.at[:, columns], sems.at[0, slot])

    def down_copy(slot, index):
        rows = pl.ds(pl.multiple_of(index * tall, tall), tall)
        columns = pl.ds(grads.shape[1] - down.shape[2], down.shape[2])
        return pltpu.make_async_copy(down.at[slot], grads.at[rows, columns], sems.at[1, slot])

    @pl.when(step >= 2)
    def _():
        wide_copy(place, step - 2).wait()
        down_copy(place, step - 2).wait()

    @pl.when(step < chunks)
    def work():
        w_down = unpacked_rows(
            w_packed[...].astype(F32), hidden_unit, width // devices, width
        ).astype(BF16)
        gate = dot_nn(normed[...], w_gate[...])
        upward = dot_nn(normed[...], w_up[...])
        d_hidden = dot_nt(upstream[...], w_down)
        square = gate * gate
        turn = jnp.tanh(GELU_SCALE * (gate + 0.044715 * gate * square))
        half = 0.5 * (1.0 + turn)
        active = gate * half
        slope = half + 0.5 * gate * (1.0 - turn * turn) * (GELU_SCALE * (1.0 + 0.134145 * square))
        wide_hidden = active * upward
        hidden = wide_hidden.astype(BF16)
        d_gate = (d_hidden * upward * slope).astype(BF16)
        d_up = (d_hidden * active).astype(BF16)
        total[...] += dot_nn(hidden, w_down)
        d_normed[...] += dot_nt(d_gate, w_gate[...]) + dot_nt(d_up, w_up[...])
        hidden_t = reordered(jnp.transpose(wide_hidden), for_hidden, hidden_unit).astype(BF16)

        d_down = dot_nn(hidden_t, upstream[...])
        down[place] = packed_rows(d_down, hidden_unit, width // devices).astype(BF16)
        wide[place, :, :chunk] = dot_nn(normed_t[...], d_gate).astype(BF16)
        wide[place, :, chunk:] = dot_nn(normed_t[...], d_up).astype(BF16)
        wide_copy(place, step).start()
        down_copy(place, step).start()

    @pl.when(step == chunks)
    def finish():
        result[...] = total[...].astype(BF16)
        back = upstream[...].astype(F32) + rms_back(mixed[...], gain, d_normed[...])
        d_mixed[...] = back
        branch = back.astype(BF16)
        d_context = dot_nt(w_out[...], branch).astype(BF16)
        each = d_first.shape[1]
        size = width // groups
        for g in range(groups):
            d_first[g] = d_context[size * g : size * g + each]
            d_rest[g] = d_context[size * g + each : size * (g + 1)]
        if whole_rows:
            d_out = reordered(dot_nn(context_t[...], branch), for_rows, unit)
        else:
            d_out = dot_nn(dot_nn(order[...], context_t[...]).astype(BF16), branch)
        wide[place, :, :width] = d_out.astype(BF16)
        wide[place, :, width:] = jnp.zeros((width, 2 * chunk - width), BF16)
        wide_copy(place, step).start()
        wide_copy(1 - place, step - 1).wait()
        down_copy(1 - place, step - 1).wait()
        wide_copy(place, step).wait()


def feed_forward(dims, ints, tokens, contexts, gains, late, upstream):
    groups, splits = dims[1:]
    rows, width = tokens.shape
    hidden = (late.shape[1] - width) // 3
    chunk = 2 * TILE
    steps = hidden // chunk
    each = contexts[0].shape[1]
    full = lambda *shape: pl.BlockSpec(shape, lambda step: (0,) * len(shape))
    return pl.pallas_call(
        functools.partial(block_kernel, dims, len(contexts)),
        grid=(steps + 1,),
        in_specs=[
            smem(),
            full(rows, width),
            pl.BlockSpec((width, width), lambda step: (0, 3 * hidden // width)),
            full(8, width),
            pl.BlockSpec((width, chunk), lambda step: (0, steps + jnp.minimum(step, steps - 1))),
            pl.BlockSpec(
                (width, chunk), lambda step: (0, 2 * steps + jnp.minimum(step, steps - 1))
            ),
            pl.BlockSpec((width // steps, hidden), lambda step: (jnp.minimum(step, steps - 1), 0)),
            full(rows, width),
        ]
        + [full(*context.shape) for context in contexts],
        out_specs=[
            full(rows, width),
            full(rows, width),
            full(groups, each, rows),
            full(groups, width // groups - each, rows),
        ]
        + [pl.BlockSpec(memory_space=pl.ANY)],
        out_shape=[
            jax.ShapeDtypeStruct((rows, width), BF16),
            jax.ShapeDtypeStruct((rows, width), F32),
            jax.ShapeDtypeStruct((groups, each, rows), BF16),
            jax.ShapeDtypeStruct((groups, width // groups - each, rows), BF16),
        ]
        + [jax.ShapeDtypeStruct((width, 3 * hidden + 2 * chunk), BF16)],
        scratch_shapes=[
            pltpu.VMEM((width, rows), BF16),
            pltpu.VMEM((rows, width), F32),
            pltpu.VMEM((rows, width), BF16),
            pltpu.VMEM((width, rows), BF16),
            pltpu.VMEM((rows, width), F32),
            pltpu.VMEM((rows, width), F32),
            pltpu.VMEM((width, width), BF16),
            pltpu.VMEM((2, width, 2 * chunk), BF16),
            pltpu.VMEM((2, width // steps, hidden), BF16),
            pltpu.SemaphoreType.DMA((2, 2)),
        ],
        compiler_params=pltpu.CompilerParams(vmem_limit_bytes=VMEM),
        cost_estimate=pl.CostEstimate(
            flops=18 * rows * width * hidden + 6 * rows * width * width,
            bytes_accessed=12 * width * hidden,
            transcendentals=rows * hidden,
        ),
        name="feed_forward",
    )(ints, tokens, late, gains, late, late, late, upstream, *contexts)


def weight_kernel(splits, normed_t, *refs):
    d_heads, outs, total = refs[: -splits - 1], refs[-splits - 1 : -1], refs[-1]
    step = pl.program_id(0)
    added = dot_nt(normed_t[...], jnp.concatenate([d_head[...] for d_head in d_heads], axis=0))

    @pl.when(step == 0)
    def _():
        total[...] = added

    @pl.when(step > 0)
    def _():
        total[...] += added

    @pl.when(step == pl.num_programs(0) - 1)
    def _():
        part = total.shape[0] // splits
        for other in range(splits):
            outs[other][...] = total[part * other : part * (other + 1), :].astype(BF16)


def weight_grads(splits, normed_t, d_heads):
    groups, rows, tokens = d_heads[0].shape
    width = normed_t.shape[0]
    out = (width // splits, rows * len(d_heads))
    return pl.pallas_call(
        functools.partial(weight_kernel, splits),
        grid=(groups,),
        in_specs=[pl.BlockSpec((width, tokens), lambda step: (0, step))]
        + [by_slot(rows, tokens)] * len(d_heads),
        out_specs=[pl.BlockSpec(out, lambda step: (0, 0))] * splits,
        out_shape=[jax.ShapeDtypeStruct(out, BF16)] * splits,
        scratch_shapes=[pltpu.VMEM((width, out[1]), F32)],
        compiler_params=pltpu.CompilerParams(vmem_limit_bytes=VMEM),
        cost_estimate=pl.CostEstimate(
            flops=2 * width * out[1] * groups * tokens,
            bytes_accessed=2 * width * groups * tokens,
            transcendentals=0,
        ),
        name="weight_grads",
    )(normed_t, *d_heads)


def added_kernel(count, *refs):
    held, outs = refs[:count], refs[count:]
    total = held[0][...].astype(F32)
    for piece in held[1:]:
        total += piece[...].astype(F32)
    part = total.shape[0] // len(outs)
    for index, out in enumerate(outs):
        out[...] = total[part * index : part * (index + 1)].astype(out.dtype)


def added(pieces, parts):
    rows, columns = pieces[0].shape
    return pl.pallas_call(
        functools.partial(added_kernel, len(pieces)),
        out_shape=[jax.ShapeDtypeStruct((rows // parts, columns), BF16)] * parts,
        compiler_params=pltpu.CompilerParams(vmem_limit_bytes=VMEM),
        cost_estimate=pl.CostEstimate(flops=0, bytes_accessed=2**20, transcendentals=0),
        name="added",
    )(*pieces)


def unpacked(pieces, heads, size):
    return jnp.concatenate(
        [
            piece[:, (3 * head + part) * size : (3 * head + part + 1) * size]
            for part in range(3)
            for piece in pieces
            for head in range(heads)
        ],
        axis=1,
    )


def count_kernel(groups, heads, size, count, down, ints, *refs):
    held, tables, grads = refs[:count], refs[count : count + heads], refs[count + heads]
    outs, counts = refs[count + heads + 1 : -1], refs[-1]
    total = held[0][...].astype(F32)
    for piece in held[1:]:
        total += piece[...].astype(F32)
    part = total.shape[0] // groups
    blank = jnp.zeros((part, counts.shape[1] - total.shape[1]), F32)
    for index, out in enumerate(outs):
        rows = total[part * index : part * (index + 1)]
        out[...] = jnp.concatenate([rows, blank], axis=1)
    squares = jnp.sum(total * total, axis=0, keepdims=True)
    table = jnp.concatenate(
        [jnp.sum(jnp.transpose(table[...]), axis=0, keepdims=True) for table in tables], axis=1
    )
    mine = [(ints[4] == g).astype(F32) for g in range(groups)]
    values = grads[...].astype(F32)
    values = values * values
    wide = values.shape[1] - down[0]
    piece = math.gcd(*down[1:3])
    across = down[2] // piece
    each = down[0] * piece // down[1]
    packed = []
    for part in range(across):
        rows = jnp.sum(values[piece * part : piece * (part + 1), wide:], axis=0, keepdims=True)
        packed.append(sum(rows[:, start : start + each] for start in range(0, down[0], each)))
    row = jnp.concatenate(
        [table * own for own in mine]
        + [unpacked([squares * own for own in mine], heads, size)]
        + [jnp.sum(values[:, : wide - down[3]], axis=0, keepdims=True)]
        + packed,
        axis=1,
    )
    counts[...] = jnp.zeros_like(counts)
    each = counts.shape[1]
    for start in range(0, row.shape[1], each):
        held_row = row[:, start : start + each]
        counts[start // each : start // each + 1, : held_row.shape[1]] = held_row


def counted(groups, heads, size, ints, pieces, tables, grads, down):
    rows, columns = pieces[0].shape
    buckets = tables[0].shape[0]
    length = groups * (heads * buckets + columns) + grads.shape[1] - down[0] - down[3]
    length += down[0] * down[2] // down[1]
    across = -(-columns // LANES) * LANES
    counts = -(-length // (8 * across)) * 8
    vmem = pl.BlockSpec(memory_space=pltpu.VMEM)
    return pl.pallas_call(
        functools.partial(count_kernel, groups, heads, size, len(pieces), down),
        in_specs=[smem()] + [vmem] * (len(pieces) + len(tables) + 1),
        out_shape=[jax.ShapeDtypeStruct((rows // groups, across), F32)] * groups
        + [jax.ShapeDtypeStruct((counts, across), F32)],
        compiler_params=pltpu.CompilerParams(vmem_limit_bytes=VMEM),
        cost_estimate=pl.CostEstimate(flops=0, bytes_accessed=2**20, transcendentals=0),
        name="counted",
    )(ints, *pieces, *tables, grads)


def input_kernel(heads, weights, own, gains, d_mixed, *refs):
    d_heads, (out, total) = refs[:heads], refs[heads:]
    step = pl.program_id(0)
    size = d_heads[0].shape[0] // 3
    blank = jnp.zeros((size, own.shape[0]), BF16)
    pieces = [d_head[size:, :] for d_head in d_heads]
    pieces += [d_head[:size, :] for d_head in d_heads] + [blank]
    added = dot_nn(weights[...], jnp.concatenate(pieces, axis=0))

    @pl.when(step == 0)
    def _():
        total[...] = added

    @pl.when(step > 0)
    def _():
        total[...] += added

    @pl.when(step == pl.num_programs(0) - 1)
    def _():
        back = rms_back(own[...].astype(F32), gains[0:1, :], jnp.transpose(total[...]))
        out[...] = (d_mixed[...] + back).astype(BF16)


def input_grads(groups, weights, own, gains, d_mixed, d_heads):
    tokens, width = own.shape
    full = lambda *shape: pl.BlockSpec(shape, lambda step: (0,) * len(shape))
    return pl.pallas_call(
        functools.partial(input_kernel, len(d_heads)),
        grid=(groups,),
        in_specs=[
            pl.BlockSpec((width, weights.shape[1] // groups), lambda step: (0, step)),
            full(tokens, width),
            full(8, width),
            full(tokens, width),
        ]
        + [by_slot(*d_heads[0].shape[1:])] * len(d_heads),
        out_specs=full(tokens, width),
        out_shape=jax.ShapeDtypeStruct((tokens, width), BF16),
        scratch_shapes=[pltpu.VMEM((width, tokens), F32)],
        compiler_params=pltpu.CompilerParams(vmem_limit_bytes=VMEM),
        cost_estimate=pl.CostEstimate(
            flops=2 * tokens * width * weights.shape[1],
            bytes_accessed=16 * tokens * width,
            transcendentals=0,
        ),
        name="input_grads",
    )(weights, own, gains, d_mixed, *d_heads)


def by_slot(rows, tokens):
    return pl.BlockSpec((None, rows, tokens), lambda slot: (slot, 0, 0))


def smem():
    return pl.BlockSpec(memory_space=pltpu.SMEM)


def attend(head, tokens, groups, splits, ints, table, query, kvs):
    seq, rows = tokens * groups * splits, tokens * groups
    half = LANES // 2
    whole = pl.BlockSpec((rows, LANES), lambda slot: (0, head))
    return pl.pallas_call(
        functools.partial(forward_kernel, tokens, groups, splits),
        grid=(groups,),
        in_specs=[smem(), smem(), pl.BlockSpec((tokens, LANES), lambda slot: (slot, head))]
        + [whole] * splits,
        out_specs=[
            pl.BlockSpec((seq, tokens), lambda slot: (slot, 0)),
            by_slot(half, tokens),
            by_slot(half + 16, tokens),
        ],
        out_shape=[
            jax.ShapeDtypeStruct((groups * seq, tokens), BF16),
            jax.ShapeDtypeStruct((groups, half, tokens), BF16),
            jax.ShapeDtypeStruct((groups, half + 16, tokens), F32),
        ],
        scratch_shapes=[
            pltpu.VMEM((seq + 2 * LANES, LANES), BF16),
            pltpu.VMEM((half + 16, seq + 2 * LANES), BF16),
            pltpu.VMEM((tokens + 2 * LANES, tokens), F32),
            pltpu.VMEM((3, LANES, LANES), F32),
            pltpu.VMEM((8, tokens), F32),
        ],
        compiler_params=pltpu.CompilerParams(vmem_limit_bytes=VMEM),
        cost_estimate=pl.CostEstimate(
            flops=16 * seq * rows * half, bytes_accessed=2 * seq * rows, transcendentals=seq * rows
        ),
        name="attend",
    )(ints, table, query, *kvs)


def attend_back(
    head, tokens, groups, splits, ints, buckets, query, d_context, place, stats, probs, kvs
):
    seq, rows = tokens * groups * splits, tokens * groups
    half = LANES // 2
    whole = pl.BlockSpec((rows, LANES), lambda slot: (0, head))
    kept = pl.BlockSpec((groups, LANES, tokens), lambda slot: (0, 0, 0))
    return pl.pallas_call(
        functools.partial(backward_kernel, tokens, groups, splits),
        grid=(groups,),
        in_specs=[
            smem(),
            pl.BlockSpec((tokens, LANES), lambda slot: (slot, head)),
            pl.BlockSpec((None, None, half, tokens), lambda slot: (slot, place, 0, 0)),
            by_slot(half + 16, tokens),
            pl.BlockSpec((seq, tokens), lambda slot: (slot, 0)),
        ]
        + [whole] * splits,
        out_specs=[pl.BlockSpec((groups, half + LANES, tokens), lambda slot: (0, 0, 0))]
        + [kept] * (splits - 1)
        + [pl.BlockSpec((buckets, LANES), lambda slot: (0, 0))],
        out_shape=[jax.ShapeDtypeStruct((groups, half + LANES, tokens), BF16)]
        + [jax.ShapeDtypeStruct((groups, LANES, tokens), BF16)] * (splits - 1)
        + [jax.ShapeDtypeStruct((buckets, LANES), F32)],
        scratch_shapes=[
            pltpu.VMEM((seq + 2 * LANES, LANES), BF16),
            pltpu.VMEM((half + 16, seq + 2 * LANES), BF16),
            pltpu.VMEM((seq + 2 * LANES, LANES), F32),
            pltpu.VMEM((3, LANES, LANES), F32),
            pltpu.VMEM((2, 8, tokens), F32),
            pltpu.VMEM((half + 16, tokens), F32),
        ],
        compiler_params=pltpu.CompilerParams(vmem_limit_bytes=VMEM),
        cost_estimate=pl.CostEstimate(
            flops=32 * seq * rows * half, bytes_accessed=2 * seq * rows, transcendentals=0
        ),
        name="attend_back",
    )(ints, query, d_context, stats, probs, *kvs)


def factored(grad_shard, column_total, row_old, column_old, row_total):
    columns = grad_shard.shape[1]
    mean_square = jnp.sum(column_total) / (row_total * columns) + EPSILON
    row_new = (
        DECAY_RATE * row_old
        + (1.0 - DECAY_RATE) * (jnp.sum(grad_shard * grad_shard, axis=1) / columns) / mean_square
    )
    column_new = (
        DECAY_RATE * column_old + (1.0 - DECAY_RATE) * (column_total / row_total) / mean_square
    )
    return (row_new, column_new)


def shards(
    tokens,
    lengths,
    norm_one,
    w_qkv,
    rel_table,
    w_out,
    norm_two,
    w_gateup,
    w_down,
    cotangent,
    row_qkv,
    col_qkv,
    row_out,
    col_out,
    row_gateup,
    col_gateup,
    row_down,
    col_down,
):
    own = tokens[0]
    tok_rows, width = own.shape
    heads = rel_table.shape[1]
    buckets = rel_table.shape[0]
    rows_apart, groups, splits = (lax.axis_size(name) for name in ALL)
    group_heads = heads // groups
    head_size = width // heads
    group, split = lax.axis_index("group"), lax.axis_index("split")
    group_width = width // groups

    def ahead(array, axis, by):
        size = lax.axis_size(axis)
        return lax.ppermute(array, axis, [((i + by) % size, i) for i in range(size)])

    def swap_groups(array):
        return lax.all_to_all(array, "group", 0, 0)

    def swap_rows(array):
        return lax.all_to_all(array, "batch", 0, 0)

    def line(array, by):
        pairs = [(i, i + by) for i in range(groups) if 0 <= i + by < groups]
        return lax.ppermute(array, "group", pairs)

    before, behind = [own], [own]
    for _ in range(groups - 1):
        before.append(line(before[-1], 1))
        behind.append(line(behind[-1], -1))

    unit = w_qkv.shape[0]
    by_part = w_qkv.reshape(unit, 3, groups, group_heads, head_size)
    gains = jnp.pad(jnp.stack([norm_one, norm_two], axis=1), ((0, 0), (0, head_size - 2)))
    packed = jnp.concatenate(
        [
            jnp.concatenate([by_part[:, 1], by_part[:, 2]], axis=-1).reshape(unit, groups, -1),
            by_part[:, 0].reshape(unit, groups, -1),
            jnp.broadcast_to(gains[:, None], (unit, groups, head_size)),
        ],
        axis=2,
    )
    early = lax.all_gather(packed.reshape(unit, -1), ALL, axis=0, tiled=True)
    together = math.gcd(unit, w_down.shape[0])
    packed_down = w_down.reshape(w_down.shape[0] // together, together, unit // together, -1)
    packed_down = jnp.transpose(packed_down, (2, 1, 0, 3)).reshape(unit, -1)
    late = lax.all_gather(
        after(jnp.concatenate([packed_down, w_gateup, w_out], axis=1), before[1], behind[1]),
        ALL,
        axis=0,
        tiled=True,
    )

    dims = (rows_apart, groups, splits)
    far = jnp.where(group == 0, groups - 1, jnp.where(group == groups - 1, 0, group))
    ends = jnp.cumsum(lengths[0])
    ints = jnp.concatenate(
        [
            split.astype(jnp.int32)[None],
            ends.astype(jnp.int32),
            jnp.stack([group, lax.axis_index("batch"), far]).astype(jnp.int32),
        ]
    )
    *blocks, gains, order = project(dims, ints, early, own, before[1:-1] + behind[1:-1])
    normed_t, query, kv = project_last(
        dims, ints, early, own, before[-1], behind[-1], order, gains, *blocks
    )
    kvs = [kv] + [ahead(kv, "split", other) for other in range(1, splits)]

    table_own = lax.dynamic_slice_in_dim(rel_table.T, group * group_heads, group_heads, 0)

    contexts, moved, stats, probs = [], [], [], []
    for head in range(group_heads):
        prob, context, stat = attend(
            head,
            tok_rows,
            groups,
            splits,
            after(ints, *contexts[-1:]),
            table_own[head : head + 1],
            query,
            kvs,
        )
        contexts.append(context)
        moved.append(swap_groups(after(context, *moved[-1:])))
        stats.append(stat)
        probs.append(prob)

    outs = feed_forward(
        dims, ints, own, moved, gains, late, cotangent[0]
    )
    result, d_mixed, d_first, d_rest, held = outs

    d_first = swap_groups(d_first)
    d_rest = swap_groups(d_rest)
    d_contexts = [d_first[:, None], d_rest.reshape(groups, group_heads - 1, head_size, tok_rows)]
    row_sum = lax.psum_scatter(held, ("batch", "split"), scatter_dimension=0, tiled=True)
    row_sum = after(row_sum)
    grads_own = lax.psum_scatter(row_sum, "group", scatter_dimension=0, tiled=True)

    d_heads, d_received, d_tables = [], [], []
    ready = [(), ()] + [(row_sum,)] * (group_heads - 2)
    for head in range(group_heads):
        outs = attend_back(
            head,
            tok_rows,
            groups,
            splits,
            ints,
            buckets,
            query,
            after(d_contexts[int(head > 0)], *ready[head], *d_heads[-1:]),
            head - int(head > 0),
            stats[head],
            probs[head],
            kvs,
        )
        beside = d_received[-1] if head else d_contexts[1]
        if head < group_heads - 1:
            outs = lax.optimization_barrier((*outs, beside))[:-1]
        d_head = outs[0].astype(F32)
        for other in range(1, splits):
            d_kv = ahead(outs[other], "split", splits - other).astype(F32)
            d_head = d_head + jnp.pad(d_kv, ((0, 0), (head_size, 0), (0, 0)))
        d_head = d_head.astype(BF16)
        if head == group_heads - 1:
            d_head = after(d_head, beside)
        d_heads.append(d_head)
        d_received.append(swap_groups(d_head))
        d_tables.append(outs[-1])

    down_shape = (w_down.shape[0] * width // unit, w_down.shape[0], unit)
    down_start = grads_own.shape[1] - down_shape[0]
    down_shape += (down_start - w_gateup.shape[1] - width,)
    grads = weight_grads(splits, normed_t, d_heads)
    held = added(
        [grads[0]] + [ahead(grads[by], "split", splits - by) for by in range(1, splits)], rows_apart
    )
    held = [held[0]] + [ahead(held[by], "batch", rows_apart - by) for by in range(1, rows_apart)]
    held[0] = after(held[0], d_received[-1])
    *columns, counts = counted(
        groups, group_heads, head_size, ints, held, d_tables, grads_own, down_shape
    )
    counts = sum([ahead(counts, "batch", by) for by in range(1, rows_apart)], counts)
    d_received[-1] = after(d_received[-1], counts)
    d_inputs = input_grads(groups, early, own, gains, d_mixed, d_received)
    counts_rows = counts.shape[0]
    travelled = [jnp.concatenate([counts, columns[0]], axis=0)] + [
        ahead(jnp.concatenate([counts, columns[by]], axis=0), "group", groups - by)
        for by in range(1, groups)
    ]
    *travelled, d_inputs = lax.optimization_barrier((*travelled, d_inputs))
    columns = [both[counts_rows:] for both in travelled]
    counts = sum([both[:counts_rows] for both in travelled[1:]], travelled[0][:counts_rows])
    counts = sum([ahead(counts, "split", by) for by in range(1, splits)], counts)
    pieces = []
    for index in range(groups):
        piece = columns[0]
        for by in range(1, groups):
            piece = jnp.where((group + groups - by) % groups == index, columns[by], piece)
        pieces.append(piece)
    shard_qkv = unpacked(pieces, group_heads, head_size)
    steps = w_down.shape[0] * rows_apart * groups * splits // (2 * TILE)

    def in_order(array):
        array = array.reshape(*array.shape[:-1], steps, 2, -1)
        return jnp.swapaxes(array, -3, -2).reshape(*array.shape[:-3], -1)

    shard_rest = grads_own.astype(F32)
    shard_gateup = in_order(shard_rest[:, : w_gateup.shape[1]])
    shard_out = shard_rest[:, w_gateup.shape[1] :][:, :width]
    shard_down = shard_rest[:, down_start:].reshape(
        unit // together, together, w_down.shape[0] // together, -1
    )
    shard_down = jnp.transpose(shard_down, (2, 1, 0, 3)).reshape(-1, width)
    summed = counts.reshape(-1)
    sizes = (heads * buckets, 3 * width, w_gateup.shape[1], width, width)
    table_total, column_qkv, column_gateup, column_out, column_down, _ = jnp.split(
        summed, [sum(sizes[: i + 1]) for i in range(len(sizes))]
    )
    table_total = table_total.reshape(heads, buckets)
    column_gateup = in_order(column_gateup)
    shard_gain_one = jnp.sum(w_qkv.astype(F32) * shard_qkv, axis=1) / norm_one.astype(F32)
    shard_gain_two = jnp.sum(w_gateup.astype(F32) * shard_gateup, axis=1) / norm_two.astype(F32)
    new_row_qkv, new_col_qkv = factored(shard_qkv, column_qkv, row_qkv, col_qkv, width)
    new_row_out, new_col_out = factored(shard_out, column_out, row_out, col_out, width)
    new_row_gateup, new_col_gateup = factored(
        shard_gateup, column_gateup, row_gateup, col_gateup, width
    )
    new_row_down, new_col_down = factored(
        shard_down, column_down, row_down, col_down, w_down.shape[0] * rows_apart * groups * splits
    )
    return (
        result[None],
        d_inputs[None],
        shard_gain_one,
        shard_qkv,
        table_total.T,
        shard_out,
        shard_gain_two,
        shard_gateup,
        shard_down,
        new_row_qkv,
        new_col_qkv,
        new_row_out,
        new_col_out,
        new_row_gateup,
        new_col_gateup,
        new_row_down,
        new_col_down,
    )


def solution(mesh):
    row_blocks = P("batch", ("group", "split"), None)
    split_rows = P(ALL, None)
    split_row = P(ALL)

    def run(*arrays):
        rows, ring = mesh.devices.shape
        groups = math.gcd(ring, arrays[4].shape[1])
        fine = Mesh(mesh.devices.reshape(rows, groups, ring // groups), ALL)
        return jax.shard_map(
            shards,
            mesh=fine,
            in_specs=(
                row_blocks,
                P("batch", None),
                split_row,
                split_rows,
                P(),
                split_rows,
                split_row,
                split_rows,
                split_rows,
                row_blocks,
            )
            + (split_row, P()) * 4,
            out_specs=(
                row_blocks,
                row_blocks,
                split_row,
                split_rows,
                P(),
                split_rows,
                split_row,
                split_rows,
                split_rows,
            )
            + (split_row, P()) * 4,
            check_vma=False,
        )(*arrays)

    return run
```

```python
import functools
import math

import jax
import jax.numpy as jnp
from jax import lax
from jax.experimental import pallas as pl
from jax.experimental.pallas import tpu as pltpu
from jax.sharding import Mesh
from jax.sharding import PartitionSpec as P

THRESHOLDS = (12, 16, 23, 32, 46, 64, 91)
EPSILON = 1e-06
DECAY_RATE = 0.5
GELU_SCALE = 0.7978845608028654
MASKED = -1e9
LEEWAY = 20.0
ALL = ("batch", "group", "split")
LANES = 128
TILE = 256
GROUP = 4
VMEM = 60 * 2**20
F32 = jnp.float32
BF16 = jnp.bfloat16


def bucket_of(offset):
    distance = jnp.abs(offset)
    steps_up = 8 + sum(((distance >= limit).astype(jnp.int32) for limit in THRESHOLDS))
    within = jnp.where(distance < 8, distance, steps_up)
    return within + 16 * (offset > 0).astype(jnp.int32)


def after(value, *others):
    return lax.optimization_barrier((value, *others))[0]


def rms_scale(values, gain):
    return values * lax.rsqrt(jnp.mean(values * values, axis=-1, keepdims=True) + EPSILON) * gain


def rms_back(values, gain, grad):
    scale = lax.rsqrt(jnp.mean(values * values, axis=-1, keepdims=True) + EPSILON)
    scaled = grad * gain
    return scale * scaled - values * scale**3 * jnp.mean(scaled * values, axis=-1, keepdims=True)


def dot_nn(left, right):
    return jnp.dot(left, right, preferred_element_type=F32)


def dot_nt(left, right):
    return lax.dot_general(left, right, (((1,), (1,)), ((), ())), preferred_element_type=F32)


def dot_tt(left, right):
    return lax.dot_general(left, right, (((0,), (1,)), ((), ())), preferred_element_type=F32)


class Layout:
    def __init__(self, tokens, groups, splits, ints):
        self.tokens, self.groups, self.splits = tokens, groups, splits
        self.blocks = groups * splits
        self.seq = tokens * self.blocks
        self.near = tokens + 2 * LANES
        self.subs = tokens // LANES
        self.split = ints[0]
        self.ends = (ints[1], ints[2], ints[3])
        slot = pl.program_id(0)
        self.block = self.block_of(slot, 0)
        self.first = pl.multiple_of(self.block * tokens, LANES)
        self.lefts = jnp.maximum(0, self.block * (tokens // TILE) - 1)
        self.loops = (self.seq // TILE - 2 - tokens // TILE) // GROUP
        self.edge = jnp.logical_or(self.block == 0, self.block == self.blocks - 1)

    def block_of(self, slot, other):
        return slot * self.splits + lax.rem(self.split + other, self.splits)

    def keys_of(self, tile):
        before = 2 * LANES + TILE * tile
        after = self.first + self.near + TILE * (tile - self.lefts)
        return pl.ds(pl.multiple_of(jnp.where(tile < self.lefts, before, after), LANES), TILE)

    def rows_of(self, tile):
        return pl.ds(pl.multiple_of(self.near + TILE * tile, LANES), TILE)

    def segment(self, positions):
        return sum((positions >= end).astype(jnp.int32) for end in self.ends)


def iota(shape, dim):
    return lax.broadcasted_iota(jnp.int32, shape, dim)


def fold(values):
    return values.reshape(values.shape[0] // 8, 8, values.shape[1])


def forward_kernel(tokens, groups, splits, ints, table, query, *refs):
    kvs, (probs, context, stats, k_aug, v_t, scores, biases, best) = refs[:splits], refs[splits:]
    lay = Layout(tokens, groups, splits, ints)
    half = query.shape[1] // 2
    buckets = table.shape[1]

    @pl.when(pl.program_id(0) == 0)
    def prepare():
        lane = iota((tokens, LANES), 1)
        for slot in range(groups):
            for other in range(splits):
                start = lay.block_of(slot, other) * tokens
                rows = pl.ds(pl.multiple_of(LANES + start, LANES), tokens)
                kv = kvs[other][slot * tokens : (slot + 1) * tokens, :].astype(F32)
                seg = lay.segment(start + iota((tokens, LANES), 0))
                k_aug[rows, :] = jnp.where(lane < half, kv, (lane - half == seg).astype(F32)).astype(BF16)
                turned = jnp.transpose(kv)
                ones = (iota((16, tokens), 0) == 0).astype(F32)
                v_t[:, rows] = jnp.concatenate([turned[half:], ones], axis=0).astype(BF16)
        outside = (iota((LANES, LANES), 1) == half + 3).astype(BF16)
        for start in (0, lay.seq + LANES):
            k_aug[start : start + LANES, :] = outside
            v_t[:, start : start + LANES] = jnp.zeros((half + 16, LANES), BF16)
        for place in range(3):
            bucket = bucket_of(
                LANES * (place - 1) + iota((LANES, LANES), 0) - iota((LANES, LANES), 1)
            )
            bias = jnp.zeros((LANES, LANES), F32)
            for label in range(buckets):
                bias = jnp.where(bucket == label, table[0, label], bias)
            biases[place] = bias

    far_left, far_right = table[0, buckets // 2 - 1], table[0, buckets - 1]
    positions = lay.block * tokens + iota((1, tokens), 1)
    seg_q = lay.segment(positions)
    row = iota((2 * half, tokens), 0)
    apart = jnp.logical_or(row - half != seg_q, row == half + 3)
    q_aug = jnp.where(
        row < half, jnp.transpose(query[...].astype(F32)), jnp.where(apart, MASKED, 0.0)
    ).astype(BF16)

    near = dot_nn(k_aug[pl.ds(lay.first, lay.near), :], q_aug)
    eye = iota((LANES, LANES), 0) == iota((LANES, LANES), 1)
    for sub_q in range(lay.subs):
        lanes = slice(LANES * sub_q, LANES * (sub_q + 1))
        top = None
        for sub_k in range(lay.subs + 2):
            rows = slice(LANES * sub_k, LANES * (sub_k + 1))
            place = sub_k - sub_q
            piece = near[rows, lanes] + (
                far_left if place < 0 else far_right if place > 2 else biases[place]
            )
            if place == 1:
                alone = jnp.logical_and(eye, positions[:, lanes] >= lay.ends[2])
                piece = jnp.where(alone, 0.0, piece)
            scores[rows, lanes] = piece
            high = jnp.max(fold(piece), axis=0)
            top = high if top is None else jnp.maximum(top, high)
        best[:, lanes] = top

    def sweep(peak):
        weights = jnp.exp(scores[...] - peak).astype(BF16)
        probs[: lay.near, :] = weights
        stats[...] = dot_nn(v_t[:, pl.ds(lay.first, lay.near)], weights)
        left_peak, right_peak = peak - far_left, peak - far_right

        def tiles(index, count):
            places = [lay.keys_of(index + step) for step in range(count)]
            piece = dot_nn(jnp.concatenate([k_aug[keys, :] for keys in places], axis=0), q_aug)
            parts, top = [], best[...]
            for step in range(count):
                score = piece[TILE * step : TILE * (step + 1)]
                is_left = index + step < lay.lefts
                top = jnp.maximum(
                    top,
                    jnp.max(fold(score), axis=0) + jnp.where(is_left, far_left, far_right),
                )
                part = jnp.exp(score - jnp.where(is_left, left_peak, right_peak)).astype(BF16)
                probs[lay.rows_of(index + step), :] = part
                parts.append(part)
            best[...] = top
            values = jnp.concatenate([v_t[:, keys] for keys in places], axis=1)
            stats[...] += dot_nn(values, jnp.concatenate(parts, axis=0))

        if lay.loops <= 3:
            for index in range(lay.loops):
                tiles(index * GROUP, GROUP)
        else:

            def group(index, carry):
                tiles(index * GROUP, GROUP)
                return carry

            lax.fori_loop(0, lay.loops, group, 0)

        @pl.when(lay.edge)
        def _():
            tiles(lay.loops * GROUP, 1)

    peak = jnp.max(best[...], axis=0, keepdims=True)
    sweep(peak)
    true_peak = jnp.max(best[...], axis=0, keepdims=True)

    @pl.when(jnp.max(true_peak - peak) > LEEWAY)
    def _():
        sweep(true_peak)

    inverse = 1.0 / stats[half : half + 1, :]
    result = stats[:half, :] * inverse
    context[...] = result.astype(BF16)
    stats[:half, :] = result
    stats[half : half + 1, :] = inverse


def backward_kernel(tokens, groups, splits, ints, query, d_context, stats, probs, *refs):
    kvs, d_kvs = refs[:splits], refs[splits : 2 * splits]
    d_table, v_aug, k_t, d_kv, bands, sides, d_q = refs[2 * splits :]
    lay = Layout(tokens, groups, splits, ints)
    half = query.shape[1] // 2
    buckets = d_table.shape[0]

    @pl.when(pl.program_id(0) == 0)
    def prepare():
        lane = iota((tokens, LANES), 1)
        for slot in range(groups):
            for other in range(splits):
                start = lay.block_of(slot, other) * tokens
                rows = pl.ds(pl.multiple_of(LANES + start, LANES), tokens)
                kv = kvs[other][slot * tokens : (slot + 1) * tokens, :].astype(F32)
                v_aug[rows, :] = jnp.where(lane >= half, kv, (lane < 3).astype(F32)).astype(BF16)
                ones = (iota((16, tokens), 0) == 0).astype(F32)
                k_t[:, rows] = jnp.concatenate([jnp.transpose(kv)[:half], ones], axis=0).astype(BF16)
        for start in (0, lay.seq + LANES):
            v_aug[start : start + LANES, :] = jnp.zeros((LANES, LANES), BF16)
            k_t[:, start : start + LANES] = jnp.zeros((half + 16, LANES), BF16)
        d_kv[...] = jnp.zeros_like(d_kv)
        bands[...] = jnp.zeros_like(bands)
        sides[...] = jnp.zeros_like(sides)

    inverse = stats[half : half + 1, :]
    upstream = d_context[...].astype(F32)
    delta = jnp.sum(upstream * stats[:half, :], axis=0, keepdims=True) * inverse
    scaled = upstream * inverse
    high = delta.astype(BF16).astype(F32)
    middle = (delta - high).astype(BF16).astype(F32)
    low = delta - high - middle
    row = iota((half, tokens), 0)
    shift = jnp.where(row == 0, high, jnp.where(row == 1, middle, jnp.where(row == 2, low, 0.0)))
    up_aug = jnp.concatenate([-shift, scaled], axis=0).astype(BF16)
    up_rows = jnp.transpose(jnp.concatenate([jnp.zeros_like(scaled), scaled], axis=0)).astype(BF16)
    both = jnp.concatenate([query[...], up_rows], axis=0)

    def grads(keys, rows):
        part = jnp.concatenate([probs[where, :] for where in rows], axis=0)
        values = jnp.concatenate([v_aug[where, :] for where in keys], axis=0)
        d_scores = part.astype(F32) * dot_nn(values, up_aug)
        rounded = d_scores.astype(BF16)
        added = dot_nn(jnp.concatenate([rounded, part], axis=1), both)
        size = part.shape[0] // len(keys)
        for index, where in enumerate(keys):
            d_kv[where, :] += added[size * index : size * (index + 1)]
        return d_scores, rounded

    near, rounded = grads([pl.ds(lay.first, lay.near)], [pl.ds(0, lay.near)])
    total = dot_nn(k_t[:, pl.ds(lay.first, lay.near)], rounded)
    for sub_q in range(lay.subs):
        lanes = slice(LANES * sub_q, LANES * (sub_q + 1))
        for sub_k in range(lay.subs + 2):
            piece = near[LANES * sub_k : LANES * (sub_k + 1), lanes]
            place = sub_k - sub_q
            if 0 <= place <= 2:
                bands[place] += piece
            else:
                sides[int(place > 2), :, lanes] += jnp.sum(fold(piece), axis=0)
    d_q[...] = total
    near_sum = total[half : half + 8, :]

    def far(index, count):
        places = [lay.keys_of(index + step) for step in range(count)]
        rounded = grads(places, [lay.rows_of(index + step) for step in range(count)])[1]
        keys = jnp.concatenate([k_t[:, where] for where in places], axis=1)
        lefts = jnp.clip(lay.lefts - index, 0, count) * TILE
        row = iota(keys.shape, 0)
        side = jnp.logical_and(row == half + 8, iota(keys.shape, 1) < lefts)
        keys = jnp.where(side, 1.0, keys.astype(F32)).astype(BF16)
        d_q[...] += dot_nn(keys, rounded)

    if lay.loops <= 3:
        for index in range(lay.loops):
            far(index * GROUP, GROUP)
    else:

        def group(index, carry):
            far(index * GROUP, GROUP)
            return carry

        lax.fori_loop(0, lay.loops, group, 0)

    @pl.when(lay.edge)
    def _():
        far(lay.loops * GROUP, 1)

    left_sum = d_q[half + 8 : half + 16, :]
    sides[0] += left_sum
    sides[1] += d_q[half : half + 8, :] - near_sum - left_sum
    d_kvs[0][pl.program_id(0), :half, :] = d_q[:half, :].astype(BF16)

    @pl.when(pl.program_id(0) == groups - 1)
    def finish():
        for slot in range(groups):
            for other in range(splits):
                start = lay.block_of(slot, other) * tokens
                rows = pl.ds(pl.multiple_of(LANES + start, LANES), tokens)
                turned = jnp.transpose(d_kv[rows, :]).astype(BF16)
                if other:
                    d_kvs[other][slot] = turned
                else:
                    d_kvs[0][slot, half:, :] = turned
        labels = [
            bucket_of(LANES * (place - 1) + iota((LANES, LANES), 0) - iota((LANES, LANES), 1))
            for place in range(3)
        ]
        for label in range(buckets):
            found = jnp.zeros((8, LANES), F32)
            for place in range(3):
                kept = jnp.where(labels[place] == label, bands[place], 0.0)
                found += jnp.sum(fold(kept), axis=0)
            if label in (buckets // 2 - 1, buckets - 1):
                side = sides[int(label == buckets - 1)]
                for sub in range(lay.subs):
                    found += side[:, LANES * sub : LANES * (sub + 1)]
            d_table[label : label + 1, :] = jnp.sum(found, axis=0, keepdims=True)


def chosen(shape, source):
    return (source(iota((shape[0], 1), 0)) == iota(shape, 1)).astype(F32).astype(BF16)


def project_block(values, weights, gains, order, normed_t, query, kv):
    normed = rms_scale(values.astype(F32), gains[0:1, :]).astype(BF16)
    normed_t[...] = dot_nt(order[...], normed).astype(BF16)
    both = dot_nn(normed, weights[...])
    narrow = kv.shape[1]
    kv[...] = both[:, :narrow].astype(BF16)
    size = LANES // 2
    blank = jnp.zeros((both.shape[0], size), F32)
    parts = []
    for start in range(narrow, narrow + narrow // 2, size):
        parts += [both[:, start : start + size], blank]
    query[...] = jnp.concatenate(parts, axis=1).astype(BF16)


def project_kernel(dims, ints, weights, own, *refs):
    rows_apart, groups, splits = dims
    others, (normed_t, query, kv, gains, order, values) = refs[:-6], refs[-6:]
    slot, split, group, batch = pl.program_id(0), ints[0], ints[4], ints[5]
    width, narrow = own.shape[1], kv.shape[1]
    unit = width // (rows_apart * groups * splits)

    @pl.when(slot == 0)
    def _():
        def source(index):
            within = lax.rem(index, unit)
            index = index // unit
            g = lax.rem(group + lax.rem(index, groups), groups)
            index = index // groups
            b = lax.rem(batch + lax.rem(index, rows_apart), rows_apart)
            r = lax.rem(split + index // rows_apart, splits)
            return ((b * groups + g) * splits + r) * unit + within

        order[...] = chosen((width, width), source)
        turned = jnp.transpose(weights[:, weights.shape[1] - LANES :].astype(F32))
        gains[...] = turned[LANES // 2 : LANES // 2 + 8]

    @pl.when(slot == group)
    def _():
        values[...] = own[...]

    for by in range(1, groups - 1):

        @pl.when(slot == group - by)
        def _():
            values[...] = others[by - 1][...]

        @pl.when(slot == group + by)
        def _():
            values[...] = others[groups + by - 3][...]

    @pl.when(jnp.abs(slot - group) < groups - 1)
    def _():
        project_block(values[...], weights, gains, order, normed_t, query, kv)


def project(dims, ints, weights, own, others):
    tokens, width = own.shape
    groups = dims[1]
    narrow = 2 * width // groups
    whole = pl.BlockSpec((tokens, width), lambda slot, ints: (0, 0))
    by_row = pl.BlockSpec((tokens, narrow), lambda slot, ints: (slot, 0))
    return pl.pallas_call(
        functools.partial(project_kernel, dims),
        grid_spec=pltpu.PrefetchScalarGridSpec(
            num_scalar_prefetch=1,
            grid=(groups,),
            in_specs=[pl.BlockSpec((width, weights.shape[1] // groups), lambda slot, ints: (0, ints[4]))]
            + [whole] * (1 + len(others)),
            out_specs=[
                pl.BlockSpec((width, tokens), lambda slot, ints: (0, slot)),
                by_row,
                by_row,
                pl.BlockSpec((8, width), lambda slot, ints: (0, 0)),
                pl.BlockSpec((width, width), lambda slot, ints: (0, 0)),
            ],
            scratch_shapes=[pltpu.VMEM((tokens, width), BF16)],
        ),
        out_shape=[
            jax.ShapeDtypeStruct((width, groups * tokens), BF16),
            jax.ShapeDtypeStruct((groups * tokens, narrow), BF16),
            jax.ShapeDtypeStruct((groups * tokens, narrow), BF16),
            jax.ShapeDtypeStruct((8, width), F32),
            jax.ShapeDtypeStruct((width, width), BF16),
        ],
        compiler_params=pltpu.CompilerParams(vmem_limit_bytes=VMEM),
        cost_estimate=pl.CostEstimate(
            flops=4 * groups * tokens * width * width,
            bytes_accessed=8 * groups * tokens * width,
            transcendentals=0,
        ),
        name="project",
    )(ints, weights, own, *others)


def project_last_kernel(groups, ints, weights, own, before, behind, order, gains, *refs):
    normed_t, query, kv, values = refs[3:]
    group = ints[4]
    values[...] = own[...]

    @pl.when(group == 0)
    def _():
        values[...] = behind[...]

    @pl.when(group == groups - 1)
    def _():
        values[...] = before[...]

    project_block(values[...], weights, gains, order, normed_t, query, kv)


def project_last(dims, ints, weights, own, before, behind, order, gains, normed_t, query, kv):
    tokens, width = own.shape
    narrow = kv.shape[1]
    whole = lambda array: pl.BlockSpec(array.shape, lambda step, ints: (0, 0))
    by_row = pl.BlockSpec((tokens, narrow), lambda step, ints: (ints[6], 0))
    return pl.pallas_call(
        functools.partial(project_last_kernel, dims[1]),
        grid_spec=pltpu.PrefetchScalarGridSpec(
            num_scalar_prefetch=1,
            grid=(1,),
            in_specs=[
                pl.BlockSpec((width, weights.shape[1] // dims[1]), lambda step, ints: (0, ints[4]))
            ]
            + [whole(array) for array in (own, before, behind, order, gains)]
            + [pl.BlockSpec(memory_space=pl.ANY)] * 3,
            out_specs=[
                pl.BlockSpec((width, tokens), lambda step, ints: (0, ints[6])),
                by_row,
                by_row,
            ],
            scratch_shapes=[pltpu.VMEM((tokens, width), BF16)],
        ),
        out_shape=[jax.ShapeDtypeStruct(x.shape, x.dtype) for x in (normed_t, query, kv)],
        input_output_aliases={7: 0, 8: 1, 9: 2},
        compiler_params=pltpu.CompilerParams(vmem_limit_bytes=VMEM),
        cost_estimate=pl.CostEstimate(
            flops=4 * tokens * width * width, bytes_accessed=8 * tokens * width, transcendentals=0
        ),
        name="project_last",
    )(ints, weights, own, before, behind, order, gains, normed_t, query, kv)


def scatter_order(groups, splits, unit):
    def source(index):
        within = index % unit
        index = index // unit
        g = index % groups
        index = index // groups
        return ((index // splits * groups + g) * splits + index % splits) * unit + within

    return source


def reordered(values, source, unit):
    return jnp.concatenate(
        [
            values[source(start) : source(start) + unit]
            for start in range(0, values.shape[0], unit)
        ],
        axis=0,
    )


def packed_rows(values, tall, low):
    piece = math.gcd(tall, low)
    across, down = low // piece, tall // piece
    wide = values.shape[1] // across
    rows = []
    for start in range(0, values.shape[0], tall):
        for part in range(across):
            columns = slice(wide * part, wide * (part + 1))
            rows.append(
                jnp.concatenate(
                    [
                        values[start + piece * i : start + piece * (i + 1), columns]
                        for i in range(down)
                    ],
                    axis=1,
                )
            )
    return jnp.concatenate(rows, axis=0)


def unpacked_rows(values, tall, low, columns):
    piece = math.gcd(tall, low)
    across, down = low // piece, tall // piece
    wide = columns // across
    rows = []
    for start in range(0, values.shape[0], low):
        for index in range(down):
            lanes = slice(wide * index, wide * (index + 1))
            rows.append(
                jnp.concatenate(
                    [
                        values[start + piece * part : start + piece * (part + 1), lanes]
                        for part in range(across)
                    ],
                    axis=1,
                )
            )
    return jnp.concatenate(rows, axis=0)


def block_kernel(
    dims, heads, ints, tokens, w_out, gains, w_gate, w_up, w_packed, upstream, *refs
):
    rows_apart, groups, splits = dims
    contexts, refs = refs[:heads], refs[heads:]
    result, d_mixed, d_first, d_rest, grads = refs[:5]
    (context_t, mixed, normed, normed_t, d_normed, total, order) = refs[5:12]
    wide, down, sems = refs[12:]
    step, chunks = pl.program_id(0), pl.num_programs(0) - 1
    width, chunk = w_gate.shape
    devices = rows_apart * groups * splits
    hidden_unit = chunk * chunks // devices
    gain = gains[1:2, :]
    unit = width // devices
    for_rows = scatter_order(groups, splits, unit)
    for_hidden = scatter_order(groups, splits, hidden_unit)
    whole_rows = unit % 8 == 0

    @pl.when(step == 0)
    def first():
        if not whole_rows:
            order[...] = chosen((width, width), for_rows)
        each = width // groups // heads
        for g in range(groups):
            for head in range(heads):
                start = (g * heads + head) * each
                context_t[start : start + each, :] = contexts[head][g]
        context = jnp.transpose(context_t[...].astype(F32)).astype(BF16)
        values = tokens[...].astype(F32) + dot_nn(context, w_out[...])
        mixed[...] = values
        total[...] = values
        wide_values = rms_scale(values, gain)
        normed[...] = wide_values.astype(BF16)
        if whole_rows:
            turned = reordered(jnp.transpose(wide_values), for_rows, unit)
        else:
            turned = dot_nt(order[...], normed[...])
        normed_t[...] = turned.astype(BF16)
        d_normed[...] = jnp.zeros_like(d_normed)

    place = lax.rem(step, 2)
    tall = down.shape[1]

    def wide_copy(slot, index):
        columns = pl.ds(pl.multiple_of(index * 2 * chunk, 2 * chunk), 2 * chunk)
        return pltpu.make_async_copy(wide.at[slot], grads.at[:, columns], sems.at[0, slot])

    def down_copy(slot, index):
        rows = pl.ds(pl.multiple_of(index * tall, tall), tall)
        columns = pl.ds(grads.shape[1] - down.shape[2], down.shape[2])
        return pltpu.make_async_copy(down.at[slot], grads.at[rows, columns], sems.at[1, slot])

    @pl.when(step >= 2)
    def _():
        wide_copy(place, step - 2).wait()
        down_copy(place, step - 2).wait()

    @pl.when(step < chunks)
    def work():
        w_down = unpacked_rows(
            w_packed[...].astype(F32), hidden_unit, width // devices, width
        ).astype(BF16)
        gate = dot_nn(normed[...], w_gate[...])
        upward = dot_nn(normed[...], w_up[...])
        d_hidden = dot_nt(upstream[...], w_down)
        square = gate * gate
        turn = jnp.tanh(GELU_SCALE * (gate + 0.044715 * gate * square))
        half = 0.5 * (1.0 + turn)
        active = gate * half
        slope = half + 0.5 * gate * (1.0 - turn * turn) * (GELU_SCALE * (1.0 + 0.134145 * square))
        wide_hidden = active * upward
        hidden = wide_hidden.astype(BF16)
        d_gate = (d_hidden * upward * slope).astype(BF16)
        d_up = (d_hidden * active).astype(BF16)
        total[...] += dot_nn(hidden, w_down)
        d_normed[...] += dot_nt(d_gate, w_gate[...]) + dot_nt(d_up, w_up[...])
        hidden_t = reordered(jnp.transpose(wide_hidden), for_hidden, hidden_unit).astype(BF16)

        d_down = dot_nn(hidden_t, upstream[...])
        down[place] = packed_rows(d_down, hidden_unit, width // devices).astype(BF16)
        wide[place, :, :chunk] = dot_nn(normed_t[...], d_gate).astype(BF16)
        wide[place, :, chunk:] = dot_nn(normed_t[...], d_up).astype(BF16)
        wide_copy(place, step).start()
        down_copy(place, step).start()

    @pl.when(step == chunks)
    def finish():
        result[...] = total[...].astype(BF16)
        back = upstream[...].astype(F32) + rms_back(mixed[...], gain, d_normed[...])
        d_mixed[...] = back
        branch = back.astype(BF16)
        d_context = dot_nt(w_out[...], branch).astype(BF16)
        each = d_first.shape[1]
        size = width // groups
        for g in range(groups):
            d_first[g] = d_context[size * g : size * g + each]
            d_rest[g] = d_context[size * g + each : size * (g + 1)]
        if whole_rows:
            d_out = reordered(dot_nn(context_t[...], branch), for_rows, unit)
        else:
            d_out = dot_nn(dot_nn(order[...], context_t[...]).astype(BF16), branch)
        wide[place, :, :width] = d_out.astype(BF16)
        wide[place, :, width:] = jnp.zeros((width, 2 * chunk - width), BF16)
        wide_copy(place, step).start()
        wide_copy(1 - place, step - 1).wait()
        down_copy(1 - place, step - 1).wait()
        wide_copy(place, step).wait()


def feed_forward(dims, ints, tokens, contexts, gains, late, upstream):
    groups, splits = dims[1:]
    rows, width = tokens.shape
    hidden = (late.shape[1] - width) // 3
    chunk = 2 * TILE
    steps = hidden // chunk
    each = contexts[0].shape[1]
    full = lambda *shape: pl.BlockSpec(shape, lambda step: (0,) * len(shape))
    return pl.pallas_call(
        functools.partial(block_kernel, dims, len(contexts)),
        grid=(steps + 1,),
        in_specs=[
            smem(),
            full(rows, width),
            pl.BlockSpec((width, width), lambda step: (0, 3 * hidden // width)),
            full(8, width),
            pl.BlockSpec((width, chunk), lambda step: (0, steps + jnp.minimum(step, steps - 1))),
            pl.BlockSpec(
                (width, chunk), lambda step: (0, 2 * steps + jnp.minimum(step, steps - 1))
            ),
            pl.BlockSpec((width // steps, hidden), lambda step: (jnp.minimum(step, steps - 1), 0)),
            full(rows, width),
        ]
        + [full(*context.shape) for context in contexts],
        out_specs=[
            full(rows, width),
            full(rows, width),
            full(groups, each, rows),
            full(groups, width // groups - each, rows),
        ]
        + [pl.BlockSpec(memory_space=pl.ANY)],
        out_shape=[
            jax.ShapeDtypeStruct((rows, width), BF16),
            jax.ShapeDtypeStruct((rows, width), F32),
            jax.ShapeDtypeStruct((groups, each, rows), BF16),
            jax.ShapeDtypeStruct((groups, width // groups - each, rows), BF16),
        ]
        + [jax.ShapeDtypeStruct((width, 3 * hidden + 2 * chunk), BF16)],
        scratch_shapes=[
            pltpu.VMEM((width, rows), BF16),
            pltpu.VMEM((rows, width), F32),
            pltpu.VMEM((rows, width), BF16),
            pltpu.VMEM((width, rows), BF16),
            pltpu.VMEM((rows, width), F32),
            pltpu.VMEM((rows, width), F32),
            pltpu.VMEM((width, width), BF16),
            pltpu.VMEM((2, width, 2 * chunk), BF16),
            pltpu.VMEM((2, width // steps, hidden), BF16),
            pltpu.SemaphoreType.DMA((2, 2)),
        ],
        compiler_params=pltpu.CompilerParams(vmem_limit_bytes=VMEM),
        cost_estimate=pl.CostEstimate(
            flops=18 * rows * width * hidden + 6 * rows * width * width,
            bytes_accessed=12 * width * hidden,
            transcendentals=rows * hidden,
        ),
        name="feed_forward",
    )(ints, tokens, late, gains, late, late, late, upstream, *contexts)


def weight_kernel(splits, normed_t, *refs):
    d_heads, outs, total = refs[: -splits - 1], refs[-splits - 1 : -1], refs[-1]
    step = pl.program_id(0)
    added = dot_nt(normed_t[...], jnp.concatenate([d_head[...] for d_head in d_heads], axis=0))

    @pl.when(step == 0)
    def _():
        total[...] = added

    @pl.when(step > 0)
    def _():
        total[...] += added

    @pl.when(step == pl.num_programs(0) - 1)
    def _():
        part = total.shape[0] // splits
        for other in range(splits):
            outs[other][...] = total[part * other : part * (other + 1), :].astype(BF16)


def weight_grads(splits, normed_t, d_heads):
    groups, rows, tokens = d_heads[0].shape
    width = normed_t.shape[0]
    out = (width // splits, rows * len(d_heads))
    return pl.pallas_call(
        functools.partial(weight_kernel, splits),
        grid=(groups,),
        in_specs=[pl.BlockSpec((width, tokens), lambda step: (0, step))]
        + [by_slot(rows, tokens)] * len(d_heads),
        out_specs=[pl.BlockSpec(out, lambda step: (0, 0))] * splits,
        out_shape=[jax.ShapeDtypeStruct(out, BF16)] * splits,
        scratch_shapes=[pltpu.VMEM((width, out[1]), F32)],
        compiler_params=pltpu.CompilerParams(vmem_limit_bytes=VMEM),
        cost_estimate=pl.CostEstimate(
            flops=2 * width * out[1] * groups * tokens,
            bytes_accessed=2 * width * groups * tokens,
            transcendentals=0,
        ),
        name="weight_grads",
    )(normed_t, *d_heads)


def added_kernel(count, *refs):
    held, outs = refs[:count], refs[count:]
    total = held[0][...].astype(F32)
    for piece in held[1:]:
        total += piece[...].astype(F32)
    part = total.shape[0] // len(outs)
    for index, out in enumerate(outs):
        out[...] = total[part * index : part * (index + 1)].astype(out.dtype)


def added(pieces, parts):
    rows, columns = pieces[0].shape
    return pl.pallas_call(
        functools.partial(added_kernel, len(pieces)),
        out_shape=[jax.ShapeDtypeStruct((rows // parts, columns), BF16)] * parts,
        compiler_params=pltpu.CompilerParams(vmem_limit_bytes=VMEM),
        cost_estimate=pl.CostEstimate(flops=0, bytes_accessed=2**20, transcendentals=0),
        name="added",
    )(*pieces)


def unpacked(pieces, heads, size):
    return jnp.concatenate(
        [
            piece[:, (3 * head + part) * size : (3 * head + part + 1) * size]
            for part in range(3)
            for piece in pieces
            for head in range(heads)
        ],
        axis=1,
    )


def count_kernel(groups, heads, size, count, down, ints, *refs):
    held, tables, grads = refs[:count], refs[count : count + heads], refs[count + heads]
    outs, counts = refs[count + heads + 1 : -1], refs[-1]
    total = held[0][...].astype(F32)
    for piece in held[1:]:
        total += piece[...].astype(F32)
    part = total.shape[0] // groups
    blank = jnp.zeros((part, counts.shape[1] - total.shape[1]), F32)
    for index, out in enumerate(outs):
        rows = total[part * index : part * (index + 1)]
        out[...] = jnp.concatenate([rows, blank], axis=1)
    squares = jnp.sum(total * total, axis=0, keepdims=True)
    table = jnp.concatenate(
        [jnp.sum(jnp.transpose(table[...]), axis=0, keepdims=True) for table in tables], axis=1
    )
    mine = [(ints[4] == g).astype(F32) for g in range(groups)]
    values = grads[...].astype(F32)
    values = values * values
    wide = values.shape[1] - down[0]
    piece = math.gcd(*down[1:3])
    across = down[2] // piece
    each = down[0] * piece // down[1]
    packed = []
    for part in range(across):
        rows = jnp.sum(values[piece * part : piece * (part + 1), wide:], axis=0, keepdims=True)
        packed.append(sum(rows[:, start : start + each] for start in range(0, down[0], each)))
    row = jnp.concatenate(
        [table * own for own in mine]
        + [unpacked([squares * own for own in mine], heads, size)]
        + [jnp.sum(values[:, : wide - down[3]], axis=0, keepdims=True)]
        + packed,
        axis=1,
    )
    counts[...] = jnp.zeros_like(counts)
    each = counts.shape[1]
    for start in range(0, row.shape[1], each):
        held_row = row[:, start : start + each]
        counts[start // each : start // each + 1, : held_row.shape[1]] = held_row


def counted(groups, heads, size, ints, pieces, tables, grads, down):
    rows, columns = pieces[0].shape
    buckets = tables[0].shape[0]
    length = groups * (heads * buckets + columns) + grads.shape[1] - down[0] - down[3]
    length += down[0] * down[2] // down[1]
    across = -(-columns // LANES) * LANES
    counts = -(-length // (8 * across)) * 8
    vmem = pl.BlockSpec(memory_space=pltpu.VMEM)
    return pl.pallas_call(
        functools.partial(count_kernel, groups, heads, size, len(pieces), down),
        in_specs=[smem()] + [vmem] * (len(pieces) + len(tables) + 1),
        out_shape=[jax.ShapeDtypeStruct((rows // groups, across), F32)] * groups
        + [jax.ShapeDtypeStruct((counts, across), F32)],
        compiler_params=pltpu.CompilerParams(vmem_limit_bytes=VMEM),
        cost_estimate=pl.CostEstimate(flops=0, bytes_accessed=2**20, transcendentals=0),
        name="counted",
    )(ints, *pieces, *tables, grads)


def input_kernel(heads, weights, own, gains, d_mixed, *refs):
    d_heads, (out, total) = refs[:heads], refs[heads:]
    step = pl.program_id(0)
    size = d_heads[0].shape[0] // 3
    blank = jnp.zeros((size, own.shape[0]), BF16)
    pieces = [d_head[size:, :] for d_head in d_heads]
    pieces += [d_head[:size, :] for d_head in d_heads] + [blank]
    added = dot_nn(weights[...], jnp.concatenate(pieces, axis=0))

    @pl.when(step == 0)
    def _():
        total[...] = added

    @pl.when(step > 0)
    def _():
        total[...] += added

    @pl.when(step == pl.num_programs(0) - 1)
    def _():
        back = rms_back(own[...].astype(F32), gains[0:1, :], jnp.transpose(total[...]))
        out[...] = (d_mixed[...] + back).astype(BF16)


def input_grads(groups, weights, own, gains, d_mixed, d_heads):
    tokens, width = own.shape
    full = lambda *shape: pl.BlockSpec(shape, lambda step: (0,) * len(shape))
    return pl.pallas_call(
        functools.partial(input_kernel, len(d_heads)),
        grid=(groups,),
        in_specs=[
            pl.BlockSpec((width, weights.shape[1] // groups), lambda step: (0, step)),
            full(tokens, width),
            full(8, width),
            full(tokens, width),
        ]
        + [by_slot(*d_heads[0].shape[1:])] * len(d_heads),
        out_specs=full(tokens, width),
        out_shape=jax.ShapeDtypeStruct((tokens, width), BF16),
        scratch_shapes=[pltpu.VMEM((width, tokens), F32)],
        compiler_params=pltpu.CompilerParams(vmem_limit_bytes=VMEM),
        cost_estimate=pl.CostEstimate(
            flops=2 * tokens * width * weights.shape[1],
            bytes_accessed=16 * tokens * width,
            transcendentals=0,
        ),
        name="input_grads",
    )(weights, own, gains, d_mixed, *d_heads)


def by_slot(rows, tokens):
    return pl.BlockSpec((None, rows, tokens), lambda slot: (slot, 0, 0))


def smem():
    return pl.BlockSpec(memory_space=pltpu.SMEM)


def attend(head, tokens, groups, splits, ints, table, query, kvs):
    seq, rows = tokens * groups * splits, tokens * groups
    half = LANES // 2
    whole = pl.BlockSpec((rows, LANES), lambda slot: (0, head))
    return pl.pallas_call(
        functools.partial(forward_kernel, tokens, groups, splits),
        grid=(groups,),
        in_specs=[smem(), smem(), pl.BlockSpec((tokens, LANES), lambda slot: (slot, head))]
        + [whole] * splits,
        out_specs=[
            pl.BlockSpec((seq, tokens), lambda slot: (slot, 0)),
            by_slot(half, tokens),
            by_slot(half + 16, tokens),
        ],
        out_shape=[
            jax.ShapeDtypeStruct((groups * seq, tokens), BF16),
            jax.ShapeDtypeStruct((groups, half, tokens), BF16),
            jax.ShapeDtypeStruct((groups, half + 16, tokens), F32),
        ],
        scratch_shapes=[
            pltpu.VMEM((seq + 2 * LANES, LANES), BF16),
            pltpu.VMEM((half + 16, seq + 2 * LANES), BF16),
            pltpu.VMEM((tokens + 2 * LANES, tokens), F32),
            pltpu.VMEM((3, LANES, LANES), F32),
            pltpu.VMEM((8, tokens), F32),
        ],
        compiler_params=pltpu.CompilerParams(vmem_limit_bytes=VMEM),
        cost_estimate=pl.CostEstimate(
            flops=16 * seq * rows * half, bytes_accessed=2 * seq * rows, transcendentals=seq * rows
        ),
        name="attend",
    )(ints, table, query, *kvs)


def attend_back(
    head, tokens, groups, splits, ints, buckets, query, d_context, place, stats, probs, kvs
):
    seq, rows = tokens * groups * splits, tokens * groups
    half = LANES // 2
    whole = pl.BlockSpec((rows, LANES), lambda slot: (0, head))
    kept = pl.BlockSpec((groups, LANES, tokens), lambda slot: (0, 0, 0))
    return pl.pallas_call(
        functools.partial(backward_kernel, tokens, groups, splits),
        grid=(groups,),
        in_specs=[
            smem(),
            pl.BlockSpec((tokens, LANES), lambda slot: (slot, head)),
            pl.BlockSpec((None, None, half, tokens), lambda slot: (slot, place, 0, 0)),
            by_slot(half + 16, tokens),
            pl.BlockSpec((seq, tokens), lambda slot: (slot, 0)),
        ]
        + [whole] * splits,
        out_specs=[pl.BlockSpec((groups, half + LANES, tokens), lambda slot: (0, 0, 0))]
        + [kept] * (splits - 1)
        + [pl.BlockSpec((buckets, LANES), lambda slot: (0, 0))],
        out_shape=[jax.ShapeDtypeStruct((groups, half + LANES, tokens), BF16)]
        + [jax.ShapeDtypeStruct((groups, LANES, tokens), BF16)] * (splits - 1)
        + [jax.ShapeDtypeStruct((buckets, LANES), F32)],
        scratch_shapes=[
            pltpu.VMEM((seq + 2 * LANES, LANES), BF16),
            pltpu.VMEM((half + 16, seq + 2 * LANES), BF16),
            pltpu.VMEM((seq + 2 * LANES, LANES), F32),
            pltpu.VMEM((3, LANES, LANES), F32),
            pltpu.VMEM((2, 8, tokens), F32),
            pltpu.VMEM((half + 16, tokens), F32),
        ],
        compiler_params=pltpu.CompilerParams(vmem_limit_bytes=VMEM),
        cost_estimate=pl.CostEstimate(
            flops=32 * seq * rows * half, bytes_accessed=2 * seq * rows, transcendentals=0
        ),
        name="attend_back",
    )(ints, query, d_context, stats, probs, *kvs)


def factored(grad_shard, column_total, row_old, column_old, row_total):
    columns = grad_shard.shape[1]
    mean_square = jnp.sum(column_total) / (row_total * columns) + EPSILON
    row_new = (
        DECAY_RATE * row_old
        + (1.0 - DECAY_RATE) * (jnp.sum(grad_shard * grad_shard, axis=1) / columns) / mean_square
    )
    column_new = (
        DECAY_RATE * column_old + (1.0 - DECAY_RATE) * (column_total / row_total) / mean_square
    )
    return (row_new, column_new)


def shards(
    tokens,
    lengths,
    norm_one,
    w_qkv,
    rel_table,
    w_out,
    norm_two,
    w_gateup,
    w_down,
    cotangent,
    row_qkv,
    col_qkv,
    row_out,
    col_out,
    row_gateup,
    col_gateup,
    row_down,
    col_down,
):
    own = tokens[0]
    tok_rows, width = own.shape
    heads = rel_table.shape[1]
    buckets = rel_table.shape[0]
    rows_apart, groups, splits = (lax.axis_size(name) for name in ALL)
    group_heads = heads // groups
    head_size = width // heads
    group, split = lax.axis_index("group"), lax.axis_index("split")
    group_width = width // groups

    def ahead(array, axis, by):
        size = lax.axis_size(axis)
        return lax.ppermute(array, axis, [((i + by) % size, i) for i in range(size)])

    def swap_groups(array):
        return lax.all_to_all(array, "group", 0, 0)

    def swap_rows(array):
        return lax.all_to_all(array, "batch", 0, 0)

    def line(array, by):
        pairs = [(i, i + by) for i in range(groups) if 0 <= i + by < groups]
        return lax.ppermute(array, "group", pairs)

    before, behind = [own], [own]
    for _ in range(groups - 1):
        before.append(line(before[-1], 1))
        behind.append(line(behind[-1], -1))

    unit = w_qkv.shape[0]
    by_part = w_qkv.reshape(unit, 3, groups, group_heads, head_size)
    gains = jnp.pad(jnp.stack([norm_one, norm_two], axis=1), ((0, 0), (0, head_size - 2)))
    packed = jnp.concatenate(
        [
            jnp.concatenate([by_part[:, 1], by_part[:, 2]], axis=-1).reshape(unit, groups, -1),
            by_part[:, 0].reshape(unit, groups, -1),
            jnp.broadcast_to(gains[:, None], (unit, groups, head_size)),
        ],
        axis=2,
    )
    early = lax.all_gather(packed.reshape(unit, -1), ALL, axis=0, tiled=True)
    together = math.gcd(unit, w_down.shape[0])
    packed_down = w_down.reshape(w_down.shape[0] // together, together, unit // together, -1)
    packed_down = jnp.transpose(packed_down, (2, 1, 0, 3)).reshape(unit, -1)
    late = lax.all_gather(
        after(jnp.concatenate([packed_down, w_gateup, w_out], axis=1), before[1], behind[1]),
        ALL,
        axis=0,
        tiled=True,
    )

    dims = (rows_apart, groups, splits)
    far = jnp.where(group == 0, groups - 1, jnp.where(group == groups - 1, 0, group))
    ends = jnp.cumsum(lengths[0])
    ints = jnp.concatenate(
        [
            split.astype(jnp.int32)[None],
            ends.astype(jnp.int32),
            jnp.stack([group, lax.axis_index("batch"), far]).astype(jnp.int32),
        ]
    )
    *blocks, gains, order = project(dims, ints, early, own, before[1:-1] + behind[1:-1])
    normed_t, query, kv = project_last(
        dims, ints, early, own, before[-1], behind[-1], order, gains, *blocks
    )
    kvs = [kv] + [ahead(kv, "split", other) for other in range(1, splits)]

    table_own = lax.dynamic_slice_in_dim(rel_table.T, group * group_heads, group_heads, 0)

    contexts, moved, stats, probs = [], [], [], []
    for head in range(group_heads):
        prob, context, stat = attend(
            head,
            tok_rows,
            groups,
            splits,
            after(ints, *contexts[-1:]),
            table_own[head : head + 1],
            query,
            kvs,
        )
        contexts.append(context)
        moved.append(swap_groups(after(context, *moved[-1:])))
        stats.append(stat)
        probs.append(prob)

    outs = feed_forward(
        dims, ints, own, moved, gains, late, cotangent[0]
    )
    result, d_mixed, d_first, d_rest, held = outs

    parts = [lax.dynamic_index_in_dim(d_first, group, 0, keepdims=False)]
    for by in range(1, groups):
        piece = lax.dynamic_index_in_dim(d_first, (group + by) % groups, 0, keepdims=False)
        parts.append(ahead(piece, "group", groups - by))
    d_first = []
    for index in range(groups):
        piece = parts[0]
        for by in range(1, groups):
            piece = jnp.where((group + groups - by) % groups == index, parts[by], piece)
        d_first.append(piece)
    d_first = jnp.stack(d_first)
    d_rest = swap_groups(d_rest)
    d_contexts = [d_first[:, None], d_rest.reshape(groups, group_heads - 1, head_size, tok_rows)]
    row_sum = lax.psum_scatter(held, ("batch", "split"), scatter_dimension=0, tiled=True)
    row_sum = after(row_sum)
    grads_own = lax.psum_scatter(row_sum, "group", scatter_dimension=0, tiled=True)

    d_heads, d_received, d_tables = [], [], []
    ready = [(), ()] + [(row_sum,)] * (group_heads - 2)
    for head in range(group_heads):
        outs = attend_back(
            head,
            tok_rows,
            groups,
            splits,
            ints,
            buckets,
            query,
            after(d_contexts[int(head > 0)], *ready[head], *d_heads[-1:]),
            head - int(head > 0),
            stats[head],
            probs[head],
            kvs,
        )
        beside = d_received[-1] if head else d_contexts[1]
        if head < group_heads - 1:
            outs = lax.optimization_barrier((*outs, beside))[:-1]
        d_head = outs[0].astype(F32)
        for other in range(1, splits):
            d_kv = ahead(outs[other], "split", splits - other).astype(F32)
            d_head = d_head + jnp.pad(d_kv, ((0, 0), (head_size, 0), (0, 0)))
        d_head = d_head.astype(BF16)
        if head == group_heads - 1:
            d_head = after(d_head, beside)
        d_heads.append(d_head)
        d_received.append(swap_groups(d_head))
        d_tables.append(outs[-1])

    down_shape = (w_down.shape[0] * width // unit, w_down.shape[0], unit)
    down_start = grads_own.shape[1] - down_shape[0]
    down_shape += (down_start - w_gateup.shape[1] - width,)
    grads = weight_grads(splits, normed_t, d_heads)
    held = added(
        [grads[0]] + [ahead(grads[by], "split", splits - by) for by in range(1, splits)], rows_apart
    )
    held = [held[0]] + [ahead(held[by], "batch", rows_apart - by) for by in range(1, rows_apart)]
    held[0] = after(held[0], d_received[-1])
    *columns, counts = counted(
        groups, group_heads, head_size, ints, held, d_tables, grads_own, down_shape
    )
    counts = sum([ahead(counts, "batch", by) for by in range(1, rows_apart)], counts)
    d_received[-1] = after(d_received[-1], counts)
    d_inputs = input_grads(groups, early, own, gains, d_mixed, d_received)
    counts_rows = counts.shape[0]
    travelled = [jnp.concatenate([counts, columns[0]], axis=0)] + [
        ahead(jnp.concatenate([counts, columns[by]], axis=0), "group", groups - by)
        for by in range(1, groups)
    ]
    *travelled, d_inputs = lax.optimization_barrier((*travelled, d_inputs))
    columns = [both[counts_rows:] for both in travelled]
    counts = sum([both[:counts_rows] for both in travelled[1:]], travelled[0][:counts_rows])
    counts = sum([ahead(counts, "split", by) for by in range(1, splits)], counts)
    pieces = []
    for index in range(groups):
        piece = columns[0]
        for by in range(1, groups):
            piece = jnp.where((group + groups - by) % groups == index, columns[by], piece)
        pieces.append(piece)
    shard_qkv = unpacked(pieces, group_heads, head_size)
    steps = w_down.shape[0] * rows_apart * groups * splits // (2 * TILE)

    def in_order(array):
        array = array.reshape(*array.shape[:-1], steps, 2, -1)
        return jnp.swapaxes(array, -3, -2).reshape(*array.shape[:-3], -1)

    shard_rest = grads_own.astype(F32)
    shard_gateup = in_order(shard_rest[:, : w_gateup.shape[1]])
    shard_out = shard_rest[:, w_gateup.shape[1] :][:, :width]
    shard_down = shard_rest[:, down_start:].reshape(
        unit // together, together, w_down.shape[0] // together, -1
    )
    shard_down = jnp.transpose(shard_down, (2, 1, 0, 3)).reshape(-1, width)
    summed = counts.reshape(-1)
    sizes = (heads * buckets, 3 * width, w_gateup.shape[1], width, width)
    table_total, column_qkv, column_gateup, column_out, column_down, _ = jnp.split(
        summed, [sum(sizes[: i + 1]) for i in range(len(sizes))]
    )
    table_total = table_total.reshape(heads, buckets)
    column_gateup = in_order(column_gateup)
    shard_gain_one = jnp.sum(w_qkv.astype(F32) * shard_qkv, axis=1) / norm_one.astype(F32)
    shard_gain_two = jnp.sum(w_gateup.astype(F32) * shard_gateup, axis=1) / norm_two.astype(F32)
    new_row_qkv, new_col_qkv = factored(shard_qkv, column_qkv, row_qkv, col_qkv, width)
    new_row_out, new_col_out = factored(shard_out, column_out, row_out, col_out, width)
    new_row_gateup, new_col_gateup = factored(
        shard_gateup, column_gateup, row_gateup, col_gateup, width
    )
    new_row_down, new_col_down = factored(
        shard_down, column_down, row_down, col_down, w_down.shape[0] * rows_apart * groups * splits
    )
    return (
        result[None],
        d_inputs[None],
        shard_gain_one,
        shard_qkv,
        table_total.T,
        shard_out,
        shard_gain_two,
        shard_gateup,
        shard_down,
        new_row_qkv,
        new_col_qkv,
        new_row_out,
        new_col_out,
        new_row_gateup,
        new_col_gateup,
        new_row_down,
        new_col_down,
    )


def solution(mesh):
    row_blocks = P("batch", ("group", "split"), None)
    split_rows = P(ALL, None)
    split_row = P(ALL)

    def run(*arrays):
        rows, ring = mesh.devices.shape
        groups = math.gcd(ring, arrays[4].shape[1])
        fine = Mesh(mesh.devices.reshape(rows, groups, ring // groups), ALL)
        return jax.shard_map(
            shards,
            mesh=fine,
            in_specs=(
                row_blocks,
                P("batch", None),
                split_row,
                split_rows,
                P(),
                split_rows,
                split_row,
                split_rows,
                split_rows,
                row_blocks,
            )
            + (split_row, P()) * 4,
            out_specs=(
                row_blocks,
                row_blocks,
                split_row,
                split_rows,
                P(),
                split_rows,
                split_row,
                split_rows,
                split_rows,
            )
            + (split_row, P()) * 4,
            check_vma=False,
        )(*arrays)

    return run
```
